32 devices in a mesh: dp: 8 (over z, x), rows: 4 (over y, core).
Axes of the slice: x: 2, y: 2, z: 4, core: 2. Of those that a mesh axis runs over, the one named last changes fastest.
Arguments:
- images: bfloat16 [48, 32, 128, 256], P('dp', 'rows'), may hold values from -120 to 120
- kernel: bfloat16 [3, 3, 256, 128], replicated, may hold values from -0.25 to 0.25
- colors: float32 [2, 64, 64], replicated, may hold values from -0.75 to 0.75
- offset: float32 [128], replicated, may hold values from -4 to 4
- upstream: bfloat16 [48, 32, 128, 128], P('dp', 'rows'), may hold values from -8 to 8
Outputs:
- colored: bfloat16 [48, 32, 128, 128], P('dp', 'rows')
- grad_images: bfloat16 [48, 32, 128, 256], P('dp', 'rows')
- grad_kernel: float32 [3, 3, 256, 128], replicated
- grad_colors: float32 [2, 64, 64], replicated
The draws below stay inside these ranges and needn't reach their ends.
All inputs are finite; a program needn't handle non-finite values.
Results may differ from the reference program's by a relative error of at most 0.0044.
The reference program's roundings to bfloat16 on the way (of `pre_grad`) count: a program that leaves them out, or rounds other values in their place, can miss the bound.
Values may be sent and summed in bfloat16 or wider, within the bound.
No kernel may reach another device: no remote copies, remote signals or barrier semaphores. Data moves between devices by JAX's collectives and lax.ppermute only.
A program may use at most 128 MiB of HBM per device.

```python
import math
import jax
import jax.numpy as jnp
from jax import lax

CIN = 256
COUT = 128
GS = 64
WID = 128
NS_ITERS = 5
BATCH = 48
HEIGHT = 32
GROUPS = 2


def picture(key):
    first = jax.random.fold_in(key, 11)
    second = jax.random.fold_in(key, 12)
    third = jax.random.fold_in(key, 13)
    image_pos = jnp.arange(BATCH, dtype=jnp.float32) / max(BATCH - 1, 1)
    row_pos = jnp.arange(HEIGHT, dtype=jnp.float32) / max(HEIGHT - 1, 1)
    scaling = (10.0 ** image_pos)[:, None, None, None] * (3.0 ** row_pos)[None, :, None, None]
    signs = jnp.where(jax.random.bernoulli(third, 0.5, (CIN,)), 1.0, -1.0).astype(jnp.float32)
    base = jax.random.truncated_normal(first, -3.0, 3.0, (BATCH, HEIGHT, WID, CIN), jnp.float32)
    means = jax.random.uniform(second, (CIN,), jnp.float32, 0.5, 1.0) * signs
    return ((base + means) * scaling).astype(jnp.bfloat16)


def filters(key):
    inner = jax.random.fold_in(key, 23)
    base = jax.random.truncated_normal(inner, -4.0, 4.0, (3, 3, CIN, COUT), jnp.float32)
    return (base * (9.0 * CIN) ** (-0.5)).astype(jnp.bfloat16)


def draw_images(key, part):
    return picture(key)


def draw_kernel(key, part):
    return filters(key)


def draw_upstream(key, part):
    source = picture(key)
    weights = filters(key)
    forward = lax.conv_general_dilated(source, weights, (1, 1), ((1, 1), (1, 1)), dimension_numbers=('NHWC', 'HWIO', 'NHWC'), preferred_element_type=jnp.float32)
    noise_key = jax.random.fold_in(key, 37)
    level_key = jax.random.fold_in(key, 41)
    sign_key = jax.random.fold_in(key, 43)
    signs = jnp.where(jax.random.bernoulli(sign_key, 0.5, (COUT,)), 1.0, -1.0).astype(jnp.float32)
    noise = jax.random.truncated_normal(noise_key, -4.0, 4.0, (BATCH, HEIGHT, WID, COUT), jnp.float32)
    levels = jax.random.uniform(level_key, (COUT,), jnp.float32, 0.3, 1.0)
    total = 0.6 / 9.0 * forward + noise + levels * signs
    return jnp.clip(total, -8.0, 8.0).astype(jnp.bfloat16)


def gaussian(rng, dims, deviation, most, held_as=jnp.bfloat16):
    values = jax.random.normal(rng, dims, jnp.float32) * deviation
    return jnp.minimum(jnp.maximum(values, -most), most).astype(held_as)


def setup_inputs(seed: int = 0) -> dict:
    keys = jax.random.split(jax.random.key(seed), 6)
    images = draw_images(jax.random.fold_in(keys[5], 71), 0)
    kernel = draw_kernel(jax.random.fold_in(keys[5], 71), 0)
    colors = gaussian(keys[2], (GROUPS, GS, GS), GS ** -0.5, 0.75, jnp.float32)
    offset = gaussian(keys[3], (COUT,), 1.0, 4.0, jnp.float32)
    upstream = draw_upstream(jax.random.fold_in(keys[5], 71), 0)
    return {"images": images, "kernel": kernel, "colors": colors, "offset": offset, "upstream": upstream}


EPSILON = 1e-05
PRECISE = lax.Precision.HIGHEST

def batched(left, right):
    return jnp.einsum('gij,gjk->gik', left, right, precision=PRECISE)

def inv_root(sigma_mat):
    traces = jnp.trace(sigma_mat, axis1=1, axis2=2)
    normed = sigma_mat / traces[:, None, None]
    estimate = jnp.broadcast_to(jnp.eye(sigma_mat.shape[-1], dtype=sigma_mat.dtype), sigma_mat.shape)
    for repeat in range(NS_ITERS):
        cubed = batched(batched(estimate, estimate), estimate)
        estimate = 1.5 * estimate - 0.5 * batched(cubed, normed)
    return estimate / jnp.sqrt(traces)[:, None, None]

def filter_same(source, weights):
    return lax.conv_general_dilated(source, weights, (1, 1), ((1, 1), (1, 1)), dimension_numbers=('NHWC', 'HWIO', 'NHWC'), preferred_element_type=jnp.float32)

def reference(images, kernel, colors, offset, upstream):
    pre = filter_same(images, kernel)
    pixels_all = pre.shape[0] * pre.shape[1] * pre.shape[2]
    raw_cols = pre.reshape(pixels_all, GROUPS, GS)
    average = lax.optimization_barrier(jnp.sum(raw_cols, axis=0)) / pixels_all
    centred = raw_cols - average
    identity = jnp.eye(GS, dtype=centred.dtype)
    sigma_mat = jnp.einsum('pgi,pgj->gij', centred, centred, precision=PRECISE) / pixels_all + EPSILON * identity
    whitener, pullback = jax.vjp(inv_root, sigma_mat)
    whitened = jnp.einsum('gij,pgj->pgi', whitener, centred, precision=PRECISE)
    colored = jnp.einsum('gij,pgj->pgi', colors, whitened, precision=PRECISE) + offset.reshape(GROUPS, GS)
    colored = colored.astype(jnp.bfloat16).reshape(pre.shape)
    upward = upstream.reshape(pixels_all, GROUPS, GS).astype(jnp.float32)
    up_total = lax.optimization_barrier(jnp.sum(upward, axis=0))
    color_sum = jnp.einsum('pgi,pgj->gij', upward, whitened, precision=PRECISE)
    white_grad = jnp.einsum('gji,pgj->pgi', colors, upward, precision=PRECISE)
    whiten_grad = jnp.einsum('pgi,pgj->gij', white_grad, centred, precision=PRECISE)
    sigma_grad, = pullback(whiten_grad)
    symmetric = sigma_grad + jnp.transpose(sigma_grad, (0, 2, 1))
    mean_grad = jnp.einsum('gji,gj->gi', colors, up_total, precision=PRECISE) / pixels_all
    centred_grad = jnp.einsum('gji,pgj->pgi', whitener, white_grad, precision=PRECISE)
    centred_grad = centred_grad + jnp.einsum('gij,pgj->pgi', symmetric, centred, precision=PRECISE) / pixels_all
    pre_grad = centred_grad - jnp.einsum('gji,gj->gi', whitener, mean_grad, precision=PRECISE)
    pre_grad = pre_grad.astype(jnp.bfloat16).reshape(pre.shape)
    flipped = jnp.transpose(kernel[::-1, ::-1], (0, 1, 3, 2))
    grad_images = filter_same(pre_grad, flipped).astype(jnp.bfloat16)
    padded = jnp.pad(images, ((0, 0), (1, 1), (1, 1), (0, 0)))
    grad_flat = pre_grad.reshape(-1, COUT)
    height_n = images.shape[1]
    width_n = images.shape[2]
    outer = []
    for row_off in range(3):
        inner = []
        for col_off in range(3):
            window = padded[:, row_off:row_off + height_n, col_off:col_off + width_n, :].reshape(-1, CIN)
            inner.append(lax.dot_general(window, grad_flat, (((0,), (0,)), ((), ())), preferred_element_type=jnp.float32))
        outer.append(jnp.stack(inner))
    scaling = 1.0 / math.sqrt(pixels_all)
    grad_kernel = jnp.stack(outer) * scaling
    grad_colors = color_sum * scaling
    return (colored, grad_images, grad_kernel, grad_colors)
```

```python
import functools
import math

import jax
import jax.numpy as jnp
from jax import lax
from jax.experimental import pallas as pl
from jax.experimental.pallas import tpu as pltpu
from jax.sharding import PartitionSpec as P

NS_ITERS = 5
EPSILON = 1e-05
F32 = jnp.float32
BF16 = jnp.bfloat16
MIB = 1024 * 1024
AXES = ("dp", "rows")


def device_index():
    return lax.axis_index("dp") * lax.axis_size("rows") + lax.axis_index("rows")


def is_even():
    return lax.axis_index("rows") % 2 == 0


def is_upper(stage):
    index = device_index()
    return index & jnp.where(index & 1 != 0, stage[1], stage[0]) != 0


def stages(devices):
    bits = [1 << i for i in range(devices.bit_length() - 1)]
    plan = [(bit, bit) for bit in bits]
    if len(bits) > 2:
        plan[1:3] = [(2, 4), (4, 2)]
    return plan


def split(value):
    high = value.astype(BF16)
    return high, (value - high.astype(F32)).astype(BF16)


def dot(left, right, dims=((1,), (0,))):
    return lax.dot_general(left, right, (dims, ((), ())), preferred_element_type=F32)


def dot3(left, right):
    lh, ll = split(left)
    rh, rl = split(right)
    return dot(
        jnp.concatenate([lh, lh, ll], axis=1), jnp.concatenate([rh, rl, rh], axis=0)
    )


def shifted(value):
    width = value.shape[1]
    col = lax.broadcasted_iota(jnp.int32, (1, *value.shape[1:]), 1)
    after = jnp.where(col == width - 1, 0.0, pltpu.roll(value, width - 1, 1))
    before = jnp.where(col == 0, 0.0, pltpu.roll(value, 1, 1))
    return after, before


def merged(prod, shape):
    cout = shape[2]
    _, left = shifted(prod[:, :cout].reshape(shape))
    right, _ = shifted(prod[:, 2 * cout :].reshape(shape))
    return prod[:, cout : 2 * cout].reshape(shape) + left + right


def column(row):
    size = row.shape[1]
    return jnp.broadcast_to(row, (size, size)).T


def pack(full):
    half = full.shape[0] // 2
    lane = lax.broadcasted_iota(jnp.int32, (half, full.shape[1]), 1)
    return jnp.where(lane < half, full[:half], full[half:])


def unpack(packed):
    half = packed.shape[0]
    lane = lax.broadcasted_iota(jnp.int32, packed.shape, 1)
    return jnp.concatenate(
        [jnp.where(lane < half, packed, 0.0), jnp.where(lane < half, 0.0, packed)], axis=0
    )


def statistics(held):
    third = held.shape[1] // 3
    return dot(held[:, third:], held[:, : 2 * third], ((0,), (0,)))


def forward_kernel(img, kern, ups, pre_out, acc, sums, wts, held):
    step = pl.program_id(0)
    last = pl.num_programs(0) - 1
    rows, width, cin = img.shape[1:]
    cout = kern.shape[3]
    inner = (rows - 2) * width

    @pl.when(step == 0)
    def _():
        for a in range(3):
            for c in range(3):
                wts[a * cin : (a + 1) * cin, c * cout : (c + 1) * cout] = kern[a, c]
        acc[...] = jnp.zeros_like(acc)
        sums[...] = jnp.zeros_like(sums)
        held[...] = jnp.zeros_like(held)

    acc[...] += statistics(held[...])
    blank = jnp.zeros((1, width, cin), BF16)
    padded = jnp.concatenate([blank, img[0], blank], axis=0)
    wide = jnp.concatenate([padded[a : a + rows] for a in range(3)], axis=2)
    prod = dot(wide.reshape(rows * width, 3 * cin), wts[...])
    pre = merged(prod, (rows, width, cout))
    pre_out[0] = pre
    mid = pre[1 : rows - 1].reshape(inner, cout)
    mean = jnp.sum(mid, axis=0, keepdims=True) / inner
    shift = jnp.where(step == 0, mean, sums[2:3])
    sums[2:3] = shift
    delta = mid - shift
    up = ups[0, 1 : rows - 1].reshape(inner, cout)
    high, low = split(delta)
    held[:, :cout] = low
    held[:, cout : 2 * cout] = high
    held[:, 2 * cout :] = up
    sums[0:1] += jnp.sum(delta, axis=0, keepdims=True)
    sums[1:2] += jnp.sum(up.astype(F32), axis=0, keepdims=True)

    @pl.when(step == last)
    def _():
        acc[...] += statistics(held[...])


def sides(ahead, across):
    even = is_even()
    return jnp.where(even, across, ahead), jnp.where(even, ahead, across)


def slice_kernel(first, final, ahead, across):
    across[...], ahead[...] = sides(final[...], first[...])


def edge_kernel(
    total,
    stage,
    ahead,
    across,
    pre_top,
    pre_bot,
    ups_top,
    ups_bot,
    kern,
    acc,
    sums,
    low,
    high,
    keep,
    send,
    stats,
):
    count, _, width, cin = ahead.shape
    cout = kern.shape[3]
    top, bot = sides(ahead[...], across[...])
    pixels = count * width
    shape = (count, width, cout)
    edges = []
    for a, source, part, out in ((0, top, pre_top, low), (2, bot, pre_bot, high)):
        taps = jnp.concatenate([kern[a, c] for c in range(3)], axis=1)
        value = merged(dot(source.reshape(pixels, cin), taps), shape) + part[:, 0]
        out[:, 0] = value
        edges.append(value.reshape(pixels, cout))
    shift = sums[2:3]
    delta = jnp.concatenate(edges, axis=0) - shift
    up = jnp.concatenate(
        [ups_top[...].reshape(pixels, cout), ups_bot[...].reshape(pixels, cout)], axis=0
    )
    big, small = split(delta)
    gram = acc[...] + statistics(jnp.concatenate([small, big, up], axis=1))
    moved = sums[0:1] + jnp.sum(delta, axis=0, keepdims=True)
    up_sum = sums[1:2] + jnp.sum(up.astype(F32), axis=0, keepdims=True)
    mixed = gram[:cout, :cout]
    square = gram[:cout, cout:] + mixed + mixed.T
    cross = gram[cout:, :cout] + gram[cout:, cout:]
    raw = moved + total * shift
    square = square + column(moved) * shift + column(shift) * raw
    cross = cross + column(up_sum) * shift
    half = cout // 2
    stats[0:half] = pack(square)
    stats[half : 2 * half] = pack(cross)
    stats[2 * half :] = jnp.zeros_like(stats[2 * half :])
    stats[2 * half : 2 * half + 1] = raw
    stats[2 * half + 1 : 2 * half + 2] = up_sum
    part = keep.shape[0]
    upper = is_upper(stage)
    keep[...] = jnp.where(upper, stats[part:], stats[:part])
    send[...] = jnp.where(upper, stats[:part], stats[part:])


def spread(blocks):
    zero = jnp.zeros(blocks.shape[1:], F32)
    return jnp.concatenate(
        [
            jnp.concatenate([blocks[0], zero], axis=1),
            jnp.concatenate([zero, blocks[1]], axis=1),
        ],
        axis=0,
    )


def group_sum(value, half):
    cols = jnp.sum(value, axis=0, keepdims=True)
    lane = lax.broadcasted_iota(jnp.int32, cols.shape, 1)
    low = jnp.sum(jnp.where(lane < half, cols, 0.0), axis=1, keepdims=True)
    high = jnp.sum(jnp.where(lane < half, 0.0, cols), axis=1, keepdims=True)
    return jnp.where(lane < half, low, high)


def whitening(stats, colors, offset, total_pix, half):
    cout = 2 * half
    row_i = lax.broadcasted_iota(jnp.int32, (cout, cout), 0)
    col_i = lax.broadcasted_iota(jnp.int32, (cout, cout), 1)
    eye = jnp.where(row_i == col_i, 1.0, 0.0)
    block = jnp.where((row_i < half) == (col_i < half), 1.0, 0.0)
    square = unpack(stats[0:half])
    cross = unpack(stats[half : 2 * half])
    average = stats[2 * half : 2 * half + 1] / total_pix
    up_total = stats[2 * half + 1 : 2 * half + 2]
    sigma = square / total_pix - block * (column(average) * average) + EPSILON * eye
    cross = cross - block * (column(up_total) * average)
    grad = dot3(colors.T, cross)
    direction = grad + grad.T
    traces = group_sum(sigma * eye, half)
    normed = sigma / traces
    zero = jnp.zeros_like(normed)

    def stacked(value, tangent):
        return jnp.concatenate(
            [
                jnp.concatenate([value, tangent], axis=1),
                jnp.concatenate([zero, value], axis=1),
            ],
            axis=0,
        )

    source = stacked(normed, direction)
    value = 1.5 * eye - 0.5 * normed
    tangent = -0.5 * direction
    for _ in range(NS_ITERS - 1):
        first = jnp.concatenate([value, tangent], axis=1)
        both = dot3(first, jnp.concatenate([stacked(value, tangent), source], axis=1))
        squared = both[:, : 2 * cout]
        scaled = stacked(both[:, 2 * cout : 3 * cout], both[:, 3 * cout :])
        cubed = dot3(squared, scaled)
        value = 1.5 * value - 0.5 * cubed[:, :cout]
        tangent = 1.5 * tangent - 0.5 * cubed[:, cout:]
    inverse = 1.0 / jnp.sqrt(traces)
    whitener = value * inverse
    shared = group_sum(tangent * normed, half) + 0.5 * group_sum(direction * value, half)
    symmetric = (tangent - eye * shared) * (inverse / traces)
    mixed = dot3(colors, whitener)
    color_sum = dot3(cross, whitener.T)
    up_mean = jnp.broadcast_to(up_total / total_pix, (8, cout))
    bias = -dot3(up_mean, mixed)[0:1]
    return average, mixed, symmetric / total_pix, bias, offset, color_sum


def backward_kernel(
    total_pix,
    stage,
    own,
    other,
    colors,
    offset,
    pre,
    low,
    high,
    ups,
    img,
    ahead,
    across,
    colored,
    pre_grad,
    edge_ahead,
    edge_across,
    keep,
    send,
    grad_colors,
    stats,
    mats,
    rowsbuf,
    acc,
    turned,
):
    step = pl.program_id(0)
    last = pl.num_programs(0) - 1
    rows, width, cin = img.shape[1:]
    cout = pre.shape[3]
    half = cout // 2
    pixels = rows * width
    scaling = 1.0 / math.sqrt(total_pix)

    @pl.when(step == 0)
    def _():
        join_kernel(stage, own, other, stats)
        average, mixed, symmetric, bias, offs, color_sum = whitening(
            stats[...], spread(colors[...]), offset[...], total_pix, half
        )
        zero = jnp.zeros((cout, cout), BF16)
        mixed_h, mixed_l = split(mixed)
        color_h, color_l = split(mixed.T)
        sym_h, sym_l = split(symmetric)
        for index, (one, two) in enumerate(
            ((sym_h, color_h), (sym_h, color_h), (sym_l, color_l), (mixed_h, zero), (mixed_l, zero))
        ):
            mats[index * cout : (index + 1) * cout, :cout] = one
            mats[index * cout : (index + 1) * cout, cout:] = two
        rowsbuf[0:1, :cout] = average
        rowsbuf[1:2, :cout] = bias
        rowsbuf[1:2, cout:] = offs
        scaled = color_sum * scaling
        grad_colors[0] = scaled[:half, :half]
        grad_colors[1] = pltpu.roll(scaled[half:], half, 1)[:, :half]
        acc[...] = jnp.zeros_like(acc)
        turned[...] = jnp.zeros_like(turned)

    top, bot = sides(ahead[0], across[0])
    padded = jnp.concatenate([top, img[0], bot], axis=0)
    for a in range(3):
        acc[a] += dot(turned[...], padded[a : a + rows].reshape(pixels, cin))
    full = jnp.concatenate([low[0], pre[0, 1 : rows - 1], high[0]], axis=0)
    centred = full.reshape(pixels, cout) - rowsbuf[0:1, :cout]
    big, small = split(centred)
    up = ups[0].reshape(pixels, cout)
    result = dot(jnp.concatenate([big, small, big, up, up], axis=1), mats[...]) + rowsbuf[1:2]
    colored[0] = result[:, cout:].astype(BF16).reshape(rows, width, cout)
    grad = result[:, :cout].astype(BF16)
    shaped = grad.reshape(rows, width, cout)
    pre_grad[0] = shaped
    edge_across[0], edge_ahead[0] = sides(shaped[rows - 1 :], shaped[:1])
    after, before = shifted(shaped.astype(F32))
    after = after.astype(BF16).reshape(pixels, cout)
    before = before.astype(BF16).reshape(pixels, cout)
    turned[:cout] = after.T
    turned[cout : 2 * cout] = grad.T
    turned[2 * cout :] = before.T

    @pl.when(step == last)
    def _():
        upper = is_upper(stage)
        parts = [
            acc[tap // 3, tap % 3 * cout : (tap % 3 + 1) * cout, piece * cin // 2 : (piece + 1) * cin // 2].T
            * scaling
            for tap in range(9)
            for piece in range(2)
        ]
        for index in range(9):
            place = slice(index * cin // 2, (index + 1) * cin // 2)
            keep[place] = jnp.where(upper, parts[9 + index], parts[index])
            send[place] = jnp.where(upper, parts[index], parts[9 + index])


def turn_kernel(kern, out):
    cout = kern.shape[3]
    for a in range(3):
        for c in range(3):
            tap = (a * 3 + c) * cout
            out[tap : tap + cout] = kern[a, c].T


def image_kernel(pre_grad, ahead, across, wts, *rest):
    out = rest[-1]
    top, bot = sides(ahead[0], across[0])
    rows, width, cout = pre_grad.shape[1:]
    cin = wts.shape[1]
    exact = jnp.concatenate([top, pre_grad[0], bot], axis=0).astype(F32)
    after, before = shifted(exact)
    taps = [value.astype(BF16) for value in (after, exact, before)]
    wide = jnp.concatenate(
        [taps[c][2 - a : 2 - a + rows] for a in range(3) for c in range(3)], axis=2
    )
    result = dot(wide.reshape(rows * width, 9 * cout), wts[...])
    out[0] = result.astype(BF16).reshape(rows, width, cin)


def fold_kernel(stage, value, received, keep, send):
    upper = is_upper(stage)
    part = keep.shape[0]
    low = value[:part] + received[:part]
    high = value[part:] + received[part:]
    keep[...] = jnp.where(upper, high, low)
    send[...] = jnp.where(upper, low, high)


def join_kernel(stage, value, received, out):
    upper = is_upper(stage)
    part = value.shape[0]
    out[:part] = jnp.where(upper, received[...], value[...])
    out[part:] = jnp.where(upper, value[...], received[...])


def finish_kernel(stage, value, received, out):
    size = out.shape[0]
    steps = value.shape[0] // size
    step = pl.program_id(0)
    place = pl.ds(pl.multiple_of(step % steps * size, size), size)
    own = is_upper(stage) == (step >= steps)
    out[...] = jnp.where(own, value[place], received[place]).astype(F32)


def image_spec(shape, place=lambda b: b):
    return pl.BlockSpec((1, *shape[1:]), lambda b: (place(b),) + (0,) * (len(shape) - 1))


def whole_spec(shape):
    return pl.BlockSpec(shape, lambda b: (0,) * len(shape))


def in_hbm(value):
    return pltpu.with_memory_space_constraint(value, pltpu.HBM)


def resident():
    return pl.BlockSpec(memory_space=pltpu.VMEM)


def row_spec(shape, row):
    return pl.BlockSpec((shape[0], 1, *shape[2:]), lambda b: (0, row, 0, 0))


def forward(images, kernel, upstream):
    count, rows, width, cin = images.shape
    cout = kernel.shape[3]
    pre_shape = (count, rows, width, cout)
    return pl.pallas_call(
        forward_kernel,
        grid=(count,),
        in_specs=[
            image_spec(images.shape),
            whole_spec(kernel.shape),
            image_spec(upstream.shape),
        ],
        out_specs=[
            image_spec(pre_shape),
            whole_spec((2 * cout, 2 * cout)),
            whole_spec((8, cout)),
        ],
        out_shape=[
            jax.ShapeDtypeStruct(pre_shape, F32),
            jax.ShapeDtypeStruct((2 * cout, 2 * cout), F32),
            jax.ShapeDtypeStruct((8, cout), F32),
        ],
        scratch_shapes=[
            pltpu.VMEM((3 * cin, 3 * cout), BF16),
            pltpu.VMEM(((rows - 2) * width, 3 * cout), BF16),
        ],
        compiler_params=pltpu.CompilerParams(vmem_limit_bytes=20 * MIB),
        cost_estimate=pl.CostEstimate(
            flops=2 * count * rows * width * 9 * cin * cout,
            bytes_accessed=2 * images.size + 2 * upstream.size + 4 * upstream.size,
            transcendentals=0,
        ),
        name="forward_inner",
    )(
        in_hbm(images), in_hbm(kernel), in_hbm(upstream)
    )


def edges(stage, top, bot, pre, upstream, kernel, acc, sums):
    count, rows, width, cout = pre.shape
    edge = (count, 1, width, cout)

    part = (cout + 16) // 2
    shapes = [edge, edge, (part, cout), (part, cout)]
    return pl.pallas_call(
        functools.partial(edge_kernel, count * rows * width, stage),
        grid=(1,),
        in_specs=[
            resident(),
            resident(),
            row_spec(pre.shape, 0),
            row_spec(pre.shape, rows - 1),
            row_spec(upstream.shape, 0),
            row_spec(upstream.shape, rows - 1),
            resident(),
            resident(),
            resident(),
        ],
        out_specs=[whole_spec(edge), whole_spec(edge), resident(), resident()],
        out_shape=[jax.ShapeDtypeStruct(shape, F32) for shape in shapes],
        scratch_shapes=[pltpu.VMEM((2 * part, cout), F32)],
        compiler_params=pltpu.CompilerParams(vmem_limit_bytes=12 * MIB),
        cost_estimate=pl.CostEstimate(
            flops=2 * 2 * count * width * 3 * top.shape[3] * cout,
            bytes_accessed=4 * top.size + 24 * count * width * cout,
            transcendentals=0,
        ),
        name="forward_edges",
    )(top, bot, pre, pre, upstream, upstream, kernel, acc, sums)


def backward(total_pix, stage, own, other, colors, offset, pre, low, high, upstream, images, top, bot):
    count, rows, width, cin = images.shape
    cout = upstream.shape[3]
    half = cout // 2
    edge = (count, 1, width, cout)

    def here(b):
        return jnp.minimum(b, count - 1)

    def behind(b):
        return jnp.maximum(b - 1, 0)

    out_shapes = [
        (upstream.shape, BF16),
        (upstream.shape, BF16),
        (edge, BF16),
        (edge, BF16),
        ((9 * cin // 2, cout), F32),
        ((9 * cin // 2, cout), F32),
        ((2, half, half), F32),
    ]
    return pl.pallas_call(
        functools.partial(backward_kernel, total_pix, stage),
        grid=(count + 1,),
        in_specs=[
            resident(),
            resident(),
            resident(),
            resident(),
            image_spec(pre.shape, here),
            image_spec(low.shape, here),
            image_spec(high.shape, here),
            image_spec(upstream.shape, here),
            image_spec(images.shape, behind),
            image_spec(top.shape, behind),
            image_spec(bot.shape, behind),
        ],
        out_specs=[image_spec(shape, here) for shape, _ in out_shapes[:4]]
        + [resident(), resident(), resident()],
        out_shape=[jax.ShapeDtypeStruct(shape, dtype) for shape, dtype in out_shapes],
        scratch_shapes=[
            pltpu.VMEM((cout + 16, cout), F32),
            pltpu.VMEM((5 * cout, 2 * cout), BF16),
            pltpu.VMEM((8, 2 * cout), F32),
            pltpu.VMEM((3, 3 * cout, cin), F32),
            pltpu.VMEM((3 * cout, rows * width), BF16),
        ],
        compiler_params=pltpu.CompilerParams(vmem_limit_bytes=20 * MIB),
        cost_estimate=pl.CostEstimate(
            flops=2 * count * rows * width * 11 * cin * cout,
            bytes_accessed=2 * images.size + 10 * upstream.size,
            transcendentals=0,
        ),
        name="whitening_backward",
    )(own, other, colors, offset, pre, low, high, upstream, images, top, bot)


def turned_weights(kernel):
    cin, cout = kernel.shape[2:]
    return pl.pallas_call(
        turn_kernel,
        out_shape=jax.ShapeDtypeStruct((9 * cout, cin), BF16),
        compiler_params=pltpu.CompilerParams(vmem_limit_bytes=4 * MIB),
        name="turned_weights",
    )(kernel)


def image_gradient(first, count, pre_grad, top, bot, turned, out=None):
    images, rows, width, cout = pre_grad.shape
    cin = turned.shape[1]
    shape = (images, rows, width, cin)

    def place(b):
        return b + first

    operands = [pre_grad, top, bot, turned]
    in_specs = [image_spec(part.shape, place) for part in operands[:3]]
    in_specs.append(whole_spec(turned.shape))
    aliases = {}
    if out is not None:
        operands.append(out)
        in_specs.append(pl.BlockSpec(memory_space=pl.ANY))
        aliases = {4: 0}
    return pl.pallas_call(
        image_kernel,
        grid=(count,),
        in_specs=in_specs,
        out_specs=image_spec(shape, place),
        out_shape=jax.ShapeDtypeStruct(shape, BF16),
        input_output_aliases=aliases,
        compiler_params=pltpu.CompilerParams(vmem_limit_bytes=12 * MIB),
        cost_estimate=pl.CostEstimate(
            flops=2 * count * rows * width * 9 * cin * cout,
            bytes_accessed=2 * count * rows * width * (cin + cout),
            transcendentals=0,
        ),
        name="image_gradient",
    )(*operands)


def sliced(images):
    count, rows, width, cin = images.shape
    shape = (count, 1, width, cin)
    source = in_hbm(images)
    return pl.pallas_call(
        slice_kernel,
        grid=(1,),
        in_specs=[row_spec(images.shape, 0), row_spec(images.shape, rows - 1)],
        out_specs=[resident(), resident()],
        out_shape=[jax.ShapeDtypeStruct(shape, BF16)] * 2,
        compiler_params=pltpu.CompilerParams(vmem_limit_bytes=8 * MIB),
        name="edge_rows",
    )(source, source)


def small_call(kernel, name, *operands, out):
    return pl.pallas_call(
        kernel,
        in_specs=[resident()] * len(operands),
        out_specs=[resident()] * len(out),
        out_shape=out,
        compiler_params=pltpu.CompilerParams(vmem_limit_bytes=4 * MIB),
        name=name,
    )(*operands)


def fold(value, received, stage):
    half = jax.ShapeDtypeStruct((value.shape[0] // 2, value.shape[1]), value.dtype)
    return small_call(
        functools.partial(fold_kernel, stage), "fold", value, received, out=[half, half]
    )


def join(value, received, stage):
    whole = jax.ShapeDtypeStruct((value.shape[0] * 2, value.shape[1]), value.dtype)
    return small_call(
        functools.partial(join_kernel, stage), "join", value, received, out=[whole]
    )[0]


def finish(value, received, stage):
    part, lanes = value.shape
    size = part // 2
    return pl.pallas_call(
        functools.partial(finish_kernel, stage),
        grid=(4,),
        in_specs=[resident(), resident()],
        out_specs=pl.BlockSpec((size, lanes), lambda b: (b, 0)),
        out_shape=jax.ShapeDtypeStruct((2 * part, lanes), F32),
        compiler_params=pltpu.CompilerParams(vmem_limit_bytes=8 * MIB),
        name="finish",
    )(value, received)


def halos(ahead, across):
    count = lax.axis_size("rows")
    pairs = []
    for first in (0, 1):
        found = [(i, i + 1) for i in range(first, count - 1, 2)]
        pairs.append(found + [(i, j) for j, i in found])
    return lax.ppermute(ahead, "rows", pairs[0]), lax.ppermute(across, "rows", pairs[1])


def exchange(value, devices, stage):
    pairs = [(i, i ^ (stage[1] if i & 1 else stage[0])) for i in range(devices)]
    return lax.ppermute(value, AXES, pairs)


def beside(send, devices, stage, task, operands):
    send, operands = lax.optimization_barrier((send, operands))
    received = exchange(send, devices, stage)
    result = task(*operands)
    return lax.optimization_barrier((received, result))


def body(images, kernel, colors, offset, upstream):
    count, rows, width, cin = images.shape
    cout = kernel.shape[3]
    devices = lax.axis_size("dp") * lax.axis_size("rows")
    total_pix = count * rows * width * devices
    plan = stages(devices)
    top, bot = halos(*sliced(images))
    pre, acc, sums = forward(images, kernel, upstream)
    low, high, value, send = edges(plan[0], top, bot, pre, upstream, kernel, acc, sums)
    value = value + exchange(send, devices, plan[0])
    for stage in plan[1:-1]:
        value = value + exchange(value, devices, stage)
    received, turned = beside(value, devices, plan[-1], turned_weights, (kernel,))
    value = value + received
    received = exchange(value, devices, plan[0])
    colored, pre_grad, edge_ahead, edge_across, value, send, grad_colors = backward(
        total_pix,
        plan[0],
        value,
        received,
        colors,
        offset.reshape(1, cout),
        pre,
        low,
        high,
        upstream,
        images,
        top,
        bot,
    )
    shares = [1, 1, 2, 1, 1]
    state = {"next": 0, "grad": None}

    def transfer(send, stage):
        first = state["next"]
        if first >= count:
            return exchange(send, devices, stage)
        many = min(shares.pop(0), count - first) if shares else count - first
        state["next"] = first + many
        operands = (pre_grad, grad_top, grad_bot, turned)
        if state["grad"] is not None:
            operands = (*operands, state["grad"])
        received, state["grad"] = beside(
            send, devices, stage, functools.partial(image_gradient, first, many), operands
        )
        return received

    cuts = []
    received = exchange(send, devices, plan[0])
    for stage in plan[1:]:
        if value.shape[0] % 32 == 0 and value.shape[0] > 144:
            value, send = fold(value, received, stage)
            cuts.append(stage)
        else:
            value = send = value + received
        if stage == plan[1]:
            received, (grad_top, grad_bot) = beside(
                send, devices, stage, halos, (edge_ahead, edge_across)
            )
        else:
            received = transfer(send, stage)
    value = (value + received).astype(BF16)
    for stage in reversed(cuts):
        value = join(value, transfer(value, stage), stage)
    grad_kernel = finish(value, exchange(value, devices, plan[0]), plan[0])
    return colored, state["grad"], grad_kernel.reshape(3, 3, cin, cout), grad_colors


def solution(mesh):
    placed = (P("dp", "rows", None, None), P(), P(), P(), P("dp", "rows", None, None))
    return jax.shard_map(
        body,
        mesh=mesh,
        in_specs=placed,
        out_specs=(P("dp", "rows", None, None), P("dp", "rows", None, None), P(), P()),
        check_vma=False,
    )
```

```python
import functools
import math

import jax
import jax.numpy as jnp
from jax import lax
from jax.experimental import pallas as pl
from jax.experimental.pallas import tpu as pltpu
from jax.sharding import PartitionSpec as P

NS_ITERS = 5
EPSILON = 1e-05
F32 = jnp.float32
BF16 = jnp.bfloat16
MIB = 1024 * 1024
AXES = ("dp", "rows")


def device_index():
    return lax.axis_index("dp") * lax.axis_size("rows") + lax.axis_index("rows")


def is_even():
    return lax.axis_index("rows") % 2 == 0


def is_upper(stage):
    index = device_index()
    return index & jnp.where(index & 1 != 0, stage[1], stage[0]) != 0


def stages(devices):
    bits = [1 << i for i in range(devices.bit_length() - 1)]
    plan = [(bit, bit) for bit in bits]
    if len(bits) > 2:
        plan[1:3] = [(2, 4), (4, 2)]
    return plan


def split(value):
    high = value.astype(BF16)
    return high, (value - high.astype(F32)).astype(BF16)


def dot(left, right, dims=((1,), (0,))):
    return lax.dot_general(left, right, (dims, ((), ())), preferred_element_type=F32)


def dot3(left, right):
    lh, ll = split(left)
    rh, rl = split(right)
    return dot(
        jnp.concatenate([lh, lh, ll], axis=1), jnp.concatenate([rh, rl, rh], axis=0)
    )


def shifted(value):
    width = value.shape[1]
    col = lax.broadcasted_iota(jnp.int32, (1, *value.shape[1:]), 1)
    after = jnp.where(col == width - 1, 0.0, pltpu.roll(value, width - 1, 1))
    before = jnp.where(col == 0, 0.0, pltpu.roll(value, 1, 1))
    return after, before


def merged(prod, shape):
    cout = shape[2]
    _, left = shifted(prod[:, :cout].reshape(shape))
    right, _ = shifted(prod[:, 2 * cout :].reshape(shape))
    return prod[:, cout : 2 * cout].reshape(shape) + left + right


def paired_rows(padded, wts, cout):
    rows, width, cin = padded.shape[0] - 2, *padded.shape[1:]
    pairs = rows // 2
    parts = [
        jnp.concatenate([padded[2 * k + a : 2 * k + a + 1] for k in range(pairs)], axis=0)
        for a in range(4)
    ]
    wide = jnp.concatenate(parts, axis=2).reshape(pairs * width, 4 * cin)
    outer = dot(wide[:, : 3 * cin], wts[: 3 * cin])
    shared = dot(wide, wts[3 * cin : 7 * cin])
    inner = dot(wide[:, cin:], wts[7 * cin :])
    shape = (pairs, width, cout)

    def added_up(left, middle, right):
        _, before = shifted(left.reshape(shape))
        after, _ = shifted(right.reshape(shape))
        return middle.reshape(shape) + before + after

    first = added_up(outer[:, :cout], outer[:, cout:], shared[:, :cout])
    second = added_up(shared[:, cout:], inner[:, :cout], inner[:, cout:])
    ordered = [part[k : k + 1] for k in range(pairs) for part in (first, second)]
    return jnp.concatenate(ordered, axis=0)


def column(row):
    size = row.shape[1]
    return jnp.broadcast_to(row, (size, size)).T


def pack(full):
    half = full.shape[0] // 2
    lane = lax.broadcasted_iota(jnp.int32, (half, full.shape[1]), 1)
    return jnp.where(lane < half, full[:half], full[half:])


def unpack(packed):
    half = packed.shape[0]
    lane = lax.broadcasted_iota(jnp.int32, packed.shape, 1)
    return jnp.concatenate(
        [jnp.where(lane < half, packed, 0.0), jnp.where(lane < half, 0.0, packed)], axis=0
    )


def statistics(held):
    third = held.shape[1] // 3
    return dot(held[:, third:], held[:, : 2 * third], ((0,), (0,)))


def forward_kernel(img, kern, ups, pre_out, acc, sums, wts, held):
    step = pl.program_id(0)
    last = pl.num_programs(0) - 1
    rows, width, cin = img.shape[1:]
    cout = kern.shape[3]
    inner = (rows - 2) * width

    @pl.when(step == 0)
    def _():
        blank = jnp.zeros((cin, cout), BF16)
        blocks = [(kern[a, 0], kern[a, 1]) for a in range(3)]
        blocks += [
            (kern[a, 2] if a < 3 else blank, kern[a - 1, 0] if a > 0 else blank) for a in range(4)
        ]
        blocks += [(kern[a, 1], kern[a, 2]) for a in range(3)]
        for index, (one, two) in enumerate(blocks):
            wts[index * cin : (index + 1) * cin, :cout] = one
            wts[index * cin : (index + 1) * cin, cout:] = two
        acc[...] = jnp.zeros_like(acc)
        sums[...] = jnp.zeros_like(sums)
        held[...] = jnp.zeros_like(held)

    acc[...] += statistics(held[...])
    blank = jnp.zeros((1, width, cin), BF16)
    padded = jnp.concatenate([blank, img[0], blank], axis=0)
    pre = paired_rows(padded, wts, cout)
    pre_out[step] = pre
    mid = pre[1 : rows - 1].reshape(inner, cout)
    mean = jnp.sum(mid, axis=0, keepdims=True) / inner
    shift = jnp.where(step == 0, mean, sums[2:3])
    sums[2:3] = shift
    delta = mid - shift
    up = ups[0, 1 : rows - 1].reshape(inner, cout)
    high, low = split(delta)
    held[:, :cout] = low
    held[:, cout : 2 * cout] = high
    held[:, 2 * cout :] = up
    sums[0:1] += jnp.sum(delta, axis=0, keepdims=True)
    sums[1:2] += jnp.sum(up.astype(F32), axis=0, keepdims=True)

    @pl.when(step == last)
    def _():
        acc[...] += statistics(held[...])


def sides(ahead, across):
    even = is_even()
    return jnp.where(even, across, ahead), jnp.where(even, ahead, across)


def slice_kernel(images, ahead, across, sems):
    last = images.shape[1] - 1
    even = is_even()
    copies = [
        pltpu.make_async_copy(images.at[:, pl.ds(row, 1)], target, sems.at[index])
        for index, (row, target) in enumerate(
            ((jnp.where(even, last, 0), ahead), (jnp.where(even, 0, last), across))
        )
    ]
    for copy in copies:
        copy.start()
    for copy in copies:
        copy.wait()


def edge_kernel(total, stage, ahead, across, pre, ups, kern, acc, sums, low, high, keep, send, stats):
    count, _, width, cin = ahead.shape
    cout = kern.shape[3]
    last = pre.shape[1] - 1
    top, bot = sides(ahead[...], across[...])
    pixels = count * width
    shape = (count, width, cout)
    edges = []
    for a, source, row, out in ((0, top, 0, low), (2, bot, last, high)):
        taps = jnp.concatenate([kern[a, c] for c in range(3)], axis=1)
        value = merged(dot(source.reshape(pixels, cin), taps), shape) + pre[:, row]
        out[:, 0] = value
        edges.append(value.reshape(pixels, cout))
    shift = sums[2:3]
    delta = jnp.concatenate(edges, axis=0) - shift
    up = jnp.concatenate(
        [ups[:, 0].reshape(pixels, cout), ups[:, last].reshape(pixels, cout)], axis=0
    )
    big, small = split(delta)
    gram = acc[...] + statistics(jnp.concatenate([small, big, up], axis=1))
    moved = sums[0:1] + jnp.sum(delta, axis=0, keepdims=True)
    up_sum = sums[1:2] + jnp.sum(up.astype(F32), axis=0, keepdims=True)
    mixed = gram[:cout, :cout]
    square = gram[:cout, cout:] + mixed + mixed.T
    cross = gram[cout:, :cout] + gram[cout:, cout:]
    raw = moved + total * shift
    square = square + column(moved) * shift + column(shift) * raw
    cross = cross + column(up_sum) * shift
    half = cout // 2
    stats[0:half] = pack(square)
    stats[half : 2 * half] = pack(cross)
    stats[2 * half :] = jnp.zeros_like(stats[2 * half :])
    stats[2 * half : 2 * half + 1] = raw
    stats[2 * half + 1 : 2 * half + 2] = up_sum
    part = keep.shape[0]
    upper = is_upper(stage)
    keep[...] = jnp.where(upper, stats[part:], stats[:part])
    send[...] = jnp.where(upper, stats[:part], stats[part:])


def spread(blocks):
    zero = jnp.zeros(blocks.shape[1:], F32)
    return jnp.concatenate(
        [
            jnp.concatenate([blocks[0], zero], axis=1),
            jnp.concatenate([zero, blocks[1]], axis=1),
        ],
        axis=0,
    )


def group_sum(value, half):
    cols = jnp.sum(value, axis=0, keepdims=True)
    lane = lax.broadcasted_iota(jnp.int32, cols.shape, 1)
    low = jnp.sum(jnp.where(lane < half, cols, 0.0), axis=1, keepdims=True)
    high = jnp.sum(jnp.where(lane < half, 0.0, cols), axis=1, keepdims=True)
    return jnp.where(lane < half, low, high)


def whitening(stats, colors, offset, total_pix, half):
    cout = 2 * half
    row_i = lax.broadcasted_iota(jnp.int32, (cout, cout), 0)
    col_i = lax.broadcasted_iota(jnp.int32, (cout, cout), 1)
    eye = jnp.where(row_i == col_i, 1.0, 0.0)
    block = jnp.where((row_i < half) == (col_i < half), 1.0, 0.0)
    square = unpack(stats[0:half])
    cross = unpack(stats[half : 2 * half])
    average = stats[2 * half : 2 * half + 1] / total_pix
    up_total = stats[2 * half + 1 : 2 * half + 2]
    sigma = square / total_pix - block * (column(average) * average) + EPSILON * eye
    cross = cross - block * (column(up_total) * average)
    grad = dot3(colors.T, cross)
    direction = grad + grad.T
    traces = group_sum(sigma * eye, half)
    normed = sigma / traces
    zero = jnp.zeros_like(normed)

    def stacked(value, tangent):
        return jnp.concatenate(
            [
                jnp.concatenate([value, tangent], axis=1),
                jnp.concatenate([zero, value], axis=1),
            ],
            axis=0,
        )

    source = stacked(normed, direction)
    value = 1.5 * eye - 0.5 * normed
    tangent = -0.5 * direction
    for _ in range(NS_ITERS - 1):
        first = jnp.concatenate([value, tangent], axis=1)
        both = dot3(first, jnp.concatenate([stacked(value, tangent), source], axis=1))
        squared = both[:, : 2 * cout]
        scaled = stacked(both[:, 2 * cout : 3 * cout], both[:, 3 * cout :])
        cubed = dot3(squared, scaled)
        value = 1.5 * value - 0.5 * cubed[:, :cout]
        tangent = 1.5 * tangent - 0.5 * cubed[:, cout:]
    inverse = 1.0 / jnp.sqrt(traces)
    whitener = value * inverse
    shared = group_sum(tangent * normed, half) + 0.5 * group_sum(direction * value, half)
    symmetric = (tangent - eye * shared) * (inverse / traces)
    mixed = dot3(colors, whitener)
    color_sum = dot3(cross, whitener.T)
    up_mean = jnp.broadcast_to(up_total / total_pix, (8, cout))
    bias = -dot3(up_mean, mixed)[0:1]
    return average, mixed, symmetric / total_pix, bias, offset, color_sum


def moment_kernel(image, pre, low, high, ups, img, ahead, across, sums, *rest):
    acc, maps = rest[-2:]
    rows, width, cin = img.shape[1:]
    cout = pre.shape[3]
    pixels = rows * width
    top, bot = sides(ahead[image], across[image])
    padded = jnp.concatenate([top, img[image], bot], axis=0)
    turned = padded.reshape((rows + 2) * width, cin).T
    full = jnp.concatenate([low[image], pre[image, 1 : rows - 1], high[image]], axis=0)
    columns = []
    for value in (ups[image], (full - sums[2:3]).astype(BF16)):
        after, before = shifted(value.astype(F32))
        columns += [after.astype(BF16), value, before.astype(BF16)]
    right = jnp.concatenate(columns, axis=2).reshape(pixels, 6 * cout)
    left = jnp.concatenate([turned[:, a * width : a * width + pixels] for a in range(3)], axis=0)
    product = dot(left, right)
    tiles = [turned[:, row * width : (row + 1) * width].astype(F32) for row in range(rows + 2)]
    middle = functools.reduce(jnp.add, tiles[2:rows])
    outer = ((0, 1), (1, rows), (rows, rows + 1))
    totals = jnp.concatenate([middle + tiles[one] + tiles[two] for one, two in outer], axis=0)
    if len(rest) == 4:
        product = rest[0][...] + product
        totals = rest[1][...] + totals
    acc[...] = product
    maps[...] = totals


def whitening_kernel(
    total_pix,
    stage,
    own,
    other,
    colors,
    offset,
    sums,
    acc,
    maps,
    keep,
    send,
    grad_colors,
    mats,
    paint,
    paint_rows,
    stats,
):
    cout = 2 * colors.shape[1]
    half = cout // 2
    cin = acc.shape[0] // 3
    scaling = 1.0 / math.sqrt(total_pix)
    join_kernel(stage, own, other, stats)
    average, mixed, symmetric, bias, offs, color_sum = whitening(
        stats[...], spread(colors[...]), offset[...], total_pix, half
    )
    blank = jnp.zeros((cout, cout), BF16)
    mixed_h, mixed_l = split(mixed)
    color_h, color_l = split(mixed.T)
    sym_h, sym_l = split(symmetric)
    for target, blocks in (
        (mats, ((sym_h, sym_l), (mixed_h, mixed_l), (sym_h, blank))),
        (paint, ((color_h, color_l), (color_h, blank))),
    ):
        for index, (one, two) in enumerate(blocks):
            target[index * cout : (index + 1) * cout, :cout] = one
            target[index * cout : (index + 1) * cout, cout:] = two
    paint_rows[...] = jnp.zeros_like(paint_rows)
    paint_rows[0:1] = average
    paint_rows[1:2] = offs
    paint_rows[2:3] = bias
    scaled = color_sum * scaling
    grad_colors[0] = scaled[:half, :half]
    grad_colors[1] = pltpu.roll(scaled[half:], half, 1)[:, :half]

    moved = jnp.broadcast_to(sums[2:3] - average, (8, cout))
    constant = (bias + dot3(moved, symmetric)[0:1]) * scaling
    tall_h = jnp.concatenate([mixed_h, sym_h], axis=0)
    tall_l = jnp.concatenate([mixed_l, sym_l], axis=0)
    right = jnp.concatenate(
        [
            jnp.concatenate([tall_h, tall_l], axis=1),
            jnp.concatenate([tall_h, jnp.zeros_like(tall_l)], axis=1),
        ],
        axis=0,
    )
    lane = lax.broadcasted_iota(jnp.int32, (cin, maps.shape[1]), 1)
    seen = (lane < maps.shape[1] - 1, lane >= 0, lane > 0)
    parts = []
    for a in range(3):
        place = slice(a * cin, (a + 1) * cin)
        for c in range(3):
            pair = [acc[place, (k + c) * cout : (k + c + 1) * cout] for k in (0, 3)]
            left = jnp.concatenate(split(jnp.concatenate(pair, axis=1)), axis=1)
            result = dot(left, right)
            total = jnp.sum(jnp.where(seen[c], maps[place], 0.0), axis=1, keepdims=True)
            result = (result[:, :cout] + result[:, cout:]) * scaling + total * constant
            parts += [result[: cin // 2], result[cin // 2 :]]
    upper = is_upper(stage)
    for index in range(9):
        place = slice(index * cin // 2, (index + 1) * cin // 2)
        keep[place] = jnp.where(upper, parts[9 + index], parts[index])
        send[place] = jnp.where(upper, parts[index], parts[9 + index])


def centred_halves(image, pre, low, high, average):
    rows, width, cout = pre.shape[1:]
    full = jnp.concatenate([low[image], pre[image, 1 : rows - 1], high[image]], axis=0)
    return split(full.reshape(rows * width, cout) - average)


def pixel_kernel(
    pre, low, high, ups, mats, paint, paint_rows, colored, pre_grad, edge_ahead, edge_across
):
    image = pl.program_id(0)
    rows, width, cout = pre.shape[1:]
    big, small = centred_halves(image, pre, low, high, paint_rows[0:1])
    up = ups[image].reshape(rows * width, cout)
    result = dot(jnp.concatenate([big, up, small], axis=1), mats[...])
    grad = (result[:, :cout] + result[:, cout:] + paint_rows[2:3]).astype(BF16)
    shaped = grad.reshape(rows, width, cout)
    pre_grad[image] = shaped
    edge_across[image], edge_ahead[image] = sides(shaped[rows - 1 :], shaped[:1])
    result = dot(jnp.concatenate([big, small], axis=1), paint[...])
    result = result[:, :cout] + result[:, cout:] + paint_rows[1:2]
    colored[0] = result.astype(BF16).reshape(rows, width, cout)


def turn_kernel(kern, out):
    cout = kern.shape[3]
    for a in range(3):
        for c in range(3):
            tap = (a * 3 + c) * cout
            out[tap : tap + cout] = kern[a, c].T


def image_kernel(first, pre_grad, ahead, across, wts, *rest):
    out = rest[-1]
    image = pl.program_id(0) + first
    top, bot = sides(ahead[image], across[image])
    rows, width, cout = pre_grad.shape[1:]
    cin = wts.shape[1]
    exact = jnp.concatenate([top, pre_grad[image], bot], axis=0).astype(F32)
    after, before = shifted(exact)
    taps = [value.astype(BF16) for value in (after, exact, before)]
    wide = jnp.concatenate(
        [taps[c][2 - a : 2 - a + rows] for a in range(3) for c in range(3)], axis=2
    )
    result = dot(wide.reshape(rows * width, 9 * cout), wts[...])
    out[0] = result.astype(BF16).reshape(rows, width, cin)


def fold_kernel(stage, value, received, keep, send):
    upper = is_upper(stage)
    part = keep.shape[0]
    low = value[:part] + received[:part]
    high = value[part:] + received[part:]
    keep[...] = jnp.where(upper, high, low)
    send[...] = jnp.where(upper, low, high)


def join_kernel(stage, value, received, out):
    upper = is_upper(stage)
    part = value.shape[0]
    out[:part] = jnp.where(upper, received[...], value[...])
    out[part:] = jnp.where(upper, value[...], received[...])


def finish_kernel(stage, own, value, *rest):
    out, held, sems = rest[-3:]
    count, size = held.shape[:2]
    upper = is_upper(stage) if own else jnp.logical_not(is_upper(stage))
    start = jnp.where(upper, count * size, 0)
    copies = []
    for index in range(count):
        held[index] = value[index * size : (index + 1) * size].astype(F32)
        place = pl.ds(pl.multiple_of(start + index * size, size), size)
        copies.append(pltpu.make_async_copy(held.at[index], out.at[place], sems.at[index]))
        copies[-1].start()
    for copy in copies:
        copy.wait()


def image_spec(shape, place=lambda b: b):
    return pl.BlockSpec((1, *shape[1:]), lambda b: (place(b),) + (0,) * (len(shape) - 1))


def whole_spec(shape):
    return pl.BlockSpec(shape, lambda b: (0,) * len(shape))


def in_hbm(value):
    return pltpu.with_memory_space_constraint(value, pltpu.HBM)


def resident():
    return pl.BlockSpec(memory_space=pltpu.VMEM)


def forward(images, kernel, upstream):
    count, rows, width, cin = images.shape
    cout = kernel.shape[3]
    pre_shape = (count, rows, width, cout)
    return pl.pallas_call(
        forward_kernel,
        grid=(count,),
        in_specs=[
            image_spec(images.shape),
            whole_spec(kernel.shape),
            image_spec(upstream.shape),
        ],
        out_specs=[
            resident(),
            whole_spec((2 * cout, 2 * cout)),
            whole_spec((8, cout)),
        ],
        out_shape=[
            jax.ShapeDtypeStruct(pre_shape, F32),
            jax.ShapeDtypeStruct((2 * cout, 2 * cout), F32),
            jax.ShapeDtypeStruct((8, cout), F32),
        ],
        scratch_shapes=[
            pltpu.VMEM((10 * cin, 2 * cout), BF16),
            pltpu.VMEM(((rows - 2) * width, 3 * cout), BF16),
        ],
        compiler_params=pltpu.CompilerParams(vmem_limit_bytes=20 * MIB),
        cost_estimate=pl.CostEstimate(
            flops=2 * count * rows * width * 9 * cin * cout,
            bytes_accessed=2 * images.size + 2 * upstream.size + 4 * upstream.size,
            transcendentals=0,
        ),
        name="forward_inner",
    )(
        in_hbm(images), in_hbm(kernel), in_hbm(upstream)
    )


def edges(stage, top, bot, pre, upstream, kernel, acc, sums):
    count, rows, width, cout = pre.shape
    part = (cout + 16) // 2
    edge = (count, 1, width, cout)
    shapes = [edge, edge, (part, cout), (part, cout)]
    return pl.pallas_call(
        functools.partial(edge_kernel, count * rows * width, stage),
        in_specs=[resident()] * 7,
        out_specs=[resident()] * 4,
        out_shape=[jax.ShapeDtypeStruct(shape, F32) for shape in shapes],
        scratch_shapes=[pltpu.VMEM((2 * part, cout), F32)],
        compiler_params=pltpu.CompilerParams(vmem_limit_bytes=12 * MIB),
        cost_estimate=pl.CostEstimate(
            flops=2 * 2 * count * width * 3 * top.shape[3] * cout,
            bytes_accessed=4 * top.size + 24 * count * width * cout,
            transcendentals=0,
        ),
        name="forward_edges",
    )(top, bot, pre, upstream, kernel, acc, sums)


def moments(image, pre, low, high, upstream, images, top, bot, sums, *sofar):
    width, cin = images.shape[2:]
    cout = upstream.shape[3]
    rows = images.shape[1]
    operands = (pre, low, high, upstream, images, top, bot, sums, *sofar)
    return pl.pallas_call(
        functools.partial(moment_kernel, image),
        in_specs=[resident()] * len(operands),
        out_specs=[resident()] * 2,
        out_shape=[
            jax.ShapeDtypeStruct((3 * cin, 6 * cout), F32),
            jax.ShapeDtypeStruct((3 * cin, width), F32),
        ],
        input_output_aliases={8: 0, 9: 1} if sofar else {},
        compiler_params=pltpu.CompilerParams(vmem_limit_bytes=20 * MIB),
        cost_estimate=pl.CostEstimate(
            flops=2 * rows * width * 18 * cin * cout, bytes_accessed=8 * MIB, transcendentals=0
        ),
        name="moments",
    )(*operands)


def whitened(total_pix, stage, own, other, colors, offset, sums, acc, maps):
    half = colors.shape[1]
    cout = 2 * half
    cin = acc.shape[0] // 3
    shapes = [
        ((9 * cin // 2, cout), F32),
        ((9 * cin // 2, cout), F32),
        ((2, half, half), F32),
        ((3 * cout, 2 * cout), BF16),
        ((2 * cout, 2 * cout), BF16),
        ((8, cout), F32),
    ]
    return pl.pallas_call(
        functools.partial(whitening_kernel, total_pix, stage),
        in_specs=[resident()] * 7,
        out_specs=[resident()] * len(shapes),
        out_shape=[jax.ShapeDtypeStruct(shape, dtype) for shape, dtype in shapes],
        scratch_shapes=[pltpu.VMEM((cout + 16, cout), F32)],
        compiler_params=pltpu.CompilerParams(vmem_limit_bytes=20 * MIB),
        cost_estimate=pl.CostEstimate(
            flops=2 * 9 * cin * 8 * cout * cout, bytes_accessed=8 * MIB, transcendentals=0
        ),
        name="whitening",
    )(own, other, colors, offset, sums, acc, maps)


def pixels(pre, low, high, upstream, mats, paint, paint_rows):
    count, rows, width, cout = pre.shape
    shapes = [pre.shape, pre.shape, (count, 1, width, cout), (count, 1, width, cout)]
    return pl.pallas_call(
        pixel_kernel,
        grid=(count,),
        in_specs=[resident()] * 7,
        out_specs=[image_spec(pre.shape)] + [resident()] * 3,
        out_shape=[jax.ShapeDtypeStruct(shape, BF16) for shape in shapes],
        compiler_params=pltpu.CompilerParams(vmem_limit_bytes=16 * MIB),
        cost_estimate=pl.CostEstimate(
            flops=2 * count * rows * width * 12 * cout * cout,
            bytes_accessed=10 * pre.size,
            transcendentals=0,
        ),
        name="pixels",
    )(pre, low, high, upstream, mats, paint, paint_rows)


def turned_weights(kernel):
    cin, cout = kernel.shape[2:]
    return pl.pallas_call(
        turn_kernel,
        out_shape=jax.ShapeDtypeStruct((9 * cout, cin), BF16),
        compiler_params=pltpu.CompilerParams(vmem_limit_bytes=4 * MIB),
        name="turned_weights",
    )(kernel)


def image_gradient(first, count, pre_grad, top, bot, turned, out=None):
    images, rows, width, cout = pre_grad.shape
    cin = turned.shape[1]
    shape = (images, rows, width, cin)

    def place(b):
        return b + first

    operands = [pre_grad, top, bot, turned]
    in_specs = [resident()] * 4
    aliases = {}
    if out is not None:
        operands.append(out)
        in_specs.append(pl.BlockSpec(memory_space=pl.ANY))
        aliases = {4: 0}
    return pl.pallas_call(
        functools.partial(image_kernel, first),
        grid=(count,),
        in_specs=in_specs,
        out_specs=image_spec(shape, place),
        out_shape=jax.ShapeDtypeStruct(shape, BF16),
        input_output_aliases=aliases,
        compiler_params=pltpu.CompilerParams(vmem_limit_bytes=12 * MIB),
        cost_estimate=pl.CostEstimate(
            flops=2 * count * rows * width * 9 * cin * cout,
            bytes_accessed=2 * count * rows * width * (cin + cout),
            transcendentals=0,
        ),
        name="image_gradient",
    )(*operands)


def sliced(images):
    count, rows, width, cin = images.shape
    return pl.pallas_call(
        slice_kernel,
        in_specs=[pl.BlockSpec(memory_space=pltpu.HBM)],
        out_specs=[resident(), resident()],
        out_shape=[jax.ShapeDtypeStruct((count, 1, width, cin), BF16)] * 2,
        scratch_shapes=[pltpu.SemaphoreType.DMA((2,))],
        compiler_params=pltpu.CompilerParams(vmem_limit_bytes=4 * MIB),
        name="edge_rows",
    )(in_hbm(images))


def small_call(kernel, name, *operands, out):
    return pl.pallas_call(
        kernel,
        in_specs=[resident()] * len(operands),
        out_specs=[resident()] * len(out),
        out_shape=out,
        compiler_params=pltpu.CompilerParams(vmem_limit_bytes=4 * MIB),
        name=name,
    )(*operands)


def fold(value, received, stage):
    half = jax.ShapeDtypeStruct((value.shape[0] // 2, value.shape[1]), value.dtype)
    return small_call(
        functools.partial(fold_kernel, stage), "fold", value, received, out=[half, half]
    )


def join(value, received, stage):
    whole = jax.ShapeDtypeStruct((value.shape[0] * 2, value.shape[1]), value.dtype)
    return small_call(
        functools.partial(join_kernel, stage), "join", value, received, out=[whole]
    )[0]


def finish(stage, value, out=None):
    part, lanes = value.shape
    operands, aliases = (value,), {}
    if out is not None:
        operands, aliases = (value, out), {1: 0}
    space = pl.BlockSpec(memory_space=pltpu.HBM)
    return pl.pallas_call(
        functools.partial(finish_kernel, stage, out is None),
        in_specs=[resident(), space][: len(operands)],
        out_specs=space,
        out_shape=jax.ShapeDtypeStruct((2 * part, lanes), F32),
        scratch_shapes=[
            pltpu.VMEM((2, part // 2, lanes), F32),
            pltpu.SemaphoreType.DMA((2,)),
        ],
        input_output_aliases=aliases,
        compiler_params=pltpu.CompilerParams(vmem_limit_bytes=4 * MIB),
        name="finish",
    )(*operands)


def halos(ahead, across):
    count = lax.axis_size("rows")
    pairs = []
    for first in (0, 1):
        found = [(i, i + 1) for i in range(first, count - 1, 2)]
        pairs.append(found + [(i, j) for j, i in found])
    return lax.ppermute(ahead, "rows", pairs[0]), lax.ppermute(across, "rows", pairs[1])


def exchange(value, devices, stage):
    pairs = [(i, i ^ (stage[1] if i & 1 else stage[0])) for i in range(devices)]
    return lax.ppermute(value, AXES, pairs)


def beside(send, devices, stage, task, operands):
    send, operands = lax.optimization_barrier((send, operands))
    received = exchange(send, devices, stage)
    result = task(*operands)
    return lax.optimization_barrier((received, result))


def body(images, kernel, colors, offset, upstream):
    count, rows, width, cin = images.shape
    cout = kernel.shape[3]
    devices = lax.axis_size("dp") * lax.axis_size("rows")
    total_pix = count * rows * width * devices
    plan = stages(devices)
    top, bot = halos(*sliced(images))
    pre, acc, sums = forward(images, kernel, upstream)
    low, high, value, send = edges(plan[0], top, bot, pre, upstream, kernel, acc, sums)
    state = {"next": 0, "moments": (), "grad": None}

    def summed(send, stage):
        image = state["next"]
        if image >= count:
            return exchange(send, devices, stage)
        state["next"] = image + 1
        operands = (pre, low, high, upstream, images, top, bot, sums, *state["moments"])
        received, state["moments"] = beside(
            send, devices, stage, functools.partial(moments, image), operands
        )
        return received

    value = value + summed(send, plan[0])
    for stage in plan[1:]:
        value = value + summed(value, stage)
    received = summed(value, plan[0])
    for image in range(state["next"], count):
        state["moments"] = moments(
            image, pre, low, high, upstream, images, top, bot, sums, *state["moments"]
        )
    value, send, grad_colors, mats, paint, paint_rows = whitened(
        total_pix,
        plan[0],
        value,
        received,
        colors,
        offset.reshape(1, cout),
        sums,
        *state["moments"],
    )
    received, turned = beside(send, devices, plan[0], turned_weights, (kernel,))
    state["next"] = 0
    shares = [1, 2, 1, 1, 1]

    def transfer(send, stage):
        first = state["next"]
        if first >= count:
            return exchange(send, devices, stage)
        many = min(shares.pop(0), count - first) if shares else count - first
        state["next"] = first + many
        operands = (pre_grad, grad_top, grad_bot, turned)
        if state["grad"] is not None:
            operands = (*operands, state["grad"])
        received, state["grad"] = beside(
            send, devices, stage, functools.partial(image_gradient, first, many), operands
        )
        return received

    cuts = []
    for stage in plan[1:]:
        if value.shape[0] % 32 == 0 and value.shape[0] > 144:
            value, send = fold(value, received, stage)
            cuts.append(stage)
        else:
            value = send = value + received
        if stage == plan[1]:
            received, (colored, pre_grad, edge_ahead, edge_across) = beside(
                send, devices, stage, pixels, (pre, low, high, upstream, mats, paint, paint_rows)
            )
        elif stage == plan[2]:
            received, (grad_top, grad_bot) = beside(
                send, devices, stage, halos, (edge_ahead, edge_across)
            )
        else:
            received = transfer(send, stage)
    value = (value + received).astype(BF16)
    for stage in reversed(cuts):
        value = join(value, transfer(value, stage), stage)
    received, result = beside(
        value, devices, plan[0], functools.partial(finish, plan[0]), (value,)
    )
    first = state["next"]
    if first < count:
        operands = (pre_grad, grad_top, grad_bot, turned, state["grad"])
        state["grad"] = image_gradient(first, count - first, *operands)
    grad_kernel = finish(plan[0], received, result).reshape(3, 3, cin, cout)
    return colored, state["grad"], grad_kernel, grad_colors


def solution(mesh):
    placed = (P("dp", "rows", None, None), P(), P(), P(), P("dp", "rows", None, None))
    return jax.shard_map(
        body,
        mesh=mesh,
        in_specs=placed,
        out_specs=(P("dp", "rows", None, None), P("dp", "rows", None, None), P(), P()),
        check_vma=False,
    )
```

```python
import functools
import math

import jax
import jax.numpy as jnp
from jax import lax
from jax.experimental import pallas as pl
from jax.experimental.pallas import tpu as pltpu
from jax.sharding import PartitionSpec as P

NS_ITERS = 5
EPSILON = 1e-05
F32 = jnp.float32
BF16 = jnp.bfloat16
MIB = 1024 * 1024
AXES = ("dp", "rows")


def device_index():
    return lax.axis_index("dp") * lax.axis_size("rows") + lax.axis_index("rows")


def is_even():
    return lax.axis_index("rows") % 2 == 0


def is_upper(stage):
    index = device_index()
    return index & jnp.where(index & 1 != 0, stage[1], stage[0]) != 0


def stages(devices):
    bits = [1 << i for i in range(devices.bit_length() - 1)]
    plan = [(bit, bit) for bit in bits]
    if len(bits) > 2:
        plan[1:3] = [(2, 4), (4, 2)]
    return plan


def split(value):
    high = value.astype(BF16)
    return high, (value - high.astype(F32)).astype(BF16)


def dot(left, right, dims=((1,), (0,))):
    return lax.dot_general(left, right, (dims, ((), ())), preferred_element_type=F32)


def dot3(left, right):
    lh, ll = split(left)
    rh, rl = split(right)
    return dot(
        jnp.concatenate([lh, lh, ll], axis=1), jnp.concatenate([rh, rl, rh], axis=0)
    )


def shifted(value):
    width = value.shape[1]
    col = lax.broadcasted_iota(jnp.int32, (1, *value.shape[1:]), 1)
    after = jnp.where(col == width - 1, 0.0, pltpu.roll(value, width - 1, 1))
    before = jnp.where(col == 0, 0.0, pltpu.roll(value, 1, 1))
    return after, before


def merged(prod, shape):
    cout = shape[2]
    _, left = shifted(prod[:, :cout].reshape(shape))
    right, _ = shifted(prod[:, 2 * cout :].reshape(shape))
    return prod[:, cout : 2 * cout].reshape(shape) + left + right


def paired_rows(padded, wts, cout):
    rows, width, cin = padded.shape[0] - 2, *padded.shape[1:]
    pairs = rows // 2
    parts = [
        jnp.concatenate([padded[2 * k + a : 2 * k + a + 1] for k in range(pairs)], axis=0)
        for a in range(4)
    ]
    wide = jnp.concatenate(parts, axis=2).reshape(pairs * width, 4 * cin)
    outer = dot(wide[:, : 3 * cin], wts[: 3 * cin])
    shared = dot(wide, wts[3 * cin : 7 * cin])
    inner = dot(wide[:, cin:], wts[7 * cin :])
    shape = (pairs, width, cout)

    def added_up(left, middle, right):
        _, before = shifted(left.reshape(shape))
        after, _ = shifted(right.reshape(shape))
        return middle.reshape(shape) + before + after

    first = added_up(outer[:, :cout], outer[:, cout:], shared[:, :cout])
    second = added_up(shared[:, cout:], inner[:, :cout], inner[:, cout:])
    ordered = [part[k : k + 1] for k in range(pairs) for part in (first, second)]
    return jnp.concatenate(ordered, axis=0)


def column(row):
    size = row.shape[1]
    return jnp.broadcast_to(row, (size, size)).T


def pack(full):
    half = full.shape[0] // 2
    lane = lax.broadcasted_iota(jnp.int32, (half, full.shape[1]), 1)
    return jnp.where(lane < half, full[:half], full[half:])


def unpack(packed):
    half = packed.shape[0]
    lane = lax.broadcasted_iota(jnp.int32, packed.shape, 1)
    return jnp.concatenate(
        [jnp.where(lane < half, packed, 0.0), jnp.where(lane < half, 0.0, packed)], axis=0
    )


def statistics(held):
    third = held.shape[1] // 3
    return dot(held[:, third:], held[:, : 2 * third], ((0,), (0,)))


def forward_kernel(
    first, img, kern, upstream, pre_out, acc, sums, maps, ups, wts, held, map_sems, up_sems
):
    step = pl.program_id(0)
    last = pl.num_programs(0) - 1
    count, rows, width, cin = img.shape
    cout = kern.shape[3]
    inner = (rows - 2) * width

    def map_copy(image):
        return pltpu.make_async_copy(img.at[image], maps.at[image], map_sems.at[image])

    def up_copy(image):
        return pltpu.make_async_copy(upstream.at[image], ups.at[image], up_sems.at[image])

    @pl.when(step == 0)
    def _():
        up_copy(0).start()
        for image in range(1, count):
            map_copy(image).start()
            up_copy(image).start()
        blank = jnp.zeros((cin, cout), BF16)
        blocks = [(kern[a, 0], kern[a, 1]) for a in range(3)]
        blocks += [
            (kern[a, 2] if a < 3 else blank, kern[a - 1, 0] if a > 0 else blank) for a in range(4)
        ]
        blocks += [(kern[a, 1], kern[a, 2]) for a in range(3)]
        for index, (one, two) in enumerate(blocks):
            wts[index * cin : (index + 1) * cin, :cout] = one
            wts[index * cin : (index + 1) * cin, cout:] = two
        acc[...] = jnp.zeros_like(acc)
        sums[...] = jnp.zeros_like(sums)
        held[...] = jnp.zeros_like(held)

    @pl.when(step > 0)
    def _():
        map_copy(step).wait()

    acc[...] += statistics(held[...])
    blank = jnp.zeros((1, width, cin), BF16)
    padded = jnp.concatenate([blank, maps[step], blank], axis=0)
    pre = paired_rows(padded, wts, cout)
    pre_out[step] = pre
    mid = pre[1 : rows - 1].reshape(inner, cout)
    mean = jnp.sum(mid, axis=0, keepdims=True) / inner
    shift = jnp.where(step == 0, mean, sums[2:3])
    sums[2:3] = shift
    delta = mid - shift
    up_copy(step).wait()
    up = ups[step, 1 : rows - 1].reshape(inner, cout)
    high, low = split(delta)
    held[:, :cout] = low
    held[:, cout : 2 * cout] = high
    held[:, 2 * cout :] = up
    sums[0:1] += jnp.sum(delta, axis=0, keepdims=True)
    sums[1:2] += jnp.sum(up.astype(F32), axis=0, keepdims=True)

    @pl.when(step == last)
    def _():
        acc[...] += statistics(held[...])


def sides(ahead, across):
    even = is_even()
    return jnp.where(even, across, ahead), jnp.where(even, ahead, across)


def fetch_kernel(images, kern, ahead, across, taps, maps, sems):
    last = images.shape[1] - 1
    even = is_even()
    pairs = (
        (images.at[:, pl.ds(jnp.where(even, last, 0), 1)], ahead),
        (images.at[:, pl.ds(jnp.where(even, 0, last), 1)], across),
        (kern, taps),
        (images.at[0], maps.at[0]),
    )
    copies = [
        pltpu.make_async_copy(source, target, sems.at[index])
        for index, (source, target) in enumerate(pairs)
    ]
    for copy in copies:
        copy.start()
    for copy in copies:
        copy.wait()


def edge_kernel(total, stage, ahead, across, pre, ups, kern, acc, sums, low, high, keep, send, stats):
    count, _, width, cin = ahead.shape
    cout = kern.shape[3]
    last = pre.shape[1] - 1
    top, bot = sides(ahead[...], across[...])
    pixels = count * width
    shape = (count, width, cout)
    edges = []
    for a, source, row, out in ((0, top, 0, low), (2, bot, last, high)):
        taps = jnp.concatenate([kern[a, c] for c in range(3)], axis=1)
        value = merged(dot(source.reshape(pixels, cin), taps), shape) + pre[:, row]
        out[:, 0] = value
        edges.append(value.reshape(pixels, cout))
    shift = sums[2:3]
    delta = jnp.concatenate(edges, axis=0) - shift
    up = jnp.concatenate(
        [ups[:, 0].reshape(pixels, cout), ups[:, last].reshape(pixels, cout)], axis=0
    )
    big, small = split(delta)
    gram = acc[...] + statistics(jnp.concatenate([small, big, up], axis=1))
    moved = sums[0:1] + jnp.sum(delta, axis=0, keepdims=True)
    up_sum = sums[1:2] + jnp.sum(up.astype(F32), axis=0, keepdims=True)
    mixed = gram[:cout, :cout]
    square = gram[:cout, cout:] + mixed + mixed.T
    cross = gram[cout:, :cout] + gram[cout:, cout:]
    raw = moved + total * shift
    square = square + column(moved) * shift + column(shift) * raw
    cross = cross + column(up_sum) * shift
    half = cout // 2
    stats[0:half] = pack(square)
    stats[half : 2 * half] = pack(cross)
    stats[2 * half :] = jnp.zeros_like(stats[2 * half :])
    stats[2 * half : 2 * half + 1] = raw
    stats[2 * half + 1 : 2 * half + 2] = up_sum
    part = keep.shape[0]
    upper = is_upper(stage)
    keep[...] = jnp.where(upper, stats[part:], stats[:part])
    send[...] = jnp.where(upper, stats[:part], stats[part:])


def spread(blocks):
    zero = jnp.zeros(blocks.shape[1:], F32)
    return jnp.concatenate(
        [
            jnp.concatenate([blocks[0], zero], axis=1),
            jnp.concatenate([zero, blocks[1]], axis=1),
        ],
        axis=0,
    )


def group_sum(value, half):
    cols = jnp.sum(value, axis=0, keepdims=True)
    lane = lax.broadcasted_iota(jnp.int32, cols.shape, 1)
    low = jnp.sum(jnp.where(lane < half, cols, 0.0), axis=1, keepdims=True)
    high = jnp.sum(jnp.where(lane < half, 0.0, cols), axis=1, keepdims=True)
    return jnp.where(lane < half, low, high)


def whitening(stats, colors, offset, total_pix, half):
    cout = 2 * half
    row_i = lax.broadcasted_iota(jnp.int32, (cout, cout), 0)
    col_i = lax.broadcasted_iota(jnp.int32, (cout, cout), 1)
    eye = jnp.where(row_i == col_i, 1.0, 0.0)
    block = jnp.where((row_i < half) == (col_i < half), 1.0, 0.0)
    square = unpack(stats[0:half])
    cross = unpack(stats[half : 2 * half])
    average = stats[2 * half : 2 * half + 1] / total_pix
    up_total = stats[2 * half + 1 : 2 * half + 2]
    sigma = square / total_pix - block * (column(average) * average) + EPSILON * eye
    cross = cross - block * (column(up_total) * average)
    grad = dot3(colors.T, cross)
    direction = grad + grad.T
    traces = group_sum(sigma * eye, half)
    normed = sigma / traces
    zero = jnp.zeros_like(normed)

    def stacked(value, tangent):
        return jnp.concatenate(
            [
                jnp.concatenate([value, tangent], axis=1),
                jnp.concatenate([zero, value], axis=1),
            ],
            axis=0,
        )

    source = stacked(normed, direction)
    value = 1.5 * eye - 0.5 * normed
    tangent = -0.5 * direction
    for _ in range(NS_ITERS - 1):
        first = jnp.concatenate([value, tangent], axis=1)
        both = dot3(first, jnp.concatenate([stacked(value, tangent), source], axis=1))
        squared = both[:, : 2 * cout]
        scaled = stacked(both[:, 2 * cout : 3 * cout], both[:, 3 * cout :])
        cubed = dot3(squared, scaled)
        value = 1.5 * value - 0.5 * cubed[:, :cout]
        tangent = 1.5 * tangent - 0.5 * cubed[:, cout:]
    inverse = 1.0 / jnp.sqrt(traces)
    whitener = value * inverse
    shared = group_sum(tangent * normed, half) + 0.5 * group_sum(direction * value, half)
    symmetric = (tangent - eye * shared) * (inverse / traces)
    mixed = dot3(colors, whitener)
    color_sum = dot3(cross, whitener.T)
    up_mean = jnp.broadcast_to(up_total / total_pix, (8, cout))
    bias = -dot3(up_mean, mixed)[0:1]
    return average, mixed, symmetric / total_pix, bias, offset, color_sum


def image_moments(image, pre, low, high, ups, img, ahead, across, sums):
    rows, width, cin = img.shape[1:]
    cout = pre.shape[3]
    pixels = rows * width
    top, bot = sides(ahead[image], across[image])
    padded = jnp.concatenate([top, img[image], bot], axis=0)
    turned = padded.reshape((rows + 2) * width, cin).T
    full = jnp.concatenate([low[image], pre[image, 1 : rows - 1], high[image]], axis=0)
    columns = []
    for value in (ups[image], (full - sums[2:3]).astype(BF16)):
        after, before = shifted(value.astype(F32))
        columns += [after.astype(BF16), value, before.astype(BF16)]
    right = jnp.concatenate(columns, axis=2).reshape(pixels, 6 * cout)
    left = jnp.concatenate([turned[:, a * width : a * width + pixels] for a in range(3)], axis=0)
    tiles = [turned[:, row * width : (row + 1) * width].astype(F32) for row in range(rows + 2)]
    middle = functools.reduce(jnp.add, tiles[2:rows])
    outer = ((0, 1), (1, rows), (rows, rows + 1))
    totals = jnp.concatenate([middle + tiles[one] + tiles[two] for one, two in outer], axis=0)
    return dot(left, right), totals


def moment_kernel(first, count, *refs):
    acc, maps = refs[-2:]
    found = [image_moments(first + index, *refs[:8]) for index in range(count)]
    if len(refs) == 12:
        found.append((refs[8][...], refs[9][...]))
    acc[...] = functools.reduce(jnp.add, [product for product, _ in found])
    maps[...] = functools.reduce(jnp.add, [totals for _, totals in found])


def whitening_kernel(
    total_pix,
    stage,
    own,
    other,
    colors,
    offset,
    sums,
    acc,
    maps,
    keep,
    send,
    grad_colors,
    mats,
    paint,
    paint_rows,
    stats,
):
    cout = 2 * colors.shape[1]
    half = cout // 2
    cin = acc.shape[0] // 3
    scaling = 1.0 / math.sqrt(total_pix)
    join_kernel(stage, own, other, stats)
    average, mixed, symmetric, bias, offs, color_sum = whitening(
        stats[...], spread(colors[...]), offset[...], total_pix, half
    )
    blank = jnp.zeros((cout, cout), BF16)
    mixed_h, mixed_l = split(mixed)
    color_h, color_l = split(mixed.T)
    sym_h, sym_l = split(symmetric)
    for target, blocks in (
        (mats, ((sym_h, sym_l), (mixed_h, mixed_l), (sym_h, blank))),
        (paint, ((color_h, color_l), (color_h, blank))),
    ):
        for index, (one, two) in enumerate(blocks):
            target[index * cout : (index + 1) * cout, :cout] = one
            target[index * cout : (index + 1) * cout, cout:] = two
    paint_rows[...] = jnp.zeros_like(paint_rows)
    paint_rows[0:1] = average
    paint_rows[1:2] = offs
    paint_rows[2:3] = bias
    scaled = color_sum * scaling
    grad_colors[0] = scaled[:half, :half]
    grad_colors[1] = pltpu.roll(scaled[half:], half, 1)[:, :half]

    moved = jnp.broadcast_to(sums[2:3] - average, (8, cout))
    constant = (bias + dot3(moved, symmetric)[0:1]) * scaling
    tall_h = jnp.concatenate([mixed_h, sym_h], axis=0)
    tall_l = jnp.concatenate([mixed_l, sym_l], axis=0)
    right = jnp.concatenate(
        [
            jnp.concatenate([tall_h, tall_l], axis=1),
            jnp.concatenate([tall_h, jnp.zeros_like(tall_l)], axis=1),
        ],
        axis=0,
    )
    lane = lax.broadcasted_iota(jnp.int32, (cin, maps.shape[1]), 1)
    seen = (lane < maps.shape[1] - 1, lane >= 0, lane > 0)
    parts = []
    for a in range(3):
        place = slice(a * cin, (a + 1) * cin)
        for c in range(3):
            pair = [acc[place, (k + c) * cout : (k + c + 1) * cout] for k in (0, 3)]
            left = jnp.concatenate(split(jnp.concatenate(pair, axis=1)), axis=1)
            result = dot(left, right)
            total = jnp.sum(jnp.where(seen[c], maps[place], 0.0), axis=1, keepdims=True)
            result = (result[:, :cout] + result[:, cout:]) * scaling + total * constant
            parts += [result[: cin // 2], result[cin // 2 :]]
    upper = is_upper(stage)
    for index in range(9):
        place = slice(index * cin // 2, (index + 1) * cin // 2)
        keep[place] = jnp.where(upper, parts[9 + index], parts[index])
        send[place] = jnp.where(upper, parts[index], parts[9 + index])


def centred_halves(image, pre, low, high, average):
    rows, width, cout = pre.shape[1:]
    full = jnp.concatenate([low[image], pre[image, 1 : rows - 1], high[image]], axis=0)
    return split(full.reshape(rows * width, cout) - average)


def edge_gradient_kernel(low, high, ups, mats, paint_rows, edge_ahead, edge_across):
    count, _, width, cout = low.shape
    last = ups.shape[1] - 1
    pre = jnp.concatenate([low[:, 0], high[:, 0]], axis=0).reshape(2 * count * width, cout)
    up = jnp.concatenate([ups[:, 0], ups[:, last]], axis=0).reshape(2 * count * width, cout)
    grad = pre_gradient(*split(pre - paint_rows[0:1]), up, mats, paint_rows)
    shaped = grad.reshape(2 * count, width, cout)
    edge_across[:, 0], edge_ahead[:, 0] = sides(shaped[count:], shaped[:count])


def pre_gradient(big, small, up, mats, paint_rows):
    cout = up.shape[1]
    result = dot(jnp.concatenate([big, up, small], axis=1), mats[...])
    return (result[:, :cout] + result[:, cout:] + paint_rows[2:3]).astype(BF16)


def gradient_kernel(pre, low, high, ups, mats, paint_rows, pre_grad):
    image = pl.program_id(0)
    rows, width, cout = pre.shape[1:]
    big, small = centred_halves(image, pre, low, high, paint_rows[0:1])
    up = ups[image].reshape(rows * width, cout)
    grad = pre_gradient(big, small, up, mats, paint_rows)
    pre_grad[image] = grad.reshape(rows, width, cout)


def paint_kernel(pre, low, high, paint, paint_rows, colored):
    rows, width, cout = pre.shape[1:]
    halves = centred_halves(pl.program_id(0), pre, low, high, paint_rows[0:1])
    result = dot(jnp.concatenate(halves, axis=1), paint[...])
    result = result[:, :cout] + result[:, cout:] + paint_rows[1:2]
    colored[0] = result.astype(BF16).reshape(rows, width, cout)


def turn_kernel(kern, out):
    cout = kern.shape[3]
    for a in range(3):
        for c in range(3):
            tap = (a * 3 + c) * cout
            out[tap : tap + cout] = kern[a, c].T


def image_kernel(first, pre_grad, ahead, across, wts, *rest):
    out = rest[-1]
    image = pl.program_id(0) + first
    top, bot = sides(ahead[image], across[image])
    rows, width, cout = pre_grad.shape[1:]
    cin = wts.shape[1]
    exact = jnp.concatenate([top, pre_grad[image], bot], axis=0).astype(F32)
    after, before = shifted(exact)
    taps = [value.astype(BF16) for value in (after, exact, before)]
    wide = jnp.concatenate(
        [taps[c][2 - a : 2 - a + rows] for a in range(3) for c in range(3)], axis=2
    )
    result = dot(wide.reshape(rows * width, 9 * cout), wts[...])
    out[0] = result.astype(BF16).reshape(rows, width, cin)


def fold_kernel(stage, value, received, keep, send):
    upper = is_upper(stage)
    part = keep.shape[0]
    low = value[:part] + received[:part]
    high = value[part:] + received[part:]
    keep[...] = jnp.where(upper, high, low)
    send[...] = jnp.where(upper, low, high)


def join_kernel(stage, value, received, out):
    upper = is_upper(stage)
    part = value.shape[0]
    out[:part] = jnp.where(upper, received[...], value[...])
    out[part:] = jnp.where(upper, value[...], received[...])


def finish_kernel(stage, own, value, *rest):
    out, held, sems = rest[-3:]
    count, size = held.shape[:2]
    upper = is_upper(stage) if own else jnp.logical_not(is_upper(stage))
    start = jnp.where(upper, count * size, 0)
    copies = []
    for index in range(count):
        held[index] = value[index * size : (index + 1) * size].astype(F32)
        place = pl.ds(pl.multiple_of(start + index * size, size), size)
        copies.append(pltpu.make_async_copy(held.at[index], out.at[place], sems.at[index]))
        copies[-1].start()
    for copy in copies:
        copy.wait()


def image_spec(shape, place=lambda b: b):
    return pl.BlockSpec((1, *shape[1:]), lambda b: (place(b),) + (0,) * (len(shape) - 1))


def whole_spec(shape):
    return pl.BlockSpec(shape, lambda b: (0,) * len(shape))


def in_hbm(value):
    return pltpu.with_memory_space_constraint(value, pltpu.HBM)


def resident():
    return pl.BlockSpec(memory_space=pltpu.VMEM)


def forward(first, images, taps, upstream):
    count, rows, width, cin = images.shape
    cout = taps.shape[3]
    shapes = [
        ((count, rows, width, cout), F32),
        ((2 * cout, 2 * cout), F32),
        ((8, cout), F32),
        (images.shape, BF16),
        (upstream.shape, BF16),
    ]
    space = pl.BlockSpec(memory_space=pltpu.HBM)
    return pl.pallas_call(
        forward_kernel,
        grid=(count,),
        in_specs=[resident(), space, resident(), space],
        out_specs=[resident()] * len(shapes),
        out_shape=[jax.ShapeDtypeStruct(shape, dtype) for shape, dtype in shapes],
        scratch_shapes=[
            pltpu.VMEM((10 * cin, 2 * cout), BF16),
            pltpu.VMEM(((rows - 2) * width, 3 * cout), BF16),
            pltpu.SemaphoreType.DMA((count,)),
            pltpu.SemaphoreType.DMA((count,)),
        ],
        input_output_aliases={0: 3},
        compiler_params=pltpu.CompilerParams(vmem_limit_bytes=20 * MIB),
        cost_estimate=pl.CostEstimate(
            flops=2 * count * rows * width * 9 * cin * cout,
            bytes_accessed=2 * images.size + 2 * upstream.size + 4 * upstream.size,
            transcendentals=0,
        ),
        name="forward_inner",
    )(first, in_hbm(images), taps, in_hbm(upstream))


def edges(stage, top, bot, pre, upstream, kernel, acc, sums):
    count, rows, width, cout = pre.shape
    part = (cout + 16) // 2
    edge = (count, 1, width, cout)
    shapes = [edge, edge, (part, cout), (part, cout)]
    return pl.pallas_call(
        functools.partial(edge_kernel, count * rows * width, stage),
        in_specs=[resident()] * 7,
        out_specs=[resident()] * 4,
        out_shape=[jax.ShapeDtypeStruct(shape, F32) for shape in shapes],
        scratch_shapes=[pltpu.VMEM((2 * part, cout), F32)],
        compiler_params=pltpu.CompilerParams(vmem_limit_bytes=12 * MIB),
        cost_estimate=pl.CostEstimate(
            flops=2 * 2 * count * width * 3 * top.shape[3] * cout,
            bytes_accessed=4 * top.size + 24 * count * width * cout,
            transcendentals=0,
        ),
        name="forward_edges",
    )(top, bot, pre, upstream, kernel, acc, sums)


def moments(first, count, pre, low, high, upstream, images, top, bot, sums, *sofar):
    width, cin = images.shape[2:]
    cout = upstream.shape[3]
    rows = images.shape[1]
    operands = (pre, low, high, upstream, images, top, bot, sums, *sofar)
    return pl.pallas_call(
        functools.partial(moment_kernel, first, count),
        in_specs=[resident()] * len(operands),
        out_specs=[resident()] * 2,
        out_shape=[
            jax.ShapeDtypeStruct((3 * cin, 6 * cout), F32),
            jax.ShapeDtypeStruct((3 * cin, width), F32),
        ],
        input_output_aliases={8: 0, 9: 1} if sofar else {},
        compiler_params=pltpu.CompilerParams(vmem_limit_bytes=28 * MIB),
        cost_estimate=pl.CostEstimate(
            flops=2 * count * rows * width * 18 * cin * cout, bytes_accessed=8 * MIB, transcendentals=0
        ),
        name="moments",
    )(*operands)


def whitened(total_pix, stage, own, other, colors, offset, sums, acc, maps):
    half = colors.shape[1]
    cout = 2 * half
    cin = acc.shape[0] // 3
    shapes = [
        ((9 * cin // 2, cout), F32),
        ((9 * cin // 2, cout), F32),
        ((2, half, half), F32),
        ((3 * cout, 2 * cout), BF16),
        ((2 * cout, 2 * cout), BF16),
        ((8, cout), F32),
    ]
    return pl.pallas_call(
        functools.partial(whitening_kernel, total_pix, stage),
        in_specs=[resident()] * 7,
        out_specs=[resident()] * len(shapes),
        out_shape=[jax.ShapeDtypeStruct(shape, dtype) for shape, dtype in shapes],
        scratch_shapes=[pltpu.VMEM((cout + 16, cout), F32)],
        compiler_params=pltpu.CompilerParams(vmem_limit_bytes=20 * MIB),
        cost_estimate=pl.CostEstimate(
            flops=2 * 9 * cin * 8 * cout * cout, bytes_accessed=8 * MIB, transcendentals=0
        ),
        name="whitening",
    )(own, other, colors, offset, sums, acc, maps)


def edge_gradients(low, high, upstream, mats, paint_rows):
    return pl.pallas_call(
        edge_gradient_kernel,
        in_specs=[resident()] * 5,
        out_specs=[resident()] * 2,
        out_shape=[jax.ShapeDtypeStruct(low.shape, BF16)] * 2,
        compiler_params=pltpu.CompilerParams(vmem_limit_bytes=16 * MIB),
        name="edge_gradients",
    )(low, high, upstream, mats, paint_rows)


def gradients(pre, low, high, upstream, mats, paint_rows):
    count, rows, width, cout = pre.shape
    return pl.pallas_call(
        gradient_kernel,
        grid=(count,),
        in_specs=[resident()] * 6,
        out_specs=resident(),
        out_shape=jax.ShapeDtypeStruct(pre.shape, BF16),
        compiler_params=pltpu.CompilerParams(vmem_limit_bytes=16 * MIB),
        cost_estimate=pl.CostEstimate(
            flops=2 * count * rows * width * 6 * cout * cout,
            bytes_accessed=8 * pre.size,
            transcendentals=0,
        ),
        name="pre_gradient",
    )(pre, low, high, upstream, mats, paint_rows)


def painted(pre, low, high, paint, paint_rows):
    count, rows, width, cout = pre.shape
    return pl.pallas_call(
        paint_kernel,
        grid=(count,),
        in_specs=[resident()] * 5,
        out_specs=image_spec(pre.shape),
        out_shape=jax.ShapeDtypeStruct(pre.shape, BF16),
        compiler_params=pltpu.CompilerParams(vmem_limit_bytes=16 * MIB),
        cost_estimate=pl.CostEstimate(
            flops=2 * count * rows * width * 4 * cout * cout,
            bytes_accessed=6 * pre.size,
            transcendentals=0,
        ),
        name="colored",
    )(pre, low, high, paint, paint_rows)


def turned_weights(kernel):
    cin, cout = kernel.shape[2:]
    return pl.pallas_call(
        turn_kernel,
        out_shape=jax.ShapeDtypeStruct((9 * cout, cin), BF16),
        compiler_params=pltpu.CompilerParams(vmem_limit_bytes=4 * MIB),
        name="turned_weights",
    )(kernel)


def image_gradient(first, count, pre_grad, top, bot, turned, out=None):
    images, rows, width, cout = pre_grad.shape
    cin = turned.shape[1]
    shape = (images, rows, width, cin)

    def place(b):
        return b + first

    operands = [pre_grad, top, bot, turned]
    in_specs = [resident()] * 4
    aliases = {}
    if out is not None:
        operands.append(out)
        in_specs.append(pl.BlockSpec(memory_space=pl.ANY))
        aliases = {4: 0}
    return pl.pallas_call(
        functools.partial(image_kernel, first),
        grid=(count,),
        in_specs=in_specs,
        out_specs=image_spec(shape, place),
        out_shape=jax.ShapeDtypeStruct(shape, BF16),
        input_output_aliases=aliases,
        compiler_params=pltpu.CompilerParams(vmem_limit_bytes=12 * MIB),
        cost_estimate=pl.CostEstimate(
            flops=2 * count * rows * width * 9 * cin * cout,
            bytes_accessed=2 * count * rows * width * (cin + cout),
            transcendentals=0,
        ),
        name="image_gradient",
    )(*operands)


def fetched(images, kernel):
    count, rows, width, cin = images.shape
    edge = (count, 1, width, cin)
    space = pl.BlockSpec(memory_space=pltpu.HBM)
    return pl.pallas_call(
        fetch_kernel,
        in_specs=[space, space],
        out_specs=[resident()] * 4,
        out_shape=[
            jax.ShapeDtypeStruct(shape, BF16) for shape in (edge, edge, kernel.shape, images.shape)
        ],
        scratch_shapes=[pltpu.SemaphoreType.DMA((4,))],
        compiler_params=pltpu.CompilerParams(vmem_limit_bytes=4 * MIB),
        name="edge_rows",
    )(in_hbm(images), in_hbm(kernel))


def small_call(kernel, name, *operands, out):
    return pl.pallas_call(
        kernel,
        in_specs=[resident()] * len(operands),
        out_specs=[resident()] * len(out),
        out_shape=out,
        compiler_params=pltpu.CompilerParams(vmem_limit_bytes=4 * MIB),
        name=name,
    )(*operands)


def fold(value, received, stage):
    half = jax.ShapeDtypeStruct((value.shape[0] // 2, value.shape[1]), value.dtype)
    return small_call(
        functools.partial(fold_kernel, stage), "fold", value, received, out=[half, half]
    )


def join(value, received, stage):
    whole = jax.ShapeDtypeStruct((value.shape[0] * 2, value.shape[1]), value.dtype)
    return small_call(
        functools.partial(join_kernel, stage), "join", value, received, out=[whole]
    )[0]


def finish(stage, value, out=None):
    part, lanes = value.shape
    operands, aliases = (value,), {}
    if out is not None:
        operands, aliases = (value, out), {1: 0}
    space = pl.BlockSpec(memory_space=pltpu.HBM)
    return pl.pallas_call(
        functools.partial(finish_kernel, stage, out is None),
        in_specs=[resident(), space][: len(operands)],
        out_specs=space,
        out_shape=jax.ShapeDtypeStruct((2 * part, lanes), F32),
        scratch_shapes=[
            pltpu.VMEM((2, part // 2, lanes), F32),
            pltpu.SemaphoreType.DMA((2,)),
        ],
        input_output_aliases=aliases,
        compiler_params=pltpu.CompilerParams(vmem_limit_bytes=4 * MIB),
        name="finish",
    )(*operands)


def halos(ahead, across):
    count = lax.axis_size("rows")
    pairs = []
    for first in (0, 1):
        found = [(i, i + 1) for i in range(first, count - 1, 2)]
        pairs.append(found + [(i, j) for j, i in found])
    return lax.ppermute(ahead, "rows", pairs[0]), lax.ppermute(across, "rows", pairs[1])


def exchange(value, devices, stage):
    pairs = [(i, i ^ (stage[1] if i & 1 else stage[0])) for i in range(devices)]
    return lax.ppermute(value, AXES, pairs)


def beside(send, devices, stage, task, operands):
    send, operands = lax.optimization_barrier((send, operands))
    received = exchange(send, devices, stage)
    result = task(*operands)
    return lax.optimization_barrier((received, result))


def body(images, kernel, colors, offset, upstream):
    count, rows, width, cin = images.shape
    cout = kernel.shape[3]
    devices = lax.axis_size("dp") * lax.axis_size("rows")
    total_pix = count * rows * width * devices
    plan = stages(devices)
    ahead, across, kernel, maps = fetched(images, kernel)
    top, bot = halos(ahead, across)
    pre, acc, sums, images, upstream = forward(maps, images, kernel, upstream)
    low, high, value, send = edges(plan[0], top, bot, pre, upstream, kernel, acc, sums)
    state = {"next": 0, "moments": (), "grad": None}

    def summed(send, stage, many):
        first = state["next"]
        many = min(many, count - first)
        if many < 1:
            return exchange(send, devices, stage)
        state["next"] = first + many
        operands = (pre, low, high, upstream, images, top, bot, sums, *state["moments"])
        received, state["moments"] = beside(
            send, devices, stage, functools.partial(moments, first, many), operands
        )
        return received

    value = value + summed(send, plan[0], 0)
    for stage in plan[1:]:
        value = value + summed(value, stage, 2 if stage == plan[1] else 1)
    received = summed(value, plan[0], 1)
    first = state["next"]
    if first < count:
        operands = (pre, low, high, upstream, images, top, bot, sums, *state["moments"])
        state["moments"] = moments(first, count - first, *operands)
    value, send, grad_colors, mats, paint, paint_rows = whitened(
        total_pix,
        plan[0],
        value,
        received,
        colors,
        offset.reshape(1, cout),
        sums,
        *state["moments"],
    )
    received, (edge_ahead, edge_across, turned) = beside(
        send,
        devices,
        plan[0],
        lambda kernel, *operands: (*edge_gradients(*operands), turned_weights(kernel)),
        (kernel, low, high, upstream, mats, paint_rows),
    )
    state["next"] = 0
    shares = [1, 2, 1, 1, 1]

    def transfer(send, stage):
        first = state["next"]
        if first >= count:
            return exchange(send, devices, stage)
        many = min(shares.pop(0), count - first) if shares else count - first
        state["next"] = first + many
        operands = (pre_grad, grad_top, grad_bot, turned)
        if state["grad"] is not None:
            operands = (*operands, state["grad"])
        received, state["grad"] = beside(
            send, devices, stage, functools.partial(image_gradient, first, many), operands
        )
        return received

    cuts = []
    for stage in plan[1:]:
        if value.shape[0] % 32 == 0 and value.shape[0] > 144:
            value, send = fold(value, received, stage)
            cuts.append(stage)
        else:
            value = send = value + received
        if stage == plan[1]:
            send, edge_ahead, edge_across = lax.optimization_barrier(
                (send, edge_ahead, edge_across)
            )
            grad_top, grad_bot = halos(edge_ahead, edge_across)
            received, pre_grad = beside(
                send, devices, stage, gradients, (pre, low, high, upstream, mats, paint_rows)
            )
        elif stage == plan[2]:
            received, colored = beside(
                send, devices, stage, painted, (pre, low, high, paint, paint_rows)
            )
        else:
            received = transfer(send, stage)
    value = (value + received).astype(BF16)
    for stage in reversed(cuts):
        value = join(value, transfer(value, stage), stage)
    received, result = beside(
        value, devices, plan[0], functools.partial(finish, plan[0]), (value,)
    )
    first = state["next"]
    if first < count:
        operands = (pre_grad, grad_top, grad_bot, turned, state["grad"])
        state["grad"] = image_gradient(first, count - first, *operands)
    grad_kernel = finish(plan[0], received, result).reshape(3, 3, cin, cout)
    return colored, state["grad"], grad_kernel, grad_colors


def solution(mesh):
    placed = (P("dp", "rows", None, None), P(), P(), P(), P("dp", "rows", None, None))
    return jax.shard_map(
        body,
        mesh=mesh,
        in_specs=placed,
        out_specs=(P("dp", "rows", None, None), P("dp", "rows", None, None), P(), P()),
        check_vma=False,
    )
```

```python
import functools
import math

import jax
import jax.numpy as jnp
from jax import lax
from jax.experimental import pallas as pl
from jax.experimental.pallas import tpu as pltpu
from jax.sharding import PartitionSpec as P

NS_ITERS = 5
EPSILON = 1e-05
F32 = jnp.float32
BF16 = jnp.bfloat16
MIB = 1024 * 1024
AXES = ("dp", "rows")


def device_index():
    return lax.axis_index("dp") * lax.axis_size("rows") + lax.axis_index("rows")


def is_even():
    return lax.axis_index("rows") % 2 == 0


def is_upper(stage):
    index = device_index()
    return index & jnp.where(index & 1 != 0, stage[1], stage[0]) != 0


def stages(devices):
    bits = [1 << i for i in range(devices.bit_length() - 1)]
    plan = [(bit, bit) for bit in bits]
    if len(bits) > 2:
        plan[1:3] = [(4, 2), (2, 4)]
    return plan


def split(value):
    high = value.astype(BF16)
    return high, (value - high.astype(F32)).astype(BF16)


def dot(left, right, dims=((1,), (0,))):
    return lax.dot_general(left, right, (dims, ((), ())), preferred_element_type=F32)


def dot3(left, right):
    lh, ll = split(left)
    rh, rl = split(right)
    return dot(
        jnp.concatenate([lh, lh, ll], axis=1), jnp.concatenate([rh, rl, rh], axis=0)
    )


def shifted(value):
    width = value.shape[1]
    col = lax.broadcasted_iota(jnp.int32, (1, *value.shape[1:]), 1)
    after = jnp.where(col == width - 1, 0.0, pltpu.roll(value, width - 1, 1))
    before = jnp.where(col == 0, 0.0, pltpu.roll(value, 1, 1))
    return after, before


def merged(prod, shape):
    cout = shape[2]
    _, left = shifted(prod[:, :cout].reshape(shape))
    right, _ = shifted(prod[:, 2 * cout :].reshape(shape))
    return prod[:, cout : 2 * cout].reshape(shape) + left + right


def paired_rows(padded, wts, cout):
    rows, width, cin = padded.shape[0] - 2, *padded.shape[1:]
    pairs = rows // 2
    parts = [
        jnp.concatenate([padded[2 * k + a : 2 * k + a + 1] for k in range(pairs)], axis=0)
        for a in range(4)
    ]
    wide = jnp.concatenate(parts, axis=2).reshape(pairs * width, 4 * cin)
    outer = dot(wide[:, : 3 * cin], wts[: 3 * cin])
    shared = dot(wide, wts[3 * cin : 7 * cin])
    inner = dot(wide[:, cin:], wts[7 * cin :])
    shape = (pairs, width, cout)

    def added_up(left, middle, right):
        _, before = shifted(left.reshape(shape))
        after, _ = shifted(right.reshape(shape))
        return middle.reshape(shape) + before + after

    first = added_up(outer[:, :cout], outer[:, cout:], shared[:, :cout])
    second = added_up(shared[:, cout:], inner[:, :cout], inner[:, cout:])
    ordered = [part[k : k + 1] for k in range(pairs) for part in (first, second)]
    return jnp.concatenate(ordered, axis=0)


def column(row):
    size = row.shape[1]
    return jnp.broadcast_to(row, (size, size)).T


def pack(full):
    half = full.shape[0] // 2
    lane = lax.broadcasted_iota(jnp.int32, (half, full.shape[1]), 1)
    return jnp.where(lane < half, full[:half], full[half:])


def unpack(packed):
    half = packed.shape[0]
    lane = lax.broadcasted_iota(jnp.int32, packed.shape, 1)
    return jnp.concatenate(
        [jnp.where(lane < half, packed, 0.0), jnp.where(lane < half, 0.0, packed)], axis=0
    )


def statistics(held):
    third = held.shape[1] // 3
    return dot(held[:, third:], held[:, : 2 * third], ((0,), (0,)))


def forward_kernel(
    first, img, kern, upstream, pre_out, acc, sums, maps, ups, wts, held, map_sems, up_sems
):
    step = pl.program_id(0)
    last = pl.num_programs(0) - 1
    count, rows, width, cin = img.shape
    cout = kern.shape[3]
    inner = (rows - 2) * width

    def map_copy(image):
        return pltpu.make_async_copy(img.at[image], maps.at[image], map_sems.at[image])

    def up_copy(image):
        return pltpu.make_async_copy(upstream.at[image], ups.at[image], up_sems.at[image])

    @pl.when(step == 0)
    def _():
        up_copy(0).start()
        for image in range(1, count):
            map_copy(image).start()
            up_copy(image).start()
        blank = jnp.zeros((cin, cout), BF16)
        blocks = [(kern[a, 0], kern[a, 1]) for a in range(3)]
        blocks += [
            (kern[a, 2] if a < 3 else blank, kern[a - 1, 0] if a > 0 else blank) for a in range(4)
        ]
        blocks += [(kern[a, 1], kern[a, 2]) for a in range(3)]
        for index, (one, two) in enumerate(blocks):
            wts[index * cin : (index + 1) * cin, :cout] = one
            wts[index * cin : (index + 1) * cin, cout:] = two
        acc[...] = jnp.zeros_like(acc)
        sums[...] = jnp.zeros_like(sums)
        held[...] = jnp.zeros_like(held)
        sample = paired_rows(maps[0, 0:4], wts, cout).reshape(2 * width, cout)
        sums[2:3] = jnp.sum(sample, axis=0, keepdims=True) / (2 * width)

    @pl.when(step > 0)
    def _():
        map_copy(step).wait()

    up_copy(step).wait()
    shift = sums[2:3]
    acc[...] += statistics(held[...])
    blank = jnp.zeros((1, width, cin), BF16)
    padded = jnp.concatenate([blank, maps[step], blank], axis=0)
    pre = paired_rows(padded, wts, cout)
    pre_out[step] = pre
    mid = pre[1 : rows - 1].reshape(inner, cout)
    delta = mid - shift
    up = ups[step, 1 : rows - 1].reshape(inner, cout)
    high, low = split(delta)
    held[:, :cout] = low
    held[:, cout : 2 * cout] = high
    held[:, 2 * cout :] = up
    sums[0:1] += jnp.sum(delta, axis=0, keepdims=True)
    sums[1:2] += jnp.sum(up.astype(F32), axis=0, keepdims=True)

    @pl.when(step == last)
    def _():
        acc[...] += statistics(held[...])


def sides(ahead, across):
    place = lax.axis_index("rows")
    even = is_even()
    outermost = jnp.where(even, place == 0, place == lax.axis_size("rows") - 1)
    across = jnp.where(outermost, jnp.zeros_like(across), across)
    return jnp.where(even, across, ahead), jnp.where(even, ahead, across)


def edge_choice(first, final):
    even = is_even()
    return jnp.where(even, final, first), jnp.where(even, first, final)


def fetch_kernel(images, kern, ahead, across, taps, maps, sems):
    last = images.shape[1] - 1
    even = is_even()
    pairs = (
        (images.at[:, pl.ds(jnp.where(even, last, 0), 1)], ahead),
        (images.at[:, pl.ds(jnp.where(even, 0, last), 1)], across),
        (kern, taps),
        (images.at[0], maps.at[0]),
    )
    copies = [
        pltpu.make_async_copy(source, target, sems.at[index])
        for index, (source, target) in enumerate(pairs)
    ]
    for copy in copies:
        copy.start()
    for copy in copies:
        copy.wait()


def edge_kernel(total, stage, ahead, across, pre, ups, kern, acc, sums, low, high, keep, send, stats):
    count, _, width, cin = ahead.shape
    cout = kern.shape[3]
    last = pre.shape[1] - 1
    top, bot = sides(ahead[...], across[...])
    pixels = count * width
    shape = (count, width, cout)
    edges = []
    for a, source, row, out in ((0, top, 0, low), (2, bot, last, high)):
        taps = jnp.concatenate([kern[a, c] for c in range(3)], axis=1)
        value = merged(dot(source.reshape(pixels, cin), taps), shape) + pre[:, row]
        out[:, 0] = value
        edges.append(value.reshape(pixels, cout))
    shift = sums[2:3]
    delta = jnp.concatenate(edges, axis=0) - shift
    up = jnp.concatenate(
        [ups[:, 0].reshape(pixels, cout), ups[:, last].reshape(pixels, cout)], axis=0
    )
    big, small = split(delta)
    gram = acc[...] + statistics(jnp.concatenate([small, big, up], axis=1))
    moved = sums[0:1] + jnp.sum(delta, axis=0, keepdims=True)
    up_sum = sums[1:2] + jnp.sum(up.astype(F32), axis=0, keepdims=True)
    mixed = gram[:cout, :cout]
    square = gram[:cout, cout:] + mixed + mixed.T
    cross = gram[cout:, :cout] + gram[cout:, cout:]
    raw = moved + total * shift
    square = square + column(moved) * shift + column(shift) * raw
    cross = cross + column(up_sum) * shift
    half = cout // 2
    stats[0:half] = pack(square)
    stats[half : 2 * half] = pack(cross)
    stats[2 * half :] = jnp.zeros_like(stats[2 * half :])
    stats[2 * half : 2 * half + 1] = raw
    stats[2 * half + 1 : 2 * half + 2] = up_sum
    part = keep.shape[0]
    upper = is_upper(stage)
    keep[...] = jnp.where(upper, stats[part:], stats[:part])
    send[...] = jnp.where(upper, stats[:part], stats[part:])


def spread(blocks):
    zero = jnp.zeros(blocks.shape[1:], F32)
    return jnp.concatenate(
        [
            jnp.concatenate([blocks[0], zero], axis=1),
            jnp.concatenate([zero, blocks[1]], axis=1),
        ],
        axis=0,
    )


def group_sum(value, half):
    cols = jnp.sum(value, axis=0, keepdims=True)
    lane = lax.broadcasted_iota(jnp.int32, cols.shape, 1)
    low = jnp.sum(jnp.where(lane < half, cols, 0.0), axis=1, keepdims=True)
    high = jnp.sum(jnp.where(lane < half, 0.0, cols), axis=1, keepdims=True)
    return jnp.where(lane < half, low, high)


def whitening(stats, colors, offset, total_pix, half):
    cout = 2 * half
    row_i = lax.broadcasted_iota(jnp.int32, (cout, cout), 0)
    col_i = lax.broadcasted_iota(jnp.int32, (cout, cout), 1)
    eye = jnp.where(row_i == col_i, 1.0, 0.0)
    block = jnp.where((row_i < half) == (col_i < half), 1.0, 0.0)
    square = unpack(stats[0:half])
    cross = unpack(stats[half : 2 * half])
    average = stats[2 * half : 2 * half + 1] / total_pix
    up_total = stats[2 * half + 1 : 2 * half + 2]
    sigma = square / total_pix - block * (column(average) * average) + EPSILON * eye
    cross = cross - block * (column(up_total) * average)
    grad = dot3(colors.T, cross)
    direction = grad + grad.T
    traces = group_sum(sigma * eye, half)
    normed = sigma / traces
    zero = jnp.zeros_like(normed)

    def stacked(value, tangent):
        return jnp.concatenate(
            [
                jnp.concatenate([value, tangent], axis=1),
                jnp.concatenate([zero, value], axis=1),
            ],
            axis=0,
        )

    source = stacked(normed, direction)
    value = 1.5 * eye - 0.5 * normed
    tangent = -0.5 * direction
    for _ in range(NS_ITERS - 1):
        first = jnp.concatenate([value, tangent], axis=1)
        both = dot3(first, jnp.concatenate([stacked(value, tangent), source], axis=1))
        squared = both[:, : 2 * cout]
        scaled = stacked(both[:, 2 * cout : 3 * cout], both[:, 3 * cout :])
        cubed = dot3(squared, scaled)
        value = 1.5 * value - 0.5 * cubed[:, :cout]
        tangent = 1.5 * tangent - 0.5 * cubed[:, cout:]
    inverse = 1.0 / jnp.sqrt(traces)
    whitener = value * inverse
    shared = group_sum(tangent * normed, half) + 0.5 * group_sum(direction * value, half)
    symmetric = (tangent - eye * shared) * (inverse / traces)
    mixed = dot3(colors, whitener)
    color_sum = dot3(cross, whitener.T)
    up_mean = jnp.broadcast_to(up_total / total_pix, (8, cout))
    bias = -dot3(up_mean, mixed)[0:1]
    return average, mixed, symmetric / total_pix, bias, offset, color_sum


def image_moments(image, pre, low, high, ups, img, ahead, across, sums):
    rows, width, cin = img.shape[1:]
    cout = pre.shape[3]
    pixels = rows * width
    top, bot = sides(ahead[image], across[image])
    padded = jnp.concatenate([top, img[image], bot], axis=0)
    turned = padded.reshape((rows + 2) * width, cin).T
    full = jnp.concatenate([low[image], pre[image, 1 : rows - 1], high[image]], axis=0)
    columns = []
    for value in (ups[image], (full - sums[2:3]).astype(BF16)):
        after, before = shifted(value.astype(F32))
        columns += [after.astype(BF16), value, before.astype(BF16)]
    right = jnp.concatenate(columns, axis=2).reshape(pixels, 6 * cout)
    left = jnp.concatenate([turned[:, a * width : a * width + pixels] for a in range(3)], axis=0)
    tiles = [turned[:, row * width : (row + 1) * width].astype(F32) for row in range(rows + 2)]
    middle = functools.reduce(jnp.add, tiles[2:rows])
    outer = ((0, 1), (1, rows), (rows, rows + 1))
    totals = jnp.concatenate([middle + tiles[one] + tiles[two] for one, two in outer], axis=0)
    return dot(left, right), totals


def moment_kernel(first, count, *refs):
    acc, maps = refs[-2:]
    found = [image_moments(first + index, *refs[:8]) for index in range(count)]
    if len(refs) == 12:
        found.append((refs[8][...], refs[9][...]))
    acc[...] = functools.reduce(jnp.add, [product for product, _ in found])
    maps[...] = functools.reduce(jnp.add, [totals for _, totals in found])


def whitening_kernel(
    total_pix,
    stage,
    own,
    other,
    colors,
    offset,
    sums,
    acc,
    maps,
    keep,
    send,
    grad_colors,
    mats,
    paint,
    paint_rows,
    stats,
):
    cout = 2 * colors.shape[1]
    half = cout // 2
    cin = acc.shape[0] // 3
    scaling = 1.0 / math.sqrt(total_pix)
    join_kernel(stage, own, other, stats)
    average, mixed, symmetric, bias, offs, color_sum = whitening(
        stats[...], spread(colors[...]), offset[...], total_pix, half
    )
    blank = jnp.zeros((cout, cout), BF16)
    mixed_h, mixed_l = split(mixed)
    color_h, color_l = split(mixed.T)
    sym_h, sym_l = split(symmetric)
    for target, blocks in (
        (mats, ((sym_h, sym_l), (mixed_h, mixed_l), (sym_h, blank))),
        (paint, ((color_h, color_l), (color_h, blank))),
    ):
        for index, (one, two) in enumerate(blocks):
            target[index * cout : (index + 1) * cout, :cout] = one
            target[index * cout : (index + 1) * cout, cout:] = two
    paint_rows[...] = jnp.zeros_like(paint_rows)
    paint_rows[0:1] = average
    paint_rows[1:2] = offs
    paint_rows[2:3] = bias
    scaled = color_sum * scaling
    grad_colors[0] = scaled[:half, :half]
    grad_colors[1] = pltpu.roll(scaled[half:], half, 1)[:, :half]

    moved = jnp.broadcast_to(sums[2:3] - average, (8, cout))
    constant = (bias + dot3(moved, symmetric)[0:1]) * scaling
    tall_h = jnp.concatenate([mixed_h, sym_h], axis=0)
    tall_l = jnp.concatenate([mixed_l, sym_l], axis=0)
    right = jnp.concatenate(
        [
            jnp.concatenate([tall_h, tall_l], axis=1),
            jnp.concatenate([tall_h, jnp.zeros_like(tall_l)], axis=1),
        ],
        axis=0,
    )
    lane = lax.broadcasted_iota(jnp.int32, (cin, maps.shape[1]), 1)
    seen = (lane < maps.shape[1] - 1, lane >= 0, lane > 0)
    parts = []
    for a in range(3):
        place = slice(a * cin, (a + 1) * cin)
        for c in range(3):
            pair = [acc[place, (k + c) * cout : (k + c + 1) * cout] for k in (0, 3)]
            left = jnp.concatenate(split(jnp.concatenate(pair, axis=1)), axis=1)
            result = dot(left, right)
            total = jnp.sum(jnp.where(seen[c], maps[place], 0.0), axis=1, keepdims=True)
            result = (result[:, :cout] + result[:, cout:]) * scaling + total * constant
            parts += [result[: cin // 2], result[cin // 2 :]]
    upper = is_upper(stage)
    for index in range(9):
        place = slice(index * cin // 2, (index + 1) * cin // 2)
        keep[place] = jnp.where(upper, parts[9 + index], parts[index])
        send[place] = jnp.where(upper, parts[index], parts[9 + index])


def centred_halves(image, pre, low, high, average):
    rows, width, cout = pre.shape[1:]
    full = jnp.concatenate([low[image], pre[image, 1 : rows - 1], high[image]], axis=0)
    return split(full.reshape(rows * width, cout) - average)


def edge_gradient_kernel(low, high, ups, mats, paint_rows, edge_ahead, edge_across):
    count, _, width, cout = low.shape
    last = ups.shape[1] - 1
    pre = jnp.concatenate([low[:, 0], high[:, 0]], axis=0).reshape(2 * count * width, cout)
    up = jnp.concatenate([ups[:, 0], ups[:, last]], axis=0).reshape(2 * count * width, cout)
    grad = pre_gradient(*split(pre - paint_rows[0:1]), up, mats, paint_rows)
    shaped = grad.reshape(2 * count, width, cout)
    edge_ahead[:, 0], edge_across[:, 0] = edge_choice(shaped[:count], shaped[count:])


def pre_gradient(big, small, up, mats, paint_rows):
    cout = up.shape[1]
    result = dot(jnp.concatenate([big, up, small], axis=1), mats[...])
    return (result[:, :cout] + result[:, cout:] + paint_rows[2:3]).astype(BF16)


def gradient_kernel(pre, low, high, ups, mats, paint_rows, pre_grad):
    image = pl.program_id(0)
    rows, width, cout = pre.shape[1:]
    big, small = centred_halves(image, pre, low, high, paint_rows[0:1])
    up = ups[image].reshape(rows * width, cout)
    grad = pre_gradient(big, small, up, mats, paint_rows)
    pre_grad[image] = grad.reshape(rows, width, cout)


def paint_kernel(pre, low, high, paint, paint_rows, colored):
    rows, width, cout = pre.shape[1:]
    halves = centred_halves(pl.program_id(0), pre, low, high, paint_rows[0:1])
    result = dot(jnp.concatenate(halves, axis=1), paint[...])
    result = result[:, :cout] + result[:, cout:] + paint_rows[1:2]
    colored[0] = result.astype(BF16).reshape(rows, width, cout)


def turn_kernel(kern, out):
    cout = kern.shape[3]
    for a in range(3):
        for c in range(3):
            tap = (a * 3 + c) * cout
            out[tap : tap + cout] = kern[a, c].T


def image_kernel(first, pre_grad, ahead, across, wts, *rest):
    out = rest[-1]
    image = pl.program_id(0) + first
    top, bot = sides(ahead[image], across[image])
    rows, width, cout = pre_grad.shape[1:]
    cin = wts.shape[1]
    exact = jnp.concatenate([top, pre_grad[image], bot], axis=0).astype(F32)
    after, before = shifted(exact)
    taps = [value.astype(BF16) for value in (after, exact, before)]
    wide = jnp.concatenate(
        [taps[c][2 - a : 2 - a + rows] for a in range(3) for c in range(3)], axis=2
    )
    result = dot(wide.reshape(rows * width, 9 * cout), wts[...])
    out[0] = result.astype(BF16).reshape(rows, width, cin)


def fold_kernel(stage, value, received, keep, send):
    upper = is_upper(stage)
    part = keep.shape[0]
    low = value[:part] + received[:part]
    high = value[part:] + received[part:]
    keep[...] = jnp.where(upper, high, low)
    send[...] = jnp.where(upper, low, high)


def join_kernel(stage, value, received, out):
    upper = is_upper(stage)
    part = value.shape[0]
    out[:part] = jnp.where(upper, received[...], value[...])
    out[part:] = jnp.where(upper, value[...], received[...])


def finish_kernel(stage, own, value, *rest):
    out, held, sems = rest[-3:]
    count, size = held.shape[:2]
    upper = is_upper(stage) if own else jnp.logical_not(is_upper(stage))
    start = jnp.where(upper, count * size, 0)
    copies = []
    for index in range(count):
        held[index] = value[index * size : (index + 1) * size].astype(F32)
        place = pl.ds(pl.multiple_of(start + index * size, size), size)
        copies.append(pltpu.make_async_copy(held.at[index], out.at[place], sems.at[index]))
        copies[-1].start()
    for copy in copies:
        copy.wait()


def image_spec(shape, place=lambda b: b):
    return pl.BlockSpec((1, *shape[1:]), lambda b: (place(b),) + (0,) * (len(shape) - 1))


def whole_spec(shape):
    return pl.BlockSpec(shape, lambda b: (0,) * len(shape))


def in_hbm(value):
    return pltpu.with_memory_space_constraint(value, pltpu.HBM)


def resident():
    return pl.BlockSpec(memory_space=pltpu.VMEM)


def forward(first, images, taps, upstream):
    count, rows, width, cin = images.shape
    cout = taps.shape[3]
    shapes = [
        ((count, rows, width, cout), F32),
        ((2 * cout, 2 * cout), F32),
        ((8, cout), F32),
        (images.shape, BF16),
        (upstream.shape, BF16),
    ]
    space = pl.BlockSpec(memory_space=pltpu.HBM)
    return pl.pallas_call(
        forward_kernel,
        grid=(count,),
        in_specs=[resident(), space, resident(), space],
        out_specs=[resident()] * len(shapes),
        out_shape=[jax.ShapeDtypeStruct(shape, dtype) for shape, dtype in shapes],
        scratch_shapes=[
            pltpu.VMEM((10 * cin, 2 * cout), BF16),
            pltpu.VMEM(((rows - 2) * width, 3 * cout), BF16),
            pltpu.SemaphoreType.DMA((count,)),
            pltpu.SemaphoreType.DMA((count,)),
        ],
        input_output_aliases={0: 3},
        compiler_params=pltpu.CompilerParams(vmem_limit_bytes=20 * MIB),
        cost_estimate=pl.CostEstimate(
            flops=2 * count * rows * width * 9 * cin * cout,
            bytes_accessed=2 * images.size + 2 * upstream.size + 4 * upstream.size,
            transcendentals=0,
        ),
        name="forward_inner",
    )(first, in_hbm(images), taps, in_hbm(upstream))


def edges(stage, top, bot, pre, upstream, kernel, acc, sums):
    count, rows, width, cout = pre.shape
    part = (cout + 16) // 2
    edge = (count, 1, width, cout)
    shapes = [edge, edge, (part, cout), (part, cout)]
    return pl.pallas_call(
        functools.partial(edge_kernel, count * rows * width, stage),
        in_specs=[resident()] * 7,
        out_specs=[resident()] * 4,
        out_shape=[jax.ShapeDtypeStruct(shape, F32) for shape in shapes],
        scratch_shapes=[pltpu.VMEM((2 * part, cout), F32)],
        compiler_params=pltpu.CompilerParams(vmem_limit_bytes=12 * MIB),
        cost_estimate=pl.CostEstimate(
            flops=2 * 2 * count * width * 3 * top.shape[3] * cout,
            bytes_accessed=4 * top.size + 24 * count * width * cout,
            transcendentals=0,
        ),
        name="forward_edges",
    )(top, bot, pre, upstream, kernel, acc, sums)


def moments(first, count, pre, low, high, upstream, images, top, bot, sums, *sofar):
    width, cin = images.shape[2:]
    cout = upstream.shape[3]
    rows = images.shape[1]
    operands = (pre, low, high, upstream, images, top, bot, sums, *sofar)
    return pl.pallas_call(
        functools.partial(moment_kernel, first, count),
        in_specs=[resident()] * len(operands),
        out_specs=[resident()] * 2,
        out_shape=[
            jax.ShapeDtypeStruct((3 * cin, 6 * cout), F32),
            jax.ShapeDtypeStruct((3 * cin, width), F32),
        ],
        input_output_aliases={8: 0, 9: 1} if sofar else {},
        compiler_params=pltpu.CompilerParams(vmem_limit_bytes=28 * MIB),
        cost_estimate=pl.CostEstimate(
            flops=2 * count * rows * width * 18 * cin * cout, bytes_accessed=8 * MIB, transcendentals=0
        ),
        name="moments",
    )(*operands)


def whitened(total_pix, stage, own, other, colors, offset, sums, acc, maps):
    half = colors.shape[1]
    cout = 2 * half
    cin = acc.shape[0] // 3
    shapes = [
        ((9 * cin // 2, cout), F32),
        ((9 * cin // 2, cout), F32),
        ((2, half, half), F32),
        ((3 * cout, 2 * cout), BF16),
        ((2 * cout, 2 * cout), BF16),
        ((8, cout), F32),
    ]
    return pl.pallas_call(
        functools.partial(whitening_kernel, total_pix, stage),
        in_specs=[resident()] * 7,
        out_specs=[resident()] * len(shapes),
        out_shape=[jax.ShapeDtypeStruct(shape, dtype) for shape, dtype in shapes],
        scratch_shapes=[pltpu.VMEM((cout + 16, cout), F32)],
        compiler_params=pltpu.CompilerParams(vmem_limit_bytes=20 * MIB),
        cost_estimate=pl.CostEstimate(
            flops=2 * 9 * cin * 8 * cout * cout, bytes_accessed=8 * MIB, transcendentals=0
        ),
        name="whitening",
    )(own, other, colors, offset, sums, acc, maps)


def edge_gradients(low, high, upstream, mats, paint_rows):
    return pl.pallas_call(
        edge_gradient_kernel,
        in_specs=[resident()] * 5,
        out_specs=[resident()] * 2,
        out_shape=[jax.ShapeDtypeStruct(low.shape, BF16)] * 2,
        compiler_params=pltpu.CompilerParams(vmem_limit_bytes=16 * MIB),
        name="edge_gradients",
    )(low, high, upstream, mats, paint_rows)


def gradients(pre, low, high, upstream, mats, paint_rows):
    count, rows, width, cout = pre.shape
    return pl.pallas_call(
        gradient_kernel,
        grid=(count,),
        in_specs=[resident()] * 6,
        out_specs=resident(),
        out_shape=jax.ShapeDtypeStruct(pre.shape, BF16),
        compiler_params=pltpu.CompilerParams(vmem_limit_bytes=16 * MIB),
        cost_estimate=pl.CostEstimate(
            flops=2 * count * rows * width * 6 * cout * cout,
            bytes_accessed=8 * pre.size,
            transcendentals=0,
        ),
        name="pre_gradient",
    )(pre, low, high, upstream, mats, paint_rows)


def painted(pre, low, high, paint, paint_rows):
    count, rows, width, cout = pre.shape
    return pl.pallas_call(
        paint_kernel,
        grid=(count,),
        in_specs=[resident()] * 5,
        out_specs=image_spec(pre.shape),
        out_shape=jax.ShapeDtypeStruct(pre.shape, BF16),
        compiler_params=pltpu.CompilerParams(vmem_limit_bytes=16 * MIB),
        cost_estimate=pl.CostEstimate(
            flops=2 * count * rows * width * 4 * cout * cout,
            bytes_accessed=6 * pre.size,
            transcendentals=0,
        ),
        name="colored",
    )(pre, low, high, paint, paint_rows)


def turned_weights(kernel):
    cin, cout = kernel.shape[2:]
    return pl.pallas_call(
        turn_kernel,
        out_shape=jax.ShapeDtypeStruct((9 * cout, cin), BF16),
        compiler_params=pltpu.CompilerParams(vmem_limit_bytes=4 * MIB),
        name="turned_weights",
    )(kernel)


def image_gradient(first, count, pre_grad, top, bot, turned, out=None):
    images, rows, width, cout = pre_grad.shape
    cin = turned.shape[1]
    shape = (images, rows, width, cin)

    def place(b):
        return b + first

    operands = [pre_grad, top, bot, turned]
    in_specs = [resident()] * 4
    aliases = {}
    if out is not None:
        operands.append(out)
        in_specs.append(pl.BlockSpec(memory_space=pl.ANY))
        aliases = {4: 0}
    return pl.pallas_call(
        functools.partial(image_kernel, first),
        grid=(count,),
        in_specs=in_specs,
        out_specs=image_spec(shape, place),
        out_shape=jax.ShapeDtypeStruct(shape, BF16),
        input_output_aliases=aliases,
        compiler_params=pltpu.CompilerParams(vmem_limit_bytes=12 * MIB),
        cost_estimate=pl.CostEstimate(
            flops=2 * count * rows * width * 9 * cin * cout,
            bytes_accessed=2 * count * rows * width * (cin + cout),
            transcendentals=0,
        ),
        name="image_gradient",
    )(*operands)


def fetched(images, kernel):
    count, rows, width, cin = images.shape
    edge = (count, 1, width, cin)
    space = pl.BlockSpec(memory_space=pltpu.HBM)
    return pl.pallas_call(
        fetch_kernel,
        in_specs=[space, space],
        out_specs=[resident()] * 4,
        out_shape=[
            jax.ShapeDtypeStruct(shape, BF16) for shape in (edge, edge, kernel.shape, images.shape)
        ],
        scratch_shapes=[pltpu.SemaphoreType.DMA((4,))],
        compiler_params=pltpu.CompilerParams(vmem_limit_bytes=4 * MIB),
        name="edge_rows",
    )(in_hbm(images), in_hbm(kernel))


def small_call(kernel, name, *operands, out):
    return pl.pallas_call(
        kernel,
        in_specs=[resident()] * len(operands),
        out_specs=[resident()] * len(out),
        out_shape=out,
        compiler_params=pltpu.CompilerParams(vmem_limit_bytes=4 * MIB),
        name=name,
    )(*operands)


def fold(value, received, stage):
    half = jax.ShapeDtypeStruct((value.shape[0] // 2, value.shape[1]), value.dtype)
    return small_call(
        functools.partial(fold_kernel, stage), "fold", value, received, out=[half, half]
    )


def join(value, received, stage):
    whole = jax.ShapeDtypeStruct((value.shape[0] * 2, value.shape[1]), value.dtype)
    return small_call(
        functools.partial(join_kernel, stage), "join", value, received, out=[whole]
    )[0]


def finish(stage, value, out=None):
    part, lanes = value.shape
    operands, aliases = (value,), {}
    if out is not None:
        operands, aliases = (value, out), {1: 0}
    space = pl.BlockSpec(memory_space=pltpu.HBM)
    return pl.pallas_call(
        functools.partial(finish_kernel, stage, out is None),
        in_specs=[resident(), space][: len(operands)],
        out_specs=space,
        out_shape=jax.ShapeDtypeStruct((2 * part, lanes), F32),
        scratch_shapes=[
            pltpu.VMEM((2, part // 2, lanes), F32),
            pltpu.SemaphoreType.DMA((2,)),
        ],
        input_output_aliases=aliases,
        compiler_params=pltpu.CompilerParams(vmem_limit_bytes=4 * MIB),
        name="finish",
    )(*operands)


def halos(ahead, across):
    count, groups = lax.axis_size("rows"), lax.axis_size("dp")
    offset = 2 if groups % 4 == 0 else 1 if groups % 2 == 0 else 0
    pairs = ([], [])
    for group in range(groups):
        for place in range(count):
            for first in (0, 1):
                partner = place + 1 if place % 2 == first else place - 1
                inside = 0 <= partner < count
                other = (group, partner) if inside else (group ^ offset, place)
                pairs[first].append((group * count + place, other[0] * count + other[1]))
    return lax.ppermute(ahead, AXES, pairs[0]), lax.ppermute(across, AXES, pairs[1])


def exchange(value, devices, stage):
    pairs = [(i, i ^ (stage[1] if i & 1 else stage[0])) for i in range(devices)]
    return lax.ppermute(value, AXES, pairs)


def beside(send, devices, stage, task, operands):
    send, operands = lax.optimization_barrier((send, operands))
    received = exchange(send, devices, stage)
    result = task(*operands)
    return lax.optimization_barrier((received, result))


def body(images, kernel, colors, offset, upstream):
    count, rows, width, cin = images.shape
    cout = kernel.shape[3]
    devices = lax.axis_size("dp") * lax.axis_size("rows")
    total_pix = count * rows * width * devices
    plan = stages(devices)
    ahead, across, kernel, maps = fetched(images, kernel)
    top, bot = halos(ahead, across)
    pre, acc, sums, images, upstream = forward(maps, images, kernel, upstream)
    low, high, value, send = edges(plan[0], top, bot, pre, upstream, kernel, acc, sums)
    state = {"next": 0, "moments": (), "grad": None}

    def summed(send, stage, many):
        first = state["next"]
        many = min(many, count - first)
        if many == 0:
            return exchange(send, devices, stage)
        state["next"] = first + many
        operands = (pre, low, high, upstream, images, top, bot, sums, *state["moments"])
        received, state["moments"] = beside(
            send, devices, stage, functools.partial(moments, first, many), operands
        )
        return received

    value = value + exchange(send, devices, plan[0])
    for stage in plan[1:]:
        value = value + summed(value, stage, 2 if stage in plan[2:4] else 1)
    received = exchange(value, devices, plan[0])
    first = state["next"]
    if first < count:
        operands = (pre, low, high, upstream, images, top, bot, sums, *state["moments"])
        state["moments"] = moments(first, count - first, *operands)
    value, send, grad_colors, mats, paint, paint_rows = whitened(
        total_pix,
        plan[0],
        value,
        received,
        colors,
        offset.reshape(1, cout),
        sums,
        *state["moments"],
    )
    received, (edge_ahead, edge_across, turned) = beside(
        send,
        devices,
        plan[0],
        lambda kernel, *operands: (*edge_gradients(*operands), turned_weights(kernel)),
        (kernel, low, high, upstream, mats, paint_rows),
    )
    state["next"] = 0
    shares = [1, 1, 1, 1, 2]

    def transfer(send, stage):
        first = state["next"]
        if first >= count:
            return exchange(send, devices, stage)
        many = min(shares.pop(0), count - first) if shares else count - first
        state["next"] = first + many
        operands = (pre_grad, grad_top, grad_bot, turned)
        if state["grad"] is not None:
            operands = (*operands, state["grad"])
        received, state["grad"] = beside(
            send, devices, stage, functools.partial(image_gradient, first, many), operands
        )
        return received

    cuts = []
    for stage in plan[1:]:
        if value.shape[0] % 32 == 0 and value.shape[0] > 144:
            value, send = fold(value, received, stage)
            cuts.append(stage)
        else:
            value = send = value + received
        if stage == plan[1]:
            send, edge_ahead, edge_across = lax.optimization_barrier(
                (send, edge_ahead, edge_across)
            )
            grad_top, grad_bot = halos(edge_ahead, edge_across)
            received, pre_grad = beside(
                send, devices, stage, gradients, (pre, low, high, upstream, mats, paint_rows)
            )
        elif stage == plan[2]:
            received, colored = beside(
                send, devices, stage, painted, (pre, low, high, paint, paint_rows)
            )
        else:
            received = transfer(send, stage)
    value = (value + received).astype(BF16)
    for stage in reversed(cuts):
        value = join(value, transfer(value, stage), stage)
    received, result = beside(
        value, devices, plan[0], functools.partial(finish, plan[0]), (value,)
    )
    first = state["next"]
    if first < count:
        operands = (pre_grad, grad_top, grad_bot, turned, state["grad"])
        state["grad"] = image_gradient(first, count - first, *operands)
    grad_kernel = finish(plan[0], received, result).reshape(3, 3, cin, cout)
    return colored, state["grad"], grad_kernel, grad_colors


def solution(mesh):
    placed = (P("dp", "rows", None, None), P(), P(), P(), P("dp", "rows", None, None))
    return jax.shard_map(
        body,
        mesh=mesh,
        in_specs=placed,
        out_specs=(P("dp", "rows", None, None), P("dp", "rows", None, None), P(), P()),
        check_vma=False,
    )
```

```python
import functools
import math

import jax
import jax.numpy as jnp
from jax import lax
from jax.experimental import pallas as pl
from jax.experimental.pallas import tpu as pltpu
from jax.sharding import PartitionSpec as P

NS_ITERS = 5
EPSILON = 1e-05
F32 = jnp.float32
BF16 = jnp.bfloat16
MIB = 1024 * 1024
AXES = ("dp", "rows")


def device_index():
    return lax.axis_index("dp") * lax.axis_size("rows") + lax.axis_index("rows")


def is_even():
    return lax.axis_index("rows") % 2 == 0


def is_upper(stage):
    index = device_index()
    return index & jnp.where(index & 1 != 0, stage[1], stage[0]) != 0


def stages(devices):
    bits = [1 << i for i in range(devices.bit_length() - 1)]
    plan = [(bit, bit) for bit in bits]
    if len(bits) > 2:
        plan[1:3] = [(4, 2), (2, 4)]
    return plan


def split(value):
    high = value.astype(BF16)
    return high, (value - high.astype(F32)).astype(BF16)


def dot(left, right, dims=((1,), (0,))):
    return lax.dot_general(left, right, (dims, ((), ())), preferred_element_type=F32)


def dot3(left, right):
    lh, ll = split(left)
    rh, rl = split(right)
    return dot(
        jnp.concatenate([lh, lh, ll], axis=1), jnp.concatenate([rh, rl, rh], axis=0)
    )


def shifted(value):
    width = value.shape[1]
    col = lax.broadcasted_iota(jnp.int32, (1, *value.shape[1:]), 1)
    after = jnp.where(col == width - 1, 0.0, pltpu.roll(value, width - 1, 1))
    before = jnp.where(col == 0, 0.0, pltpu.roll(value, 1, 1))
    return after, before


def merged(prod, shape):
    cout = shape[2]
    _, left = shifted(prod[:, :cout].reshape(shape))
    right, _ = shifted(prod[:, 2 * cout :].reshape(shape))
    return prod[:, cout : 2 * cout].reshape(shape) + left + right


def paired_rows(padded, wts, cout):
    rows, width, cin = padded.shape[0] - 2, *padded.shape[1:]
    pairs = rows // 2
    parts = [
        jnp.concatenate([padded[2 * k + a : 2 * k + a + 1] for k in range(pairs)], axis=0)
        for a in range(4)
    ]
    wide = jnp.concatenate(parts, axis=2).reshape(pairs * width, 4 * cin)
    outer = dot(wide[:, : 3 * cin], wts[: 3 * cin])
    shared = dot(wide, wts[3 * cin : 7 * cin])
    inner = dot(wide[:, cin:], wts[7 * cin :])
    shape = (pairs, width, cout)

    def added_up(left, middle, right):
        _, before = shifted(left.reshape(shape))
        after, _ = shifted(right.reshape(shape))
        return middle.reshape(shape) + before + after

    first = added_up(outer[:, :cout], outer[:, cout:], shared[:, :cout])
    second = added_up(shared[:, cout:], inner[:, :cout], inner[:, cout:])
    ordered = [part[k : k + 1] for k in range(pairs) for part in (first, second)]
    return jnp.concatenate(ordered, axis=0)


def column(row):
    size = row.shape[1]
    return jnp.broadcast_to(row, (size, size)).T


def pack(full):
    half = full.shape[0] // 2
    lane = lax.broadcasted_iota(jnp.int32, (half, full.shape[1]), 1)
    return jnp.where(lane < half, full[:half], full[half:])


def unpack(packed):
    half = packed.shape[0]
    lane = lax.broadcasted_iota(jnp.int32, packed.shape, 1)
    return jnp.concatenate(
        [jnp.where(lane < half, packed, 0.0), jnp.where(lane < half, 0.0, packed)], axis=0
    )


def statistics(low, high, up):
    return dot(
        jnp.concatenate([high, up], axis=1), jnp.concatenate([low, high], axis=1), ((0,), (0,))
    )


def forward_kernel(
    many, first, img, kern, upstream, pre_out, acc, sums, maps, ups, wts, held, map_sems, up_sems
):
    step = pl.program_id(0)
    last = pl.num_programs(0) - 1
    count, rows, width, cin = img.shape
    cout = kern.shape[3]
    inner = (rows - 2) * width

    def map_copy(image):
        return pltpu.make_async_copy(img.at[image], maps.at[image], map_sems.at[image])

    def up_copy(image):
        return pltpu.make_async_copy(upstream.at[image], ups.at[image], up_sems.at[image])

    def gather(group):
        grams, totals = [], []
        for index in range(many):
            up = ups[group * many + index, 1 : rows - 1].reshape(inner, cout)
            grams.append(statistics(held[index, 0], held[index, 1], up))
            totals.append(jnp.sum(up.astype(F32), axis=0, keepdims=True))
        acc[...] += functools.reduce(jnp.add, grams)
        sums[1:2] += functools.reduce(jnp.add, totals)

    def convolve():
        blank = jnp.zeros((1, width, cin), BF16)
        shift = sums[2:3]
        moved = []
        for index in range(many):
            image = step * many + index
            padded = jnp.concatenate([blank, maps[image], blank], axis=0)
            pre = paired_rows(padded, wts, cout)
            pre_out[image] = pre
            mid = pre[1 : rows - 1].reshape(inner, cout)
            if index == 0:
                mean = jnp.sum(mid, axis=0, keepdims=True) / inner
                shift = jnp.where(step == 0, mean, shift)
                sums[2:3] = shift
            delta = mid - shift
            high, low = split(delta)
            held[index, 0] = low
            held[index, 1] = high
            moved.append(jnp.sum(delta, axis=0, keepdims=True))
        sums[0:1] += functools.reduce(jnp.add, moved)

    @pl.when(step == 0)
    def _():
        for image in range(count):
            if image >= many:
                map_copy(image).start()
            up_copy(image).start()
        blank = jnp.zeros((cin, cout), BF16)
        blocks = [(kern[a, 0], kern[a, 1]) for a in range(3)]
        blocks += [
            (kern[a, 2] if a < 3 else blank, kern[a - 1, 0] if a > 0 else blank) for a in range(4)
        ]
        blocks += [(kern[a, 1], kern[a, 2]) for a in range(3)]
        for index, (one, two) in enumerate(blocks):
            wts[index * cin : (index + 1) * cin, :cout] = one
            wts[index * cin : (index + 1) * cin, cout:] = two
        acc[...] = jnp.zeros_like(acc)
        sums[...] = jnp.zeros_like(sums)
        convolve()

    @pl.when(step > 0)
    def _():
        for index in range(many):
            map_copy(step * many + index).wait()
            up_copy((step - 1) * many + index).wait()
        gather(step - 1)
        convolve()

    @pl.when(step == last)
    def _():
        for index in range(many):
            up_copy(step * many + index).wait()
        gather(step)


def sides(ahead, across):
    place = lax.axis_index("rows")
    even = is_even()
    outermost = jnp.where(even, place == 0, place == lax.axis_size("rows") - 1)
    across = jnp.where(outermost, jnp.zeros_like(across), across)
    return jnp.where(even, across, ahead), jnp.where(even, ahead, across)


def edge_choice(first, final):
    even = is_even()
    return jnp.where(even, final, first), jnp.where(even, first, final)


def fetch_kernel(many, images, kern, ahead, across, taps, maps, sems):
    last = images.shape[1] - 1
    even = is_even()
    pairs = (
        (images.at[:, pl.ds(jnp.where(even, last, 0), 1)], ahead),
        (images.at[:, pl.ds(jnp.where(even, 0, last), 1)], across),
        (kern, taps),
        (images.at[:many], maps.at[:many]),
    )
    copies = [
        pltpu.make_async_copy(source, target, sems.at[index])
        for index, (source, target) in enumerate(pairs)
    ]
    for copy in copies:
        copy.start()
    for copy in copies:
        copy.wait()


def edge_kernel(total, stage, ahead, across, pre, ups, kern, acc, sums, low, high, keep, send, stats):
    count, _, width, cin = ahead.shape
    cout = kern.shape[3]
    last = pre.shape[1] - 1
    top, bot = sides(ahead[...], across[...])
    pixels = count * width
    shape = (count, width, cout)
    edges = []
    for a, source, row, out in ((0, top, 0, low), (2, bot, last, high)):
        taps = jnp.concatenate([kern[a, c] for c in range(3)], axis=1)
        value = merged(dot(source.reshape(pixels, cin), taps), shape) + pre[:, row]
        out[:, 0] = value
        edges.append(value.reshape(pixels, cout))
    shift = sums[2:3]
    delta = jnp.concatenate(edges, axis=0) - shift
    up = jnp.concatenate(
        [ups[:, 0].reshape(pixels, cout), ups[:, last].reshape(pixels, cout)], axis=0
    )
    big, small = split(delta)
    gram = acc[...] + statistics(small, big, up)
    moved = sums[0:1] + jnp.sum(delta, axis=0, keepdims=True)
    up_sum = sums[1:2] + jnp.sum(up.astype(F32), axis=0, keepdims=True)
    mixed = gram[:cout, :cout]
    square = gram[:cout, cout:] + mixed + mixed.T
    cross = gram[cout:, :cout] + gram[cout:, cout:]
    raw = moved + total * shift
    square = square + column(moved) * shift + column(shift) * raw
    cross = cross + column(up_sum) * shift
    half = cout // 2
    stats[0:half] = pack(square)
    stats[half : 2 * half] = pack(cross)
    stats[2 * half :] = jnp.zeros_like(stats[2 * half :])
    stats[2 * half : 2 * half + 1] = raw
    stats[2 * half + 1 : 2 * half + 2] = up_sum
    part = keep.shape[0]
    upper = is_upper(stage)
    keep[...] = jnp.where(upper, stats[part:], stats[:part])
    send[...] = jnp.where(upper, stats[:part], stats[part:])


def spread(blocks):
    zero = jnp.zeros(blocks.shape[1:], F32)
    return jnp.concatenate(
        [
            jnp.concatenate([blocks[0], zero], axis=1),
            jnp.concatenate([zero, blocks[1]], axis=1),
        ],
        axis=0,
    )


def group_sum(value, half):
    cols = jnp.sum(value, axis=0, keepdims=True)
    lane = lax.broadcasted_iota(jnp.int32, cols.shape, 1)
    low = jnp.sum(jnp.where(lane < half, cols, 0.0), axis=1, keepdims=True)
    high = jnp.sum(jnp.where(lane < half, 0.0, cols), axis=1, keepdims=True)
    return jnp.where(lane < half, low, high)


def whitening(stats, colors, offset, total_pix, half):
    cout = 2 * half
    row_i = lax.broadcasted_iota(jnp.int32, (cout, cout), 0)
    col_i = lax.broadcasted_iota(jnp.int32, (cout, cout), 1)
    eye = jnp.where(row_i == col_i, 1.0, 0.0)
    block = jnp.where((row_i < half) == (col_i < half), 1.0, 0.0)
    square = unpack(stats[0:half])
    cross = unpack(stats[half : 2 * half])
    average = stats[2 * half : 2 * half + 1] / total_pix
    up_total = stats[2 * half + 1 : 2 * half + 2]
    sigma = square / total_pix - block * (column(average) * average) + EPSILON * eye
    cross = cross - block * (column(up_total) * average)
    grad = dot3(colors.T, cross)
    direction = grad + grad.T
    traces = group_sum(sigma * eye, half)
    normed = sigma / traces
    zero = jnp.zeros_like(normed)

    def stacked(value, tangent):
        return jnp.concatenate(
            [
                jnp.concatenate([value, tangent], axis=1),
                jnp.concatenate([zero, value], axis=1),
            ],
            axis=0,
        )

    source = stacked(normed, direction)
    value = 1.5 * eye - 0.5 * normed
    tangent = -0.5 * direction
    for _ in range(NS_ITERS - 1):
        first = jnp.concatenate([value, tangent], axis=1)
        both = dot3(first, jnp.concatenate([stacked(value, tangent), source], axis=1))
        squared = both[:, : 2 * cout]
        scaled = stacked(both[:, 2 * cout : 3 * cout], both[:, 3 * cout :])
        cubed = dot3(squared, scaled)
        value = 1.5 * value - 0.5 * cubed[:, :cout]
        tangent = 1.5 * tangent - 0.5 * cubed[:, cout:]
    inverse = 1.0 / jnp.sqrt(traces)
    whitener = value * inverse
    shared = group_sum(tangent * normed, half) + 0.5 * group_sum(direction * value, half)
    symmetric = (tangent - eye * shared) * (inverse / traces)
    mixed = dot3(colors, whitener)
    color_sum = dot3(cross, whitener.T)
    up_mean = jnp.broadcast_to(up_total / total_pix, (8, cout))
    bias = -dot3(up_mean, mixed)[0:1]
    return average, mixed, symmetric / total_pix, bias, offset, color_sum


def image_moments(image, pre, low, high, ups, img, ahead, across, sums):
    rows, width, cin = img.shape[1:]
    cout = pre.shape[3]
    pixels = rows * width
    top, bot = sides(ahead[image], across[image])
    padded = jnp.concatenate([top, img[image], bot], axis=0)
    turned = padded.reshape((rows + 2) * width, cin).T
    full = jnp.concatenate([low[image], pre[image, 1 : rows - 1], high[image]], axis=0)
    columns = []
    for value in (ups[image], (full - sums[2:3]).astype(BF16)):
        after, before = shifted(value.astype(F32))
        columns += [after.astype(BF16), value, before.astype(BF16)]
    right = jnp.concatenate(columns, axis=2).reshape(pixels, 6 * cout)
    left = jnp.concatenate([turned[:, a * width : a * width + pixels] for a in range(3)], axis=0)
    tiles = [turned[:, row * width : (row + 1) * width].astype(F32) for row in range(rows + 2)]
    middle = functools.reduce(jnp.add, tiles[2:rows])
    outer = ((0, 1), (1, rows), (rows, rows + 1))
    totals = jnp.concatenate([middle + tiles[one] + tiles[two] for one, two in outer], axis=0)
    return dot(left, right), totals


def moment_kernel(first, count, *refs):
    acc, maps = refs[-2:]
    found = [image_moments(first + index, *refs[:8]) for index in range(count)]
    if len(refs) == 12:
        found.append((refs[8][...], refs[9][...]))
    acc[...] = functools.reduce(jnp.add, [product for product, _ in found])
    maps[...] = functools.reduce(jnp.add, [totals for _, totals in found])


def whitening_kernel(
    total_pix,
    stage,
    own,
    other,
    colors,
    offset,
    sums,
    acc,
    maps,
    keep,
    send,
    grad_colors,
    mats,
    paint,
    paint_rows,
    stats,
):
    cout = 2 * colors.shape[1]
    half = cout // 2
    cin = acc.shape[0] // 3
    scaling = 1.0 / math.sqrt(total_pix)
    join_kernel(stage, own, other, stats)
    average, mixed, symmetric, bias, offs, color_sum = whitening(
        stats[...], spread(colors[...]), offset[...], total_pix, half
    )
    blank = jnp.zeros((cout, cout), BF16)
    mixed_h, mixed_l = split(mixed)
    color_h, color_l = split(mixed.T)
    sym_h, sym_l = split(symmetric)
    for target, blocks in (
        (mats, ((sym_h, sym_l), (mixed_h, mixed_l), (sym_h, blank))),
        (paint, ((color_h, color_l), (color_h, blank))),
    ):
        for index, (one, two) in enumerate(blocks):
            target[index * cout : (index + 1) * cout, :cout] = one
            target[index * cout : (index + 1) * cout, cout:] = two
    paint_rows[...] = jnp.zeros_like(paint_rows)
    paint_rows[0:1] = average
    paint_rows[1:2] = offs
    paint_rows[2:3] = bias
    scaled = color_sum * scaling
    grad_colors[0] = scaled[:half, :half]
    grad_colors[1] = pltpu.roll(scaled[half:], half, 1)[:, :half]

    moved = jnp.broadcast_to(sums[2:3] - average, (8, cout))
    constant = (bias + dot3(moved, symmetric)[0:1]) * scaling
    tall_h = jnp.concatenate([mixed_h, sym_h], axis=0)
    tall_l = jnp.concatenate([mixed_l, sym_l], axis=0)
    right = jnp.concatenate(
        [
            jnp.concatenate([tall_h, tall_l], axis=1),
            jnp.concatenate([tall_h, jnp.zeros_like(tall_l)], axis=1),
        ],
        axis=0,
    )
    lane = lax.broadcasted_iota(jnp.int32, (cin, maps.shape[1]), 1)
    seen = (lane < maps.shape[1] - 1, lane >= 0, lane > 0)
    parts = []
    for a in range(3):
        place = slice(a * cin, (a + 1) * cin)
        for c in range(3):
            pair = [acc[place, (k + c) * cout : (k + c + 1) * cout] for k in (0, 3)]
            left = jnp.concatenate(split(jnp.concatenate(pair, axis=1)), axis=1)
            result = dot(left, right)
            total = jnp.sum(jnp.where(seen[c], maps[place], 0.0), axis=1, keepdims=True)
            result = (result[:, :cout] + result[:, cout:]) * scaling + total * constant
            parts += [result[: cin // 2], result[cin // 2 :]]
    upper = is_upper(stage)
    for index in range(9):
        place = slice(index * cin // 2, (index + 1) * cin // 2)
        keep[place] = jnp.where(upper, parts[9 + index], parts[index])
        send[place] = jnp.where(upper, parts[index], parts[9 + index])


def centred_halves(image, pre, low, high, average):
    rows, width, cout = pre.shape[1:]
    full = jnp.concatenate([low[image], pre[image, 1 : rows - 1], high[image]], axis=0)
    return split(full.reshape(rows * width, cout) - average)


def edge_gradient_kernel(low, high, ups, mats, paint_rows, edge_ahead, edge_across):
    count, _, width, cout = low.shape
    last = ups.shape[1] - 1
    pre = jnp.concatenate([low[:, 0], high[:, 0]], axis=0).reshape(2 * count * width, cout)
    up = jnp.concatenate([ups[:, 0], ups[:, last]], axis=0).reshape(2 * count * width, cout)
    grad = pre_gradient(*split(pre - paint_rows[0:1]), up, mats, paint_rows)
    shaped = grad.reshape(2 * count, width, cout)
    edge_ahead[:, 0], edge_across[:, 0] = edge_choice(shaped[:count], shaped[count:])


def pre_gradient(big, small, up, mats, paint_rows):
    cout = up.shape[1]
    result = dot(jnp.concatenate([big, up, small], axis=1), mats[...])
    return (result[:, :cout] + result[:, cout:] + paint_rows[2:3]).astype(BF16)


def gradient_kernel(pre, low, high, ups, mats, paint_rows, pre_grad):
    image = pl.program_id(0)
    rows, width, cout = pre.shape[1:]
    big, small = centred_halves(image, pre, low, high, paint_rows[0:1])
    up = ups[image].reshape(rows * width, cout)
    grad = pre_gradient(big, small, up, mats, paint_rows)
    pre_grad[image] = grad.reshape(rows, width, cout)


def paint_kernel(pre, low, high, paint, paint_rows, colored):
    rows, width, cout = pre.shape[1:]
    halves = centred_halves(pl.program_id(0), pre, low, high, paint_rows[0:1])
    result = dot(jnp.concatenate(halves, axis=1), paint[...])
    result = result[:, :cout] + result[:, cout:] + paint_rows[1:2]
    colored[0] = result.astype(BF16).reshape(rows, width, cout)


def turn_kernel(kern, out):
    cout = kern.shape[3]
    for a in range(3):
        for c in range(3):
            tap = (a * 3 + c) * cout
            out[tap : tap + cout] = kern[a, c].T


def image_kernel(first, pre_grad, ahead, across, wts, *rest):
    out = rest[-1]
    image = pl.program_id(0) + first
    top, bot = sides(ahead[image], across[image])
    rows, width, cout = pre_grad.shape[1:]
    cin = wts.shape[1]
    exact = jnp.concatenate([top, pre_grad[image], bot], axis=0).astype(F32)
    after, before = shifted(exact)
    taps = [value.astype(BF16) for value in (after, exact, before)]
    wide = jnp.concatenate(
        [taps[c][2 - a : 2 - a + rows] for a in range(3) for c in range(3)], axis=2
    )
    result = dot(wide.reshape(rows * width, 9 * cout), wts[...])
    out[0] = result.astype(BF16).reshape(rows, width, cin)


def fold_kernel(stage, value, received, keep, send):
    upper = is_upper(stage)
    part = keep.shape[0]
    low = value[:part] + received[:part]
    high = value[part:] + received[part:]
    keep[...] = jnp.where(upper, high, low)
    send[...] = jnp.where(upper, low, high)


def join_kernel(stage, value, received, out):
    upper = is_upper(stage)
    part = value.shape[0]
    out[:part] = jnp.where(upper, received[...], value[...])
    out[part:] = jnp.where(upper, value[...], received[...])


def finish_kernel(stage, own, value, *rest):
    out, held, sems = rest[-3:]
    count, size = held.shape[:2]
    upper = is_upper(stage) if own else jnp.logical_not(is_upper(stage))
    start = jnp.where(upper, count * size, 0)
    copies = []
    for index in range(count):
        held[index] = value[index * size : (index + 1) * size].astype(F32)
        place = pl.ds(pl.multiple_of(start + index * size, size), size)
        copies.append(pltpu.make_async_copy(held.at[index], out.at[place], sems.at[index]))
        copies[-1].start()
    for copy in copies:
        copy.wait()


def image_spec(shape, place=lambda b: b):
    return pl.BlockSpec((1, *shape[1:]), lambda b: (place(b),) + (0,) * (len(shape) - 1))


def whole_spec(shape):
    return pl.BlockSpec(shape, lambda b: (0,) * len(shape))


def in_hbm(value):
    return pltpu.with_memory_space_constraint(value, pltpu.HBM)


def resident():
    return pl.BlockSpec(memory_space=pltpu.VMEM)


def forward(first, images, taps, upstream):
    count, rows, width, cin = images.shape
    cout = taps.shape[3]
    many = images_per_step(count)
    shapes = [
        ((count, rows, width, cout), F32),
        ((2 * cout, 2 * cout), F32),
        ((8, cout), F32),
        (images.shape, BF16),
        (upstream.shape, BF16),
    ]
    space = pl.BlockSpec(memory_space=pltpu.HBM)
    return pl.pallas_call(
        functools.partial(forward_kernel, many),
        grid=(count // many,),
        in_specs=[resident(), space, resident(), space],
        out_specs=[resident()] * len(shapes),
        out_shape=[jax.ShapeDtypeStruct(shape, dtype) for shape, dtype in shapes],
        scratch_shapes=[
            pltpu.VMEM((10 * cin, 2 * cout), BF16),
            pltpu.VMEM((many, 2, (rows - 2) * width, cout), BF16),
            pltpu.SemaphoreType.DMA((count,)),
            pltpu.SemaphoreType.DMA((count,)),
        ],
        input_output_aliases={0: 3},
        compiler_params=pltpu.CompilerParams(vmem_limit_bytes=28 * MIB),
        cost_estimate=pl.CostEstimate(
            flops=2 * count * rows * width * 9 * cin * cout,
            bytes_accessed=2 * images.size + 2 * upstream.size + 4 * upstream.size,
            transcendentals=0,
        ),
        name="forward_inner",
    )(first, in_hbm(images), taps, in_hbm(upstream))


def edges(stage, top, bot, pre, upstream, kernel, acc, sums):
    count, rows, width, cout = pre.shape
    part = (cout + 16) // 2
    edge = (count, 1, width, cout)
    shapes = [edge, edge, (part, cout), (part, cout)]
    return pl.pallas_call(
        functools.partial(edge_kernel, count * rows * width, stage),
        in_specs=[resident()] * 7,
        out_specs=[resident()] * 4,
        out_shape=[jax.ShapeDtypeStruct(shape, F32) for shape in shapes],
        scratch_shapes=[pltpu.VMEM((2 * part, cout), F32)],
        compiler_params=pltpu.CompilerParams(vmem_limit_bytes=12 * MIB),
        cost_estimate=pl.CostEstimate(
            flops=2 * 2 * count * width * 3 * top.shape[3] * cout,
            bytes_accessed=4 * top.size + 24 * count * width * cout,
            transcendentals=0,
        ),
        name="forward_edges",
    )(top, bot, pre, upstream, kernel, acc, sums)


def moments(first, count, pre, low, high, upstream, images, top, bot, sums, *sofar):
    width, cin = images.shape[2:]
    cout = upstream.shape[3]
    rows = images.shape[1]
    operands = (pre, low, high, upstream, images, top, bot, sums, *sofar)
    return pl.pallas_call(
        functools.partial(moment_kernel, first, count),
        in_specs=[resident()] * len(operands),
        out_specs=[resident()] * 2,
        out_shape=[
            jax.ShapeDtypeStruct((3 * cin, 6 * cout), F32),
            jax.ShapeDtypeStruct((3 * cin, width), F32),
        ],
        input_output_aliases={8: 0, 9: 1} if sofar else {},
        compiler_params=pltpu.CompilerParams(vmem_limit_bytes=28 * MIB),
        cost_estimate=pl.CostEstimate(
            flops=2 * count * rows * width * 18 * cin * cout, bytes_accessed=8 * MIB, transcendentals=0
        ),
        name="moments",
    )(*operands)


def whitened(total_pix, stage, own, other, colors, offset, sums, acc, maps):
    half = colors.shape[1]
    cout = 2 * half
    cin = acc.shape[0] // 3
    shapes = [
        ((9 * cin // 2, cout), F32),
        ((9 * cin // 2, cout), F32),
        ((2, half, half), F32),
        ((3 * cout, 2 * cout), BF16),
        ((2 * cout, 2 * cout), BF16),
        ((8, cout), F32),
    ]
    return pl.pallas_call(
        functools.partial(whitening_kernel, total_pix, stage),
        in_specs=[resident()] * 7,
        out_specs=[resident()] * len(shapes),
        out_shape=[jax.ShapeDtypeStruct(shape, dtype) for shape, dtype in shapes],
        scratch_shapes=[pltpu.VMEM((cout + 16, cout), F32)],
        compiler_params=pltpu.CompilerParams(vmem_limit_bytes=20 * MIB),
        cost_estimate=pl.CostEstimate(
            flops=2 * 9 * cin * 8 * cout * cout, bytes_accessed=8 * MIB, transcendentals=0
        ),
        name="whitening",
    )(own, other, colors, offset, sums, acc, maps)


def edge_gradients(low, high, upstream, mats, paint_rows):
    return pl.pallas_call(
        edge_gradient_kernel,
        in_specs=[resident()] * 5,
        out_specs=[resident()] * 2,
        out_shape=[jax.ShapeDtypeStruct(low.shape, BF16)] * 2,
        compiler_params=pltpu.CompilerParams(vmem_limit_bytes=16 * MIB),
        name="edge_gradients",
    )(low, high, upstream, mats, paint_rows)


def gradients(pre, low, high, upstream, mats, paint_rows):
    count, rows, width, cout = pre.shape
    return pl.pallas_call(
        gradient_kernel,
        grid=(count,),
        in_specs=[resident()] * 6,
        out_specs=resident(),
        out_shape=jax.ShapeDtypeStruct(pre.shape, BF16),
        compiler_params=pltpu.CompilerParams(vmem_limit_bytes=16 * MIB),
        cost_estimate=pl.CostEstimate(
            flops=2 * count * rows * width * 6 * cout * cout,
            bytes_accessed=8 * pre.size,
            transcendentals=0,
        ),
        name="pre_gradient",
    )(pre, low, high, upstream, mats, paint_rows)


def painted(pre, low, high, paint, paint_rows):
    count, rows, width, cout = pre.shape
    return pl.pallas_call(
        paint_kernel,
        grid=(count,),
        in_specs=[resident()] * 5,
        out_specs=image_spec(pre.shape),
        out_shape=jax.ShapeDtypeStruct(pre.shape, BF16),
        compiler_params=pltpu.CompilerParams(vmem_limit_bytes=16 * MIB),
        cost_estimate=pl.CostEstimate(
            flops=2 * count * rows * width * 4 * cout * cout,
            bytes_accessed=6 * pre.size,
            transcendentals=0,
        ),
        name="colored",
    )(pre, low, high, paint, paint_rows)


def turned_weights(kernel):
    cin, cout = kernel.shape[2:]
    return pl.pallas_call(
        turn_kernel,
        out_shape=jax.ShapeDtypeStruct((9 * cout, cin), BF16),
        compiler_params=pltpu.CompilerParams(vmem_limit_bytes=4 * MIB),
        name="turned_weights",
    )(kernel)


def image_gradient(first, count, pre_grad, top, bot, turned, out=None):
    images, rows, width, cout = pre_grad.shape
    cin = turned.shape[1]
    shape = (images, rows, width, cin)

    def place(b):
        return b + first

    operands = [pre_grad, top, bot, turned]
    in_specs = [resident()] * 4
    aliases = {}
    if out is not None:
        operands.append(out)
        in_specs.append(pl.BlockSpec(memory_space=pl.ANY))
        aliases = {4: 0}
    return pl.pallas_call(
        functools.partial(image_kernel, first),
        grid=(count,),
        in_specs=in_specs,
        out_specs=image_spec(shape, place),
        out_shape=jax.ShapeDtypeStruct(shape, BF16),
        input_output_aliases=aliases,
        compiler_params=pltpu.CompilerParams(vmem_limit_bytes=12 * MIB),
        cost_estimate=pl.CostEstimate(
            flops=2 * count * rows * width * 9 * cin * cout,
            bytes_accessed=2 * count * rows * width * (cin + cout),
            transcendentals=0,
        ),
        name="image_gradient",
    )(*operands)


def images_per_step(count):
    return 2 if count % 2 == 0 else 1


def fetched(images, kernel):
    count, rows, width, cin = images.shape
    edge = (count, 1, width, cin)
    space = pl.BlockSpec(memory_space=pltpu.HBM)
    return pl.pallas_call(
        functools.partial(fetch_kernel, images_per_step(count)),
        in_specs=[space, space],
        out_specs=[resident()] * 4,
        out_shape=[
            jax.ShapeDtypeStruct(shape, BF16) for shape in (edge, edge, kernel.shape, images.shape)
        ],
        scratch_shapes=[pltpu.SemaphoreType.DMA((4,))],
        compiler_params=pltpu.CompilerParams(vmem_limit_bytes=4 * MIB),
        name="edge_rows",
    )(in_hbm(images), in_hbm(kernel))


def small_call(kernel, name, *operands, out):
    return pl.pallas_call(
        kernel,
        in_specs=[resident()] * len(operands),
        out_specs=[resident()] * len(out),
        out_shape=out,
        compiler_params=pltpu.CompilerParams(vmem_limit_bytes=4 * MIB),
        name=name,
    )(*operands)


def fold(value, received, stage):
    half = jax.ShapeDtypeStruct((value.shape[0] // 2, value.shape[1]), value.dtype)
    return small_call(
        functools.partial(fold_kernel, stage), "fold", value, received, out=[half, half]
    )


def join(value, received, stage):
    whole = jax.ShapeDtypeStruct((value.shape[0] * 2, value.shape[1]), value.dtype)
    return small_call(
        functools.partial(join_kernel, stage), "join", value, received, out=[whole]
    )[0]


def finish(stage, value, out=None):
    part, lanes = value.shape
    operands, aliases = (value,), {}
    if out is not None:
        operands, aliases = (value, out), {1: 0}
    space = pl.BlockSpec(memory_space=pltpu.HBM)
    return pl.pallas_call(
        functools.partial(finish_kernel, stage, out is None),
        in_specs=[resident(), space][: len(operands)],
        out_specs=space,
        out_shape=jax.ShapeDtypeStruct((2 * part, lanes), F32),
        scratch_shapes=[
            pltpu.VMEM((2, part // 2, lanes), F32),
            pltpu.SemaphoreType.DMA((2,)),
        ],
        input_output_aliases=aliases,
        compiler_params=pltpu.CompilerParams(vmem_limit_bytes=4 * MIB),
        name="finish",
    )(*operands)


def halos(ahead, across):
    count, groups = lax.axis_size("rows"), lax.axis_size("dp")
    offset = 2 if groups % 4 == 0 else 1 if groups % 2 == 0 else 0
    pairs = ([], [])
    for group in range(groups):
        for place in range(count):
            for first in (0, 1):
                partner = place + 1 if place % 2 == first else place - 1
                inside = 0 <= partner < count
                other = (group, partner) if inside else (group ^ offset, place)
                pairs[first].append((group * count + place, other[0] * count + other[1]))
    return lax.ppermute(ahead, AXES, pairs[0]), lax.ppermute(across, AXES, pairs[1])


def exchange(value, devices, stage):
    pairs = [(i, i ^ (stage[1] if i & 1 else stage[0])) for i in range(devices)]
    return lax.ppermute(value, AXES, pairs)


def beside(send, devices, stage, task, operands):
    send, operands = lax.optimization_barrier((send, operands))
    received = exchange(send, devices, stage)
    result = task(*operands)
    return lax.optimization_barrier((received, result))


def body(images, kernel, colors, offset, upstream):
    count, rows, width, cin = images.shape
    cout = kernel.shape[3]
    devices = lax.axis_size("dp") * lax.axis_size("rows")
    total_pix = count * rows * width * devices
    plan = stages(devices)
    ahead, across, kernel, maps = fetched(images, kernel)
    top, bot = halos(ahead, across)
    pre, acc, sums, images, upstream = forward(maps, images, kernel, upstream)
    low, high, value, send = edges(plan[0], top, bot, pre, upstream, kernel, acc, sums)
    state = {"next": 0, "moments": (), "grad": None}

    def summed(send, stage, many):
        first = state["next"]
        many = min(many, count - first)
        if many == 0:
            return exchange(send, devices, stage)
        state["next"] = first + many
        operands = (pre, low, high, upstream, images, top, bot, sums, *state["moments"])
        received, state["moments"] = beside(
            send, devices, stage, functools.partial(moments, first, many), operands
        )
        return received

    value = value + exchange(send, devices, plan[0])
    for stage in plan[1:]:
        value = value + summed(value, stage, 2 if stage in plan[2:4] else 1)
    received = exchange(value, devices, plan[0])
    first = state["next"]
    if first < count:
        operands = (pre, low, high, upstream, images, top, bot, sums, *state["moments"])
        state["moments"] = moments(first, count - first, *operands)
    value, send, grad_colors, mats, paint, paint_rows = whitened(
        total_pix,
        plan[0],
        value,
        received,
        colors,
        offset.reshape(1, cout),
        sums,
        *state["moments"],
    )
    received, (edge_ahead, edge_across, turned) = beside(
        send,
        devices,
        plan[0],
        lambda kernel, *operands: (*edge_gradients(*operands), turned_weights(kernel)),
        (kernel, low, high, upstream, mats, paint_rows),
    )
    state["next"] = 0
    shares = [1, 1, 1, 1, 2]

    def transfer(send, stage):
        first = state["next"]
        if first >= count:
            return exchange(send, devices, stage)
        many = min(shares.pop(0), count - first) if shares else count - first
        state["next"] = first + many
        operands = (pre_grad, grad_top, grad_bot, turned)
        if state["grad"] is not None:
            operands = (*operands, state["grad"])
        received, state["grad"] = beside(
            send, devices, stage, functools.partial(image_gradient, first, many), operands
        )
        return received

    cuts = []
    for stage in plan[1:]:
        if value.shape[0] % 32 == 0 and value.shape[0] > 144:
            value, send = fold(value, received, stage)
            cuts.append(stage)
        else:
            value = send = value + received
        if stage == plan[1]:
            send, edge_ahead, edge_across = lax.optimization_barrier(
                (send, edge_ahead, edge_across)
            )
            grad_top, grad_bot = halos(edge_ahead, edge_across)
            received, pre_grad = beside(
                send, devices, stage, gradients, (pre, low, high, upstream, mats, paint_rows)
            )
        elif stage == plan[2]:
            received, colored = beside(
                send, devices, stage, painted, (pre, low, high, paint, paint_rows)
            )
        else:
            received = transfer(send, stage)
    value = (value + received).astype(BF16)
    for stage in reversed(cuts):
        value = join(value, transfer(value, stage), stage)
    received, result = beside(
        value, devices, plan[0], functools.partial(finish, plan[0]), (value,)
    )
    first = state["next"]
    if first < count:
        operands = (pre_grad, grad_top, grad_bot, turned, state["grad"])
        state["grad"] = image_gradient(first, count - first, *operands)
    grad_kernel = finish(plan[0], received, result).reshape(3, 3, cin, cout)
    return colored, state["grad"], grad_kernel, grad_colors


def solution(mesh):
    placed = (P("dp", "rows", None, None), P(), P(), P(), P("dp", "rows", None, None))
    return jax.shard_map(
        body,
        mesh=mesh,
        in_specs=placed,
        out_specs=(P("dp", "rows", None, None), P("dp", "rows", None, None), P(), P()),
        check_vma=False,
    )
```

```python
import functools
import math

import jax
import jax.numpy as jnp
from jax import lax
from jax.experimental import pallas as pl
from jax.experimental.pallas import tpu as pltpu
from jax.sharding import PartitionSpec as P

NS_ITERS = 5
EPSILON = 1e-05
F32 = jnp.float32
BF16 = jnp.bfloat16
MIB = 1024 * 1024
AXES = ("dp", "rows")


def device_index():
    return lax.axis_index("dp") * lax.axis_size("rows") + lax.axis_index("rows")


def is_even():
    return lax.axis_index("rows") % 2 == 0


def is_upper(stage):
    index = device_index()
    return index & jnp.where(index & 1 != 0, stage[1], stage[0]) != 0


def stages(devices):
    bits = [1 << i for i in range(devices.bit_length() - 1)]
    plan = [(bit, bit) for bit in bits]
    if len(bits) > 2:
        plan[1:3] = [(4, 2), (2, 4)]
    return plan


def split(value):
    high = value.astype(BF16)
    return high, (value - high.astype(F32)).astype(BF16)


def dot(left, right, dims=((1,), (0,))):
    return lax.dot_general(left, right, (dims, ((), ())), preferred_element_type=F32)


def dot3(left, right):
    lh, ll = split(left)
    rh, rl = split(right)
    return dot(
        jnp.concatenate([lh, lh, ll], axis=1), jnp.concatenate([rh, rl, rh], axis=0)
    )


def shifted(value):
    width = value.shape[1]
    col = lax.broadcasted_iota(jnp.int32, (1, *value.shape[1:]), 1)
    after = jnp.where(col == width - 1, 0.0, pltpu.roll(value, width - 1, 1))
    before = jnp.where(col == 0, 0.0, pltpu.roll(value, 1, 1))
    return after, before


def merged(prod, shape):
    cout = shape[2]
    _, left = shifted(prod[:, :cout].reshape(shape))
    right, _ = shifted(prod[:, 2 * cout :].reshape(shape))
    return prod[:, cout : 2 * cout].reshape(shape) + left + right


def paired_rows(padded, wts, cout):
    rows, width, cin = padded.shape[0] - 2, *padded.shape[1:]
    pairs = rows // 2
    parts = [
        jnp.concatenate([padded[2 * k + a : 2 * k + a + 1] for k in range(pairs)], axis=0)
        for a in range(4)
    ]
    wide = jnp.concatenate(parts, axis=2).reshape(pairs * width, 4 * cin)
    outer = dot(wide[:, : 3 * cin], wts[: 3 * cin])
    shared = dot(wide, wts[3 * cin : 7 * cin])
    inner = dot(wide[:, cin:], wts[7 * cin :])
    shape = (pairs, width, cout)

    def added_up(left, middle, right):
        _, before = shifted(left.reshape(shape))
        after, _ = shifted(right.reshape(shape))
        return middle.reshape(shape) + before + after

    first = added_up(outer[:, :cout], outer[:, cout:], shared[:, :cout])
    second = added_up(shared[:, cout:], inner[:, :cout], inner[:, cout:])
    ordered = [part[k : k + 1] for k in range(pairs) for part in (first, second)]
    return jnp.concatenate(ordered, axis=0)


def column(row):
    size = row.shape[1]
    return jnp.broadcast_to(row, (size, size)).T


def pack(full):
    half = full.shape[0] // 2
    lane = lax.broadcasted_iota(jnp.int32, (half, full.shape[1]), 1)
    return jnp.where(lane < half, full[:half], full[half:])


def unpack(packed):
    half = packed.shape[0]
    lane = lax.broadcasted_iota(jnp.int32, packed.shape, 1)
    return jnp.concatenate(
        [jnp.where(lane < half, packed, 0.0), jnp.where(lane < half, 0.0, packed)], axis=0
    )


def statistics(low, high, up):
    return dot(
        jnp.concatenate([high, up], axis=1), jnp.concatenate([low, high], axis=1), ((0,), (0,))
    )


def forward_kernel(
    many, first, img, kern, upstream, pre_out, acc, sums, maps, ups, wts, held, map_sems, up_sems
):
    step = pl.program_id(0)
    last = pl.num_programs(0) - 1
    count, rows, width, cin = img.shape
    cout = kern.shape[3]
    inner = (rows - 2) * width

    def map_copy(image):
        return pltpu.make_async_copy(img.at[image], maps.at[image], map_sems.at[image])

    def up_copy(image):
        return pltpu.make_async_copy(upstream.at[image], ups.at[image], up_sems.at[image])

    def gather(group):
        grams, totals = [], []
        for index in range(many):
            up = ups[group * many + index, 1 : rows - 1].reshape(inner, cout)
            grams.append(statistics(held[index, 0], held[index, 1], up))
            totals.append(jnp.sum(up.astype(F32), axis=0, keepdims=True))
        acc[...] += functools.reduce(jnp.add, grams)
        sums[1:2] += functools.reduce(jnp.add, totals)

    def convolve():
        blank = jnp.zeros((1, width, cin), BF16)
        shift = sums[2:3]
        moved = []
        for index in range(many):
            image = step * many + index
            padded = jnp.concatenate([blank, maps[image], blank], axis=0)
            pre = paired_rows(padded, wts, cout)
            pre_out[image] = pre
            mid = pre[1 : rows - 1].reshape(inner, cout)
            if index == 0:
                mean = jnp.sum(mid, axis=0, keepdims=True) / inner
                shift = jnp.where(step == 0, mean, shift)
                sums[2:3] = shift
            delta = mid - shift
            high, low = split(delta)
            held[index, 0] = low
            held[index, 1] = high
            moved.append(jnp.sum(delta, axis=0, keepdims=True))
        sums[0:1] += functools.reduce(jnp.add, moved)

    @pl.when(step == 0)
    def _():
        for image in range(count):
            if image >= many:
                map_copy(image).start()
            up_copy(image).start()
        blank = jnp.zeros((cin, cout), BF16)
        blocks = [(kern[a, 0], kern[a, 1]) for a in range(3)]
        blocks += [
            (kern[a, 2] if a < 3 else blank, kern[a - 1, 0] if a > 0 else blank) for a in range(4)
        ]
        blocks += [(kern[a, 1], kern[a, 2]) for a in range(3)]
        for index, (one, two) in enumerate(blocks):
            wts[index * cin : (index + 1) * cin, :cout] = one
            wts[index * cin : (index + 1) * cin, cout:] = two
        acc[...] = jnp.zeros_like(acc)
        sums[...] = jnp.zeros_like(sums)
        convolve()

    @pl.when(step > 0)
    def _():
        for index in range(many):
            map_copy(step * many + index).wait()
            up_copy((step - 1) * many + index).wait()
        gather(step - 1)
        convolve()

    @pl.when(step == last)
    def _():
        for index in range(many):
            up_copy(step * many + index).wait()
        gather(step)


def sides(ahead, across):
    place = lax.axis_index("rows")
    even = is_even()
    outermost = jnp.where(even, place == 0, place == lax.axis_size("rows") - 1)
    across = jnp.where(outermost, jnp.zeros_like(across), across)
    return jnp.where(even, across, ahead), jnp.where(even, ahead, across)


def edge_choice(first, final):
    even = is_even()
    return jnp.where(even, final, first), jnp.where(even, first, final)


def fetch_kernel(many, images, kern, ahead, across, taps, maps, sems):
    last = images.shape[1] - 1
    even = is_even()
    pairs = (
        (images.at[:, pl.ds(jnp.where(even, last, 0), 1)], ahead),
        (images.at[:, pl.ds(jnp.where(even, 0, last), 1)], across),
        (kern, taps),
        (images.at[:many], maps.at[:many]),
    )
    copies = [
        pltpu.make_async_copy(source, target, sems.at[index])
        for index, (source, target) in enumerate(pairs)
    ]
    for copy in copies:
        copy.start()
    for copy in copies:
        copy.wait()


def edge_kernel(total, stage, ahead, across, pre, ups, kern, acc, sums, low, high, keep, send, stats):
    count, _, width, cin = ahead.shape
    cout = kern.shape[3]
    last = pre.shape[1] - 1
    top, bot = sides(ahead[...], across[...])
    pixels = count * width
    shape = (count, width, cout)
    edges = []
    for a, source, row, out in ((0, top, 0, low), (2, bot, last, high)):
        taps = jnp.concatenate([kern[a, c] for c in range(3)], axis=1)
        value = merged(dot(source.reshape(pixels, cin), taps), shape) + pre[:, row]
        out[:, 0] = value
        edges.append(value.reshape(pixels, cout))
    shift = sums[2:3]
    delta = jnp.concatenate(edges, axis=0) - shift
    up = jnp.concatenate(
        [ups[:, 0].reshape(pixels, cout), ups[:, last].reshape(pixels, cout)], axis=0
    )
    big, small = split(delta)
    gram = acc[...] + statistics(small, big, up)
    moved = sums[0:1] + jnp.sum(delta, axis=0, keepdims=True)
    up_sum = sums[1:2] + jnp.sum(up.astype(F32), axis=0, keepdims=True)
    mixed = gram[:cout, :cout]
    square = gram[:cout, cout:] + mixed + mixed.T
    cross = gram[cout:, :cout] + gram[cout:, cout:]
    raw = moved + total * shift
    square = square + column(moved) * shift + column(shift) * raw
    cross = cross + column(up_sum) * shift
    half = cout // 2
    stats[0:half] = pack(square)
    stats[half : 2 * half] = pack(cross)
    stats[2 * half :] = jnp.zeros_like(stats[2 * half :])
    stats[2 * half : 2 * half + 1] = raw
    stats[2 * half + 1 : 2 * half + 2] = up_sum
    part = keep.shape[0]
    upper = is_upper(stage)
    keep[...] = jnp.where(upper, stats[part:], stats[:part])
    send[...] = jnp.where(upper, stats[:part], stats[part:])


def spread(blocks):
    zero = jnp.zeros(blocks.shape[1:], F32)
    return jnp.concatenate(
        [
            jnp.concatenate([blocks[0], zero], axis=1),
            jnp.concatenate([zero, blocks[1]], axis=1),
        ],
        axis=0,
    )


def group_sum(value, half):
    cols = jnp.sum(value, axis=0, keepdims=True)
    lane = lax.broadcasted_iota(jnp.int32, cols.shape, 1)
    low = jnp.sum(jnp.where(lane < half, cols, 0.0), axis=1, keepdims=True)
    high = jnp.sum(jnp.where(lane < half, 0.0, cols), axis=1, keepdims=True)
    return jnp.where(lane < half, low, high)


def whitening(stats, colors, offset, total_pix, half):
    cout = 2 * half
    row_i = lax.broadcasted_iota(jnp.int32, (cout, cout), 0)
    col_i = lax.broadcasted_iota(jnp.int32, (cout, cout), 1)
    eye = jnp.where(row_i == col_i, 1.0, 0.0)
    block = jnp.where((row_i < half) == (col_i < half), 1.0, 0.0)
    square = unpack(stats[0:half])
    cross = unpack(stats[half : 2 * half])
    average = stats[2 * half : 2 * half + 1] / total_pix
    up_total = stats[2 * half + 1 : 2 * half + 2]
    sigma = square / total_pix - block * (column(average) * average) + EPSILON * eye
    cross = cross - block * (column(up_total) * average)
    grad = dot3(colors.T, cross)
    direction = grad + grad.T
    traces = group_sum(sigma * eye, half)
    normed = sigma / traces
    zero = jnp.zeros_like(normed)

    def stacked(value, tangent):
        return jnp.concatenate(
            [
                jnp.concatenate([value, tangent], axis=1),
                jnp.concatenate([zero, value], axis=1),
            ],
            axis=0,
        )

    source = stacked(normed, direction)
    value = 1.5 * eye - 0.5 * normed
    tangent = -0.5 * direction
    for _ in range(NS_ITERS - 1):
        first = jnp.concatenate([value, tangent], axis=1)
        both = dot3(first, jnp.concatenate([stacked(value, tangent), source], axis=1))
        squared = both[:, : 2 * cout]
        scaled = stacked(both[:, 2 * cout : 3 * cout], both[:, 3 * cout :])
        cubed = dot3(squared, scaled)
        value = 1.5 * value - 0.5 * cubed[:, :cout]
        tangent = 1.5 * tangent - 0.5 * cubed[:, cout:]
    inverse = 1.0 / jnp.sqrt(traces)
    whitener = value * inverse
    shared = group_sum(tangent * normed, half) + 0.5 * group_sum(direction * value, half)
    symmetric = (tangent - eye * shared) * (inverse / traces)
    mixed = dot3(colors, whitener)
    color_sum = dot3(cross, whitener.T)
    up_mean = jnp.broadcast_to(up_total / total_pix, (8, cout))
    bias = -dot3(up_mean, mixed)[0:1]
    return average, mixed, symmetric / total_pix, bias, offset, color_sum


def image_moments(image, pre, low, high, ups, img, ahead, across, sums):
    rows, width, cin = img.shape[1:]
    cout = pre.shape[3]
    pixels = rows * width
    top, bot = sides(ahead[image], across[image])
    padded = jnp.concatenate([top, img[image], bot], axis=0)
    turned = padded.reshape((rows + 2) * width, cin).T
    full = jnp.concatenate([low[image], pre[image, 1 : rows - 1], high[image]], axis=0)
    columns = []
    for value in (ups[image], (full - sums[2:3]).astype(BF16)):
        after, before = shifted(value.astype(F32))
        columns += [after.astype(BF16), value, before.astype(BF16)]
    right = jnp.concatenate(columns, axis=2).reshape(pixels, 6 * cout)
    left = jnp.concatenate([turned[:, a * width : a * width + pixels] for a in range(3)], axis=0)
    tiles = [turned[:, row * width : (row + 1) * width].astype(F32) for row in range(rows + 2)]
    middle = functools.reduce(jnp.add, tiles[2:rows])
    outer = ((0, 1), (1, rows), (rows, rows + 1))
    totals = jnp.concatenate([middle + tiles[one] + tiles[two] for one, two in outer], axis=0)
    return dot(left, right), totals


def moment_kernel(first, count, *refs):
    acc, maps = refs[-2:]
    found = [image_moments(first + index, *refs[:8]) for index in range(count)]
    if len(refs) == 12:
        found.append((refs[8][...], refs[9][...]))
    acc[...] = functools.reduce(jnp.add, [product for product, _ in found])
    maps[...] = functools.reduce(jnp.add, [totals for _, totals in found])


def whitening_kernel(
    total_pix,
    stage,
    own,
    other,
    colors,
    offset,
    sums,
    acc,
    maps,
    keep,
    send,
    grad_colors,
    mats,
    paint,
    paint_rows,
    stats,
):
    cout = 2 * colors.shape[1]
    half = cout // 2
    cin = acc.shape[0] // 3
    scaling = 1.0 / math.sqrt(total_pix)
    join_kernel(stage, own, other, stats)
    average, mixed, symmetric, bias, offs, color_sum = whitening(
        stats[...], spread(colors[...]), offset[...], total_pix, half
    )
    blank = jnp.zeros((cout, cout), BF16)
    mixed_h, mixed_l = split(mixed)
    color_h, color_l = split(mixed.T)
    sym_h, sym_l = split(symmetric)
    for target, blocks in (
        (mats, ((sym_h, sym_l), (mixed_h, mixed_l), (sym_h, blank))),
        (paint, ((color_h, color_l), (color_h, blank))),
    ):
        for index, (one, two) in enumerate(blocks):
            target[index * cout : (index + 1) * cout, :cout] = one
            target[index * cout : (index + 1) * cout, cout:] = two
    paint_rows[...] = jnp.zeros_like(paint_rows)
    paint_rows[0:1] = average
    paint_rows[1:2] = offs
    paint_rows[2:3] = bias
    scaled = color_sum * scaling
    grad_colors[0] = scaled[:half, :half]
    grad_colors[1] = pltpu.roll(scaled[half:], half, 1)[:, :half]

    moved = jnp.broadcast_to(sums[2:3] - average, (8, cout))
    constant = (bias + dot3(moved, symmetric)[0:1]) * scaling
    tall_h = jnp.concatenate([mixed_h, sym_h], axis=0)
    tall_l = jnp.concatenate([mixed_l, sym_l], axis=0)
    right = jnp.concatenate(
        [
            jnp.concatenate([tall_h, tall_l], axis=1),
            jnp.concatenate([tall_h, jnp.zeros_like(tall_l)], axis=1),
        ],
        axis=0,
    )
    lane = lax.broadcasted_iota(jnp.int32, (cin, maps.shape[1]), 1)
    seen = (lane < maps.shape[1] - 1, lane >= 0, lane > 0)
    parts = []
    for a in range(3):
        place = slice(a * cin, (a + 1) * cin)
        for c in range(3):
            pair = [acc[place, (k + c) * cout : (k + c + 1) * cout] for k in (0, 3)]
            left = jnp.concatenate(split(jnp.concatenate(pair, axis=1)), axis=1)
            result = dot(left, right)
            total = jnp.sum(jnp.where(seen[c], maps[place], 0.0), axis=1, keepdims=True)
            result = (result[:, :cout] + result[:, cout:]) * scaling + total * constant
            parts += [result[: cin // 2], result[cin // 2 :]]
    upper = is_upper(stage)
    for index in range(9):
        place = slice(index * cin // 2, (index + 1) * cin // 2)
        keep[place] = jnp.where(upper, parts[9 + index], parts[index])
        send[place] = jnp.where(upper, parts[index], parts[9 + index])


def centred_halves(image, pre, low, high, average):
    rows, width, cout = pre.shape[1:]
    full = jnp.concatenate([low[image], pre[image, 1 : rows - 1], high[image]], axis=0)
    return split(full.reshape(rows * width, cout) - average)


def edge_gradient_kernel(low, high, ups, mats, paint_rows, edge_ahead, edge_across):
    count, _, width, cout = low.shape
    last = ups.shape[1] - 1
    pre = jnp.concatenate([low[:, 0], high[:, 0]], axis=0).reshape(2 * count * width, cout)
    up = jnp.concatenate([ups[:, 0], ups[:, last]], axis=0).reshape(2 * count * width, cout)
    grad = pre_gradient(*split(pre - paint_rows[0:1]), up, mats, paint_rows)
    shaped = grad.reshape(2 * count, width, cout)
    edge_ahead[:, 0], edge_across[:, 0] = edge_choice(shaped[:count], shaped[count:])


def pre_gradient(big, small, up, mats, paint_rows):
    cout = up.shape[1]
    result = dot(jnp.concatenate([big, up, small], axis=1), mats[...])
    return (result[:, :cout] + result[:, cout:] + paint_rows[2:3]).astype(BF16)


def gradient_kernel(pre, low, high, ups, mats, paint_rows, pre_grad):
    image = pl.program_id(0)
    rows, width, cout = pre.shape[1:]
    big, small = centred_halves(image, pre, low, high, paint_rows[0:1])
    up = ups[image].reshape(rows * width, cout)
    grad = pre_gradient(big, small, up, mats, paint_rows)
    pre_grad[image] = grad.reshape(rows, width, cout)


def paint_kernel(pre, low, high, paint, paint_rows, colored):
    rows, width, cout = pre.shape[1:]
    halves = centred_halves(pl.program_id(0), pre, low, high, paint_rows[0:1])
    result = dot(jnp.concatenate(halves, axis=1), paint[...])
    result = result[:, :cout] + result[:, cout:] + paint_rows[1:2]
    colored[0] = result.astype(BF16).reshape(rows, width, cout)


def turn_kernel(kern, out):
    cout = kern.shape[3]
    for a in range(3):
        for c in range(3):
            tap = (a * 3 + c) * cout
            out[tap : tap + cout] = kern[a, c].T


def image_kernel(first, pre_grad, ahead, across, wts, *rest):
    out = rest[-1]
    image = pl.program_id(0) + first
    top, bot = sides(ahead[image], across[image])
    rows, width, cout = pre_grad.shape[1:]
    cin = wts.shape[1]
    exact = jnp.concatenate([top, pre_grad[image], bot], axis=0).astype(F32)
    after, before = shifted(exact)
    taps = [value.astype(BF16) for value in (after, exact, before)]
    wide = jnp.concatenate(
        [taps[c][2 - a : 2 - a + rows] for a in range(3) for c in range(3)], axis=2
    )
    result = dot(wide.reshape(rows * width, 9 * cout), wts[...])
    out[0] = result.astype(BF16).reshape(rows, width, cin)


def fold_kernel(stage, value, received, keep, send):
    upper = is_upper(stage)
    part = keep.shape[0]
    low = value[:part] + received[:part]
    high = value[part:] + received[part:]
    keep[...] = jnp.where(upper, high, low)
    send[...] = jnp.where(upper, low, high)


def join_kernel(stage, value, received, out):
    upper = is_upper(stage)
    part = value.shape[0]
    out[:part] = jnp.where(upper, received[...], value[...])
    out[part:] = jnp.where(upper, value[...], received[...])


def finish_kernel(stage, own, value, *rest):
    out, held, sems = rest[-3:]
    count, size = held.shape[:2]
    upper = is_upper(stage) if own else jnp.logical_not(is_upper(stage))
    start = jnp.where(upper, count * size, 0)
    copies = []
    for index in range(count):
        held[index] = value[index * size : (index + 1) * size].astype(F32)
        place = pl.ds(pl.multiple_of(start + index * size, size), size)
        copies.append(pltpu.make_async_copy(held.at[index], out.at[place], sems.at[index]))
        copies[-1].start()
    for copy in copies:
        copy.wait()


def image_spec(shape, place=lambda b: b):
    return pl.BlockSpec((1, *shape[1:]), lambda b: (place(b),) + (0,) * (len(shape) - 1))


def whole_spec(shape):
    return pl.BlockSpec(shape, lambda b: (0,) * len(shape))


def in_hbm(value):
    return pltpu.with_memory_space_constraint(value, pltpu.HBM)


def resident():
    return pl.BlockSpec(memory_space=pltpu.VMEM)


def forward(first, images, taps, upstream):
    count, rows, width, cin = images.shape
    cout = taps.shape[3]
    many = images_per_step(count)
    shapes = [
        ((count, rows, width, cout), F32),
        ((2 * cout, 2 * cout), F32),
        ((8, cout), F32),
        (images.shape, BF16),
        (upstream.shape, BF16),
    ]
    space = pl.BlockSpec(memory_space=pltpu.HBM)
    return pl.pallas_call(
        functools.partial(forward_kernel, many),
        grid=(count // many,),
        in_specs=[resident(), space, resident(), space],
        out_specs=[resident()] * len(shapes),
        out_shape=[jax.ShapeDtypeStruct(shape, dtype) for shape, dtype in shapes],
        scratch_shapes=[
            pltpu.VMEM((10 * cin, 2 * cout), BF16),
            pltpu.VMEM((many, 2, (rows - 2) * width, cout), BF16),
            pltpu.SemaphoreType.DMA((count,)),
            pltpu.SemaphoreType.DMA((count,)),
        ],
        input_output_aliases={0: 3},
        compiler_params=pltpu.CompilerParams(vmem_limit_bytes=36 * MIB),
        cost_estimate=pl.CostEstimate(
            flops=2 * count * rows * width * 9 * cin * cout,
            bytes_accessed=2 * images.size + 2 * upstream.size + 4 * upstream.size,
            transcendentals=0,
        ),
        name="forward_inner",
    )(first, in_hbm(images), taps, in_hbm(upstream))


def edges(stage, top, bot, pre, upstream, kernel, acc, sums):
    count, rows, width, cout = pre.shape
    part = (cout + 16) // 2
    edge = (count, 1, width, cout)
    shapes = [edge, edge, (part, cout), (part, cout)]
    return pl.pallas_call(
        functools.partial(edge_kernel, count * rows * width, stage),
        in_specs=[resident()] * 7,
        out_specs=[resident()] * 4,
        out_shape=[jax.ShapeDtypeStruct(shape, F32) for shape in shapes],
        scratch_shapes=[pltpu.VMEM((2 * part, cout), F32)],
        compiler_params=pltpu.CompilerParams(vmem_limit_bytes=12 * MIB),
        cost_estimate=pl.CostEstimate(
            flops=2 * 2 * count * width * 3 * top.shape[3] * cout,
            bytes_accessed=4 * top.size + 24 * count * width * cout,
            transcendentals=0,
        ),
        name="forward_edges",
    )(top, bot, pre, upstream, kernel, acc, sums)


def moments(first, count, pre, low, high, upstream, images, top, bot, sums, *sofar):
    width, cin = images.shape[2:]
    cout = upstream.shape[3]
    rows = images.shape[1]
    operands = (pre, low, high, upstream, images, top, bot, sums, *sofar)
    return pl.pallas_call(
        functools.partial(moment_kernel, first, count),
        in_specs=[resident()] * len(operands),
        out_specs=[resident()] * 2,
        out_shape=[
            jax.ShapeDtypeStruct((3 * cin, 6 * cout), F32),
            jax.ShapeDtypeStruct((3 * cin, width), F32),
        ],
        input_output_aliases={8: 0, 9: 1} if sofar else {},
        compiler_params=pltpu.CompilerParams(vmem_limit_bytes=28 * MIB),
        cost_estimate=pl.CostEstimate(
            flops=2 * count * rows * width * 18 * cin * cout, bytes_accessed=8 * MIB, transcendentals=0
        ),
        name="moments",
    )(*operands)


def whitened(total_pix, stage, own, other, colors, offset, sums, acc, maps):
    half = colors.shape[1]
    cout = 2 * half
    cin = acc.shape[0] // 3
    shapes = [
        ((9 * cin // 2, cout), F32),
        ((9 * cin // 2, cout), F32),
        ((2, half, half), F32),
        ((3 * cout, 2 * cout), BF16),
        ((2 * cout, 2 * cout), BF16),
        ((8, cout), F32),
    ]
    return pl.pallas_call(
        functools.partial(whitening_kernel, total_pix, stage),
        in_specs=[resident()] * 7,
        out_specs=[resident()] * len(shapes),
        out_shape=[jax.ShapeDtypeStruct(shape, dtype) for shape, dtype in shapes],
        scratch_shapes=[pltpu.VMEM((cout + 16, cout), F32)],
        compiler_params=pltpu.CompilerParams(vmem_limit_bytes=20 * MIB),
        cost_estimate=pl.CostEstimate(
            flops=2 * 9 * cin * 8 * cout * cout, bytes_accessed=8 * MIB, transcendentals=0
        ),
        name="whitening",
    )(own, other, colors, offset, sums, acc, maps)


def edge_gradients(low, high, upstream, mats, paint_rows):
    return pl.pallas_call(
        edge_gradient_kernel,
        in_specs=[resident()] * 5,
        out_specs=[resident()] * 2,
        out_shape=[jax.ShapeDtypeStruct(low.shape, BF16)] * 2,
        compiler_params=pltpu.CompilerParams(vmem_limit_bytes=16 * MIB),
        name="edge_gradients",
    )(low, high, upstream, mats, paint_rows)


def gradients(pre, low, high, upstream, mats, paint_rows):
    count, rows, width, cout = pre.shape
    return pl.pallas_call(
        gradient_kernel,
        grid=(count,),
        in_specs=[resident()] * 6,
        out_specs=resident(),
        out_shape=jax.ShapeDtypeStruct(pre.shape, BF16),
        compiler_params=pltpu.CompilerParams(vmem_limit_bytes=16 * MIB),
        cost_estimate=pl.CostEstimate(
            flops=2 * count * rows * width * 6 * cout * cout,
            bytes_accessed=8 * pre.size,
            transcendentals=0,
        ),
        name="pre_gradient",
    )(pre, low, high, upstream, mats, paint_rows)


def painted(pre, low, high, paint, paint_rows):
    count, rows, width, cout = pre.shape
    return pl.pallas_call(
        paint_kernel,
        grid=(count,),
        in_specs=[resident()] * 5,
        out_specs=image_spec(pre.shape),
        out_shape=jax.ShapeDtypeStruct(pre.shape, BF16),
        compiler_params=pltpu.CompilerParams(vmem_limit_bytes=16 * MIB),
        cost_estimate=pl.CostEstimate(
            flops=2 * count * rows * width * 4 * cout * cout,
            bytes_accessed=6 * pre.size,
            transcendentals=0,
        ),
        name="colored",
    )(pre, low, high, paint, paint_rows)


def turned_weights(kernel):
    cin, cout = kernel.shape[2:]
    return pl.pallas_call(
        turn_kernel,
        out_shape=jax.ShapeDtypeStruct((9 * cout, cin), BF16),
        compiler_params=pltpu.CompilerParams(vmem_limit_bytes=4 * MIB),
        name="turned_weights",
    )(kernel)


def image_gradient(first, count, pre_grad, top, bot, turned, out=None):
    images, rows, width, cout = pre_grad.shape
    cin = turned.shape[1]
    shape = (images, rows, width, cin)

    def place(b):
        return b + first

    operands = [pre_grad, top, bot, turned]
    in_specs = [resident()] * 4
    aliases = {}
    if out is not None:
        operands.append(out)
        in_specs.append(pl.BlockSpec(memory_space=pl.ANY))
        aliases = {4: 0}
    return pl.pallas_call(
        functools.partial(image_kernel, first),
        grid=(count,),
        in_specs=in_specs,
        out_specs=image_spec(shape, place),
        out_shape=jax.ShapeDtypeStruct(shape, BF16),
        input_output_aliases=aliases,
        compiler_params=pltpu.CompilerParams(vmem_limit_bytes=12 * MIB),
        cost_estimate=pl.CostEstimate(
            flops=2 * count * rows * width * 9 * cin * cout,
            bytes_accessed=2 * count * rows * width * (cin + cout),
            transcendentals=0,
        ),
        name="image_gradient",
    )(*operands)


def images_per_step(count):
    return next(many for many in (3, 2, 1) if count % many == 0)


def fetched(images, kernel):
    count, rows, width, cin = images.shape
    edge = (count, 1, width, cin)
    space = pl.BlockSpec(memory_space=pltpu.HBM)
    return pl.pallas_call(
        functools.partial(fetch_kernel, images_per_step(count)),
        in_specs=[space, space],
        out_specs=[resident()] * 4,
        out_shape=[
            jax.ShapeDtypeStruct(shape, BF16) for shape in (edge, edge, kernel.shape, images.shape)
        ],
        scratch_shapes=[pltpu.SemaphoreType.DMA((4,))],
        compiler_params=pltpu.CompilerParams(vmem_limit_bytes=4 * MIB),
        name="edge_rows",
    )(in_hbm(images), in_hbm(kernel))


def small_call(kernel, name, *operands, out):
    return pl.pallas_call(
        kernel,
        in_specs=[resident()] * len(operands),
        out_specs=[resident()] * len(out),
        out_shape=out,
        compiler_params=pltpu.CompilerParams(vmem_limit_bytes=4 * MIB),
        name=name,
    )(*operands)


def fold(value, received, stage):
    half = jax.ShapeDtypeStruct((value.shape[0] // 2, value.shape[1]), value.dtype)
    return small_call(
        functools.partial(fold_kernel, stage), "fold", value, received, out=[half, half]
    )


def join(value, received, stage):
    whole = jax.ShapeDtypeStruct((value.shape[0] * 2, value.shape[1]), value.dtype)
    return small_call(
        functools.partial(join_kernel, stage), "join", value, received, out=[whole]
    )[0]


def finish(stage, value, out=None):
    part, lanes = value.shape
    operands, aliases = (value,), {}
    if out is not None:
        operands, aliases = (value, out), {1: 0}
    space = pl.BlockSpec(memory_space=pltpu.HBM)
    return pl.pallas_call(
        functools.partial(finish_kernel, stage, out is None),
        in_specs=[resident(), space][: len(operands)],
        out_specs=space,
        out_shape=jax.ShapeDtypeStruct((2 * part, lanes), F32),
        scratch_shapes=[
            pltpu.VMEM((2, part // 2, lanes), F32),
            pltpu.SemaphoreType.DMA((2,)),
        ],
        input_output_aliases=aliases,
        compiler_params=pltpu.CompilerParams(vmem_limit_bytes=4 * MIB),
        name="finish",
    )(*operands)


def halos(ahead, across):
    count, groups = lax.axis_size("rows"), lax.axis_size("dp")
    offset = 2 if groups % 4 == 0 else 1 if groups % 2 == 0 else 0
    pairs = ([], [])
    for group in range(groups):
        for place in range(count):
            for first in (0, 1):
                partner = place + 1 if place % 2 == first else place - 1
                inside = 0 <= partner < count
                other = (group, partner) if inside else (group ^ offset, place)
                pairs[first].append((group * count + place, other[0] * count + other[1]))
    return lax.ppermute(ahead, AXES, pairs[0]), lax.ppermute(across, AXES, pairs[1])


def exchange(value, devices, stage):
    pairs = [(i, i ^ (stage[1] if i & 1 else stage[0])) for i in range(devices)]
    return lax.ppermute(value, AXES, pairs)


def beside(send, devices, stage, task, operands):
    send, operands = lax.optimization_barrier((send, operands))
    received = exchange(send, devices, stage)
    result = task(*operands)
    return lax.optimization_barrier((received, result))


def body(images, kernel, colors, offset, upstream):
    count, rows, width, cin = images.shape
    cout = kernel.shape[3]
    devices = lax.axis_size("dp") * lax.axis_size("rows")
    total_pix = count * rows * width * devices
    plan = stages(devices)
    ahead, across, kernel, maps = fetched(images, kernel)
    top, bot = halos(ahead, across)
    pre, acc, sums, images, upstream = forward(maps, images, kernel, upstream)
    low, high, value, send = edges(plan[0], top, bot, pre, upstream, kernel, acc, sums)
    state = {"next": 0, "moments": (), "grad": None}

    def summed(send, stage, many):
        first = state["next"]
        many = min(many, count - first)
        if many == 0:
            return exchange(send, devices, stage)
        state["next"] = first + many
        operands = (pre, low, high, upstream, images, top, bot, sums, *state["moments"])
        received, state["moments"] = beside(
            send, devices, stage, functools.partial(moments, first, many), operands
        )
        return received

    value = value + exchange(send, devices, plan[0])
    for stage in plan[1:]:
        value = value + summed(value, stage, 2 if stage in plan[1:3] else 1)
    received = exchange(value, devices, plan[0])
    first = state["next"]
    if first < count:
        operands = (pre, low, high, upstream, images, top, bot, sums, *state["moments"])
        state["moments"] = moments(first, count - first, *operands)
    value, send, grad_colors, mats, paint, paint_rows = whitened(
        total_pix,
        plan[0],
        value,
        received,
        colors,
        offset.reshape(1, cout),
        sums,
        *state["moments"],
    )
    received, (edge_ahead, edge_across, turned) = beside(
        send,
        devices,
        plan[0],
        lambda kernel, *operands: (*edge_gradients(*operands), turned_weights(kernel)),
        (kernel, low, high, upstream, mats, paint_rows),
    )
    state["next"] = 0
    shares = [1, 1, 1, 1, 2]

    def transfer(send, stage):
        first = state["next"]
        if first >= count:
            return exchange(send, devices, stage)
        many = min(shares.pop(0), count - first) if shares else count - first
        state["next"] = first + many
        operands = (pre_grad, grad_top, grad_bot, turned)
        if state["grad"] is not None:
            operands = (*operands, state["grad"])
        received, state["grad"] = beside(
            send, devices, stage, functools.partial(image_gradient, first, many), operands
        )
        return received

    cuts = []
    for stage in plan[1:]:
        if value.shape[0] % 32 == 0 and value.shape[0] > 144:
            value, send = fold(value, received, stage)
            cuts.append(stage)
        else:
            value = send = value + received
        if stage == plan[1]:
            send, edge_ahead, edge_across = lax.optimization_barrier(
                (send, edge_ahead, edge_across)
            )
            grad_top, grad_bot = halos(edge_ahead, edge_across)
            received, pre_grad = beside(
                send, devices, stage, gradients, (pre, low, high, upstream, mats, paint_rows)
            )
        elif stage == plan[2]:
            received, colored = beside(
                send, devices, stage, painted, (pre, low, high, paint, paint_rows)
            )
        else:
            received = transfer(send, stage)
    value = (value + received).astype(BF16)
    for stage in reversed(cuts):
        value = join(value, transfer(value, stage), stage)
    received, result = beside(
        value, devices, plan[0], functools.partial(finish, plan[0]), (value,)
    )
    first = state["next"]
    if first < count:
        operands = (pre_grad, grad_top, grad_bot, turned, state["grad"])
        state["grad"] = image_gradient(first, count - first, *operands)
    grad_kernel = finish(plan[0], received, result).reshape(3, 3, cin, cout)
    return colored, state["grad"], grad_kernel, grad_colors


def solution(mesh):
    placed = (P("dp", "rows", None, None), P(), P(), P(), P("dp", "rows", None, None))
    return jax.shard_map(
        body,
        mesh=mesh,
        in_specs=placed,
        out_specs=(P("dp", "rows", None, None), P("dp", "rows", None, None), P(), P()),
        check_vma=False,
    )
```

```python
import functools
import math

import jax
import jax.numpy as jnp
from jax import lax
from jax.experimental import pallas as pl
from jax.experimental.pallas import tpu as pltpu
from jax.sharding import PartitionSpec as P

NS_ITERS = 5
EPSILON = 1e-05
F32 = jnp.float32
BF16 = jnp.bfloat16
MIB = 1024 * 1024
AXES = ("dp", "rows")


def device_index():
    return lax.axis_index("dp") * lax.axis_size("rows") + lax.axis_index("rows")


def is_even():
    return lax.axis_index("rows") % 2 == 0


def is_upper(stage):
    index = device_index()
    return index & jnp.where(index & 1 != 0, stage[1], stage[0]) != 0


def stages(devices):
    bits = [1 << i for i in range(devices.bit_length() - 1)]
    plan = [(bit, bit) for bit in bits]
    if len(bits) > 2:
        plan[1:3] = [(4, 2), (2, 4)]
    return plan


def split(value):
    high = value.astype(BF16)
    return high, (value - high.astype(F32)).astype(BF16)


def dot(left, right, dims=((1,), (0,))):
    return lax.dot_general(left, right, (dims, ((), ())), preferred_element_type=F32)


def dot3(left, right):
    lh, ll = split(left)
    rh, rl = split(right)
    return dot(
        jnp.concatenate([lh, lh, ll], axis=1), jnp.concatenate([rh, rl, rh], axis=0)
    )


def shifted(value):
    width = value.shape[1]
    col = lax.broadcasted_iota(jnp.int32, (1, *value.shape[1:]), 1)
    after = jnp.where(col == width - 1, 0.0, pltpu.roll(value, width - 1, 1))
    before = jnp.where(col == 0, 0.0, pltpu.roll(value, 1, 1))
    return after, before


def merged(prod, shape):
    cout = shape[2]
    _, left = shifted(prod[:, :cout].reshape(shape))
    right, _ = shifted(prod[:, 2 * cout :].reshape(shape))
    return prod[:, cout : 2 * cout].reshape(shape) + left + right


def paired_rows(padded, wts, cout):
    rows, width, cin = padded.shape[0] - 2, *padded.shape[1:]
    pairs = rows // 2
    parts = [
        jnp.concatenate([padded[2 * k + a : 2 * k + a + 1] for k in range(pairs)], axis=0)
        for a in range(4)
    ]
    wide = jnp.concatenate(parts, axis=2).reshape(pairs * width, 4 * cin)
    outer = dot(wide[:, : 3 * cin], wts[: 3 * cin])
    shared = dot(wide, wts[3 * cin : 7 * cin])
    inner = dot(wide[:, cin:], wts[7 * cin :])
    shape = (pairs, width, cout)

    def added_up(left, middle, right):
        _, before = shifted(left.reshape(shape))
        after, _ = shifted(right.reshape(shape))
        return middle.reshape(shape) + before + after

    first = added_up(outer[:, :cout], outer[:, cout:], shared[:, :cout])
    second = added_up(shared[:, cout:], inner[:, :cout], inner[:, cout:])
    ordered = [part[k : k + 1] for k in range(pairs) for part in (first, second)]
    return jnp.concatenate(ordered, axis=0)


def column(row):
    size = row.shape[1]
    return jnp.broadcast_to(row, (size, size)).T


def pack(full):
    half = full.shape[0] // 2
    lane = lax.broadcasted_iota(jnp.int32, (half, full.shape[1]), 1)
    return jnp.where(lane < half, full[:half], full[half:])


def unpack(packed):
    half = packed.shape[0]
    lane = lax.broadcasted_iota(jnp.int32, packed.shape, 1)
    return jnp.concatenate(
        [jnp.where(lane < half, packed, 0.0), jnp.where(lane < half, 0.0, packed)], axis=0
    )


def statistics(low, high, up):
    return dot(
        jnp.concatenate([high, up], axis=1), jnp.concatenate([low, high], axis=1), ((0,), (0,))
    )


def forward_kernel(
    many, first, img, kern, upstream, pre_out, acc, sums, maps, ups, wts, held, map_sems, up_sems
):
    step = pl.program_id(0)
    last = pl.num_programs(0) - 1
    count, rows, width, cin = img.shape
    cout = kern.shape[3]
    inner = (rows - 2) * width

    def map_copy(image):
        return pltpu.make_async_copy(img.at[image], maps.at[image], map_sems.at[image])

    def up_copy(image):
        return pltpu.make_async_copy(upstream.at[image], ups.at[image], up_sems.at[image])

    def gather(group):
        grams, totals = [], []
        for index in range(many):
            up = ups[group * many + index, 1 : rows - 1].reshape(inner, cout)
            grams.append(statistics(held[index, 0], held[index, 1], up))
            totals.append(jnp.sum(up.astype(F32), axis=0, keepdims=True))
        acc[...] += functools.reduce(jnp.add, grams)
        sums[1:2] += functools.reduce(jnp.add, totals)

    def convolve(initial):
        blank = jnp.zeros((1, width, cin), BF16)
        shift = sums[2:3]
        moved = []
        for index in range(many):
            image = step * many + index
            padded = jnp.concatenate([blank, maps[image], blank], axis=0)
            pre = paired_rows(padded, wts, cout)
            pre_out[image] = pre
            mid = pre[1 : rows - 1].reshape(inner, cout)
            if initial and index == 0:
                shift = jnp.sum(mid, axis=0, keepdims=True) / inner
                sums[2:3] = shift
            delta = mid - shift
            high, low = split(delta)
            held[index, 0] = low
            held[index, 1] = high
            moved.append(jnp.sum(delta, axis=0, keepdims=True))
        sums[0:1] += functools.reduce(jnp.add, moved)

    @pl.when(step == 0)
    def _():
        for image in range(count):
            if image >= many:
                map_copy(image).start()
            up_copy(image).start()
        blank = jnp.zeros((cin, cout), BF16)
        blocks = [(kern[a, 0], kern[a, 1]) for a in range(3)]
        blocks += [
            (kern[a, 2] if a < 3 else blank, kern[a - 1, 0] if a > 0 else blank) for a in range(4)
        ]
        blocks += [(kern[a, 1], kern[a, 2]) for a in range(3)]
        for index, (one, two) in enumerate(blocks):
            wts[index * cin : (index + 1) * cin, :cout] = one
            wts[index * cin : (index + 1) * cin, cout:] = two
        acc[...] = jnp.zeros_like(acc)
        sums[...] = jnp.zeros_like(sums)
        convolve(True)

    @pl.when(step > 0)
    def _():
        for index in range(many):
            map_copy(step * many + index).wait()
            up_copy((step - 1) * many + index).wait()
        gather(step - 1)
        convolve(False)

    @pl.when(step == last)
    def _():
        for index in range(many):
            up_copy(step * many + index).wait()
        gather(step)


def sides(ahead, across):
    place = lax.axis_index("rows")
    even = is_even()
    outermost = jnp.where(even, place == 0, place == lax.axis_size("rows") - 1)
    across = jnp.where(outermost, jnp.zeros_like(across), across)
    return jnp.where(even, across, ahead), jnp.where(even, ahead, across)


def edge_choice(first, final):
    even = is_even()
    return jnp.where(even, final, first), jnp.where(even, first, final)


def fetch_kernel(many, images, kern, ahead, across, taps, maps, sems):
    last = images.shape[1] - 1
    even = is_even()
    pairs = (
        (images.at[:, pl.ds(jnp.where(even, last, 0), 1)], ahead),
        (images.at[:, pl.ds(jnp.where(even, 0, last), 1)], across),
        (kern, taps),
        (images.at[:many], maps.at[:many]),
    )
    copies = [
        pltpu.make_async_copy(source, target, sems.at[index])
        for index, (source, target) in enumerate(pairs)
    ]
    for copy in copies:
        copy.start()
    for copy in copies:
        copy.wait()


def edge_kernel(total, stage, ahead, across, pre, ups, kern, acc, sums, low, high, keep, send, stats):
    count, _, width, cin = ahead.shape
    cout = kern.shape[3]
    last = pre.shape[1] - 1
    top, bot = sides(ahead[...], across[...])
    pixels = count * width
    shape = (count, width, cout)
    edges = []
    for a, source, row, out in ((0, top, 0, low), (2, bot, last, high)):
        taps = jnp.concatenate([kern[a, c] for c in range(3)], axis=1)
        value = merged(dot(source.reshape(pixels, cin), taps), shape) + pre[:, row]
        out[:, 0] = value
        edges.append(value.reshape(pixels, cout))
    shift = sums[2:3]
    delta = jnp.concatenate(edges, axis=0) - shift
    up = jnp.concatenate(
        [ups[:, 0].reshape(pixels, cout), ups[:, last].reshape(pixels, cout)], axis=0
    )
    big, small = split(delta)
    gram = acc[...] + statistics(small, big, up)
    moved = sums[0:1] + jnp.sum(delta, axis=0, keepdims=True)
    up_sum = sums[1:2] + jnp.sum(up.astype(F32), axis=0, keepdims=True)
    mixed = gram[:cout, :cout]
    square = gram[:cout, cout:] + mixed + mixed.T
    cross = gram[cout:, :cout] + gram[cout:, cout:]
    raw = moved + total * shift
    square = square + column(moved) * shift + column(shift) * raw
    cross = cross + column(up_sum) * shift
    half = cout // 2
    stats[0:half] = pack(square)
    stats[half : 2 * half] = pack(cross)
    stats[2 * half :] = jnp.zeros_like(stats[2 * half :])
    stats[2 * half : 2 * half + 1] = raw
    stats[2 * half + 1 : 2 * half + 2] = up_sum
    part = keep.shape[0]
    upper = is_upper(stage)
    keep[...] = jnp.where(upper, stats[part:], stats[:part])
    send[...] = jnp.where(upper, stats[:part], stats[part:])


def spread(blocks):
    zero = jnp.zeros(blocks.shape[1:], F32)
    return jnp.concatenate(
        [
            jnp.concatenate([blocks[0], zero], axis=1),
            jnp.concatenate([zero, blocks[1]], axis=1),
        ],
        axis=0,
    )


def group_sum(value, half):
    cols = jnp.sum(value, axis=0, keepdims=True)
    lane = lax.broadcasted_iota(jnp.int32, cols.shape, 1)
    low = jnp.sum(jnp.where(lane < half, cols, 0.0), axis=1, keepdims=True)
    high = jnp.sum(jnp.where(lane < half, 0.0, cols), axis=1, keepdims=True)
    return jnp.where(lane < half, low, high)


def whitening(stats, colors, offset, total_pix, half):
    cout = 2 * half
    row_i = lax.broadcasted_iota(jnp.int32, (cout, cout), 0)
    col_i = lax.broadcasted_iota(jnp.int32, (cout, cout), 1)
    eye = jnp.where(row_i == col_i, 1.0, 0.0)
    block = jnp.where((row_i < half) == (col_i < half), 1.0, 0.0)
    square = unpack(stats[0:half])
    cross = unpack(stats[half : 2 * half])
    average = stats[2 * half : 2 * half + 1] / total_pix
    up_total = stats[2 * half + 1 : 2 * half + 2]
    sigma = square / total_pix - block * (column(average) * average) + EPSILON * eye
    cross = cross - block * (column(up_total) * average)
    grad = dot3(colors.T, cross)
    direction = grad + grad.T
    traces = group_sum(sigma * eye, half)
    normed = sigma / traces
    zero = jnp.zeros_like(normed)

    def stacked(value, tangent):
        return jnp.concatenate(
            [
                jnp.concatenate([value, tangent], axis=1),
                jnp.concatenate([zero, value], axis=1),
            ],
            axis=0,
        )

    source = stacked(normed, direction)
    value = 1.5 * eye - 0.5 * normed
    tangent = -0.5 * direction
    for _ in range(NS_ITERS - 1):
        first = jnp.concatenate([value, tangent], axis=1)
        both = dot3(first, jnp.concatenate([stacked(value, tangent), source], axis=1))
        squared = both[:, : 2 * cout]
        scaled = stacked(both[:, 2 * cout : 3 * cout], both[:, 3 * cout :])
        cubed = dot3(squared, scaled)
        value = 1.5 * value - 0.5 * cubed[:, :cout]
        tangent = 1.5 * tangent - 0.5 * cubed[:, cout:]
    inverse = 1.0 / jnp.sqrt(traces)
    whitener = value * inverse
    shared = group_sum(tangent * normed, half) + 0.5 * group_sum(direction * value, half)
    symmetric = (tangent - eye * shared) * (inverse / traces)
    mixed = dot3(colors, whitener)
    color_sum = dot3(cross, whitener.T)
    up_mean = jnp.broadcast_to(up_total / total_pix, (8, cout))
    bias = -dot3(up_mean, mixed)[0:1]
    return average, mixed, symmetric / total_pix, bias, offset, color_sum


def image_moments(image, pre, low, high, ups, img, ahead, across, sums):
    rows, width, cin = img.shape[1:]
    cout = pre.shape[3]
    pixels = rows * width
    top, bot = sides(ahead[image], across[image])
    padded = jnp.concatenate([top, img[image], bot], axis=0)
    turned = padded.reshape((rows + 2) * width, cin).T
    full = jnp.concatenate([low[image], pre[image, 1 : rows - 1], high[image]], axis=0)
    columns = []
    for value in (ups[image], (full - sums[2:3]).astype(BF16)):
        after, before = shifted(value.astype(F32))
        columns += [after.astype(BF16), value, before.astype(BF16)]
    right = jnp.concatenate(columns, axis=2).reshape(pixels, 6 * cout)
    left = jnp.concatenate([turned[:, a * width : a * width + pixels] for a in range(3)], axis=0)
    tiles = [turned[:, row * width : (row + 1) * width].astype(F32) for row in range(rows + 2)]
    middle = functools.reduce(jnp.add, tiles[2:rows])
    outer = ((0, 1), (1, rows), (rows, rows + 1))
    totals = jnp.concatenate([middle + tiles[one] + tiles[two] for one, two in outer], axis=0)
    return left, right, totals


def moment_kernel(first, count, *refs):
    acc, maps = refs[-2:]
    found = [image_moments(first + index, *refs[:8]) for index in range(count)]
    product = dot(
        jnp.concatenate([left for left, _, _ in found], axis=1),
        jnp.concatenate([right for _, right, _ in found], axis=0),
    )
    totals = functools.reduce(jnp.add, [part for _, _, part in found])
    if len(refs) == 12:
        product = refs[8][...] + product
        totals = refs[9][...] + totals
    acc[...] = product
    maps[...] = totals


def whitening_kernel(
    total_pix,
    stage,
    own,
    other,
    colors,
    offset,
    sums,
    acc,
    maps,
    keep,
    send,
    grad_colors,
    mats,
    paint,
    paint_rows,
    stats,
):
    cout = 2 * colors.shape[1]
    half = cout // 2
    cin = acc.shape[0] // 3
    scaling = 1.0 / math.sqrt(total_pix)
    join_kernel(stage, own, other, stats)
    average, mixed, symmetric, bias, offs, color_sum = whitening(
        stats[...], spread(colors[...]), offset[...], total_pix, half
    )
    blank = jnp.zeros((cout, cout), BF16)
    mixed_h, mixed_l = split(mixed)
    color_h, color_l = split(mixed.T)
    sym_h, sym_l = split(symmetric)
    for target, blocks in (
        (mats, ((sym_h, sym_l), (mixed_h, mixed_l), (sym_h, blank))),
        (paint, ((color_h, color_l), (color_h, blank))),
    ):
        for index, (one, two) in enumerate(blocks):
            target[index * cout : (index + 1) * cout, :cout] = one
            target[index * cout : (index + 1) * cout, cout:] = two
    paint_rows[...] = jnp.zeros_like(paint_rows)
    paint_rows[0:1] = average
    paint_rows[1:2] = offs
    paint_rows[2:3] = bias
    scaled = color_sum * scaling
    grad_colors[0] = scaled[:half, :half]
    grad_colors[1] = pltpu.roll(scaled[half:], half, 1)[:, :half]

    moved = jnp.broadcast_to(sums[2:3] - average, (8, cout))
    constant = (bias + dot3(moved, symmetric)[0:1]) * scaling
    tall_h = jnp.concatenate([mixed_h, sym_h], axis=0)
    tall_l = jnp.concatenate([mixed_l, sym_l], axis=0)
    right = jnp.concatenate(
        [
            jnp.concatenate([tall_h, tall_l], axis=1),
            jnp.concatenate([tall_h, jnp.zeros_like(tall_l)], axis=1),
        ],
        axis=0,
    )
    lane = lax.broadcasted_iota(jnp.int32, (cin, maps.shape[1]), 1)
    seen = (lane < maps.shape[1] - 1, lane >= 0, lane > 0)
    parts = []
    for a in range(3):
        place = slice(a * cin, (a + 1) * cin)
        for c in range(3):
            pair = [acc[place, (k + c) * cout : (k + c + 1) * cout] for k in (0, 3)]
            left = jnp.concatenate(split(jnp.concatenate(pair, axis=1)), axis=1)
            result = dot(left, right)
            total = jnp.sum(jnp.where(seen[c], maps[place], 0.0), axis=1, keepdims=True)
            result = (result[:, :cout] + result[:, cout:]) * scaling + total * constant
            parts += [result[: cin // 2], result[cin // 2 :]]
    upper = is_upper(stage)
    for index in range(9):
        place = slice(index * cin // 2, (index + 1) * cin // 2)
        keep[place] = jnp.where(upper, parts[9 + index], parts[index])
        send[place] = jnp.where(upper, parts[index], parts[9 + index])


def centred_halves(image, pre, low, high, average):
    rows, width, cout = pre.shape[1:]
    full = jnp.concatenate([low[image], pre[image, 1 : rows - 1], high[image]], axis=0)
    return split(full.reshape(rows * width, cout) - average)


def edge_gradient_kernel(low, high, ups, mats, paint_rows, edge_ahead, edge_across):
    count, _, width, cout = low.shape
    last = ups.shape[1] - 1
    pre = jnp.concatenate([low[:, 0], high[:, 0]], axis=0).reshape(2 * count * width, cout)
    up = jnp.concatenate([ups[:, 0], ups[:, last]], axis=0).reshape(2 * count * width, cout)
    grad = pre_gradient(*split(pre - paint_rows[0:1]), up, mats, paint_rows)
    shaped = grad.reshape(2 * count, width, cout)
    edge_ahead[:, 0], edge_across[:, 0] = edge_choice(shaped[:count], shaped[count:])


def pre_gradient(big, small, up, mats, paint_rows):
    cout = up.shape[1]
    result = dot(jnp.concatenate([big, up, small], axis=1), mats[...])
    return (result[:, :cout] + result[:, cout:] + paint_rows[2:3]).astype(BF16)


def gradient_kernel(pre, low, high, ups, mats, paint_rows, pre_grad):
    image = pl.program_id(0)
    rows, width, cout = pre.shape[1:]
    big, small = centred_halves(image, pre, low, high, paint_rows[0:1])
    up = ups[image].reshape(rows * width, cout)
    grad = pre_gradient(big, small, up, mats, paint_rows)
    pre_grad[image] = grad.reshape(rows, width, cout)


def paint_kernel(pre, low, high, paint, paint_rows, colored):
    rows, width, cout = pre.shape[1:]
    halves = centred_halves(pl.program_id(0), pre, low, high, paint_rows[0:1])
    result = dot(jnp.concatenate(halves, axis=1), paint[...])
    result = result[:, :cout] + result[:, cout:] + paint_rows[1:2]
    colored[0] = result.astype(BF16).reshape(rows, width, cout)


def turn_kernel(kern, out):
    cout = kern.shape[3]
    for a in range(3):
        for c in range(3):
            tap = (a * 3 + c) * cout
            out[tap : tap + cout] = kern[a, c].T


def image_kernel(first, pre_grad, ahead, across, wts, *rest):
    out = rest[-1]
    image = pl.program_id(0) + first
    top, bot = sides(ahead[image], across[image])
    rows, width, cout = pre_grad.shape[1:]
    cin = wts.shape[1]
    exact = jnp.concatenate([top, pre_grad[image], bot], axis=0).astype(F32)
    after, before = shifted(exact)
    taps = [value.astype(BF16) for value in (after, exact, before)]
    wide = jnp.concatenate(
        [taps[c][2 - a : 2 - a + rows] for a in range(3) for c in range(3)], axis=2
    )
    result = dot(wide.reshape(rows * width, 9 * cout), wts[...])
    out[0] = result.astype(BF16).reshape(rows, width, cin)


def fold_kernel(stage, value, received, keep, send):
    upper = is_upper(stage)
    part = keep.shape[0]
    low = value[:part] + received[:part]
    high = value[part:] + received[part:]
    keep[...] = jnp.where(upper, high, low)
    send[...] = jnp.where(upper, low, high)


def join_kernel(stage, value, received, out):
    upper = is_upper(stage)
    part = value.shape[0]
    out[:part] = jnp.where(upper, received[...], value[...])
    out[part:] = jnp.where(upper, value[...], received[...])


def finish_kernel(stage, own, value, *rest):
    out, held, sems = rest[-3:]
    count, size = held.shape[:2]
    upper = is_upper(stage) if own else jnp.logical_not(is_upper(stage))
    start = jnp.where(upper, count * size, 0)
    copies = []
    for index in range(count):
        held[index] = value[index * size : (index + 1) * size].astype(F32)
        place = pl.ds(pl.multiple_of(start + index * size, size), size)
        copies.append(pltpu.make_async_copy(held.at[index], out.at[place], sems.at[index]))
        copies[-1].start()
    for copy in copies:
        copy.wait()


def image_spec(shape, place=lambda b: b):
    return pl.BlockSpec((1, *shape[1:]), lambda b: (place(b),) + (0,) * (len(shape) - 1))


def whole_spec(shape):
    return pl.BlockSpec(shape, lambda b: (0,) * len(shape))


def in_hbm(value):
    return pltpu.with_memory_space_constraint(value, pltpu.HBM)


def resident():
    return pl.BlockSpec(memory_space=pltpu.VMEM)


def forward(first, images, taps, upstream):
    count, rows, width, cin = images.shape
    cout = taps.shape[3]
    many = images_per_step(count)
    shapes = [
        ((count, rows, width, cout), F32),
        ((2 * cout, 2 * cout), F32),
        ((8, cout), F32),
        (images.shape, BF16),
        (upstream.shape, BF16),
    ]
    space = pl.BlockSpec(memory_space=pltpu.HBM)
    return pl.pallas_call(
        functools.partial(forward_kernel, many),
        grid=(count // many,),
        in_specs=[resident(), space, resident(), space],
        out_specs=[resident()] * len(shapes),
        out_shape=[jax.ShapeDtypeStruct(shape, dtype) for shape, dtype in shapes],
        scratch_shapes=[
            pltpu.VMEM((10 * cin, 2 * cout), BF16),
            pltpu.VMEM((many, 2, (rows - 2) * width, cout), BF16),
            pltpu.SemaphoreType.DMA((count,)),
            pltpu.SemaphoreType.DMA((count,)),
        ],
        input_output_aliases={0: 3},
        compiler_params=pltpu.CompilerParams(vmem_limit_bytes=28 * MIB),
        cost_estimate=pl.CostEstimate(
            flops=2 * count * rows * width * 9 * cin * cout,
            bytes_accessed=2 * images.size + 2 * upstream.size + 4 * upstream.size,
            transcendentals=0,
        ),
        name="forward_inner",
    )(first, in_hbm(images), taps, in_hbm(upstream))


def edges(stage, top, bot, pre, upstream, kernel, acc, sums):
    count, rows, width, cout = pre.shape
    part = (cout + 16) // 2
    edge = (count, 1, width, cout)
    shapes = [edge, edge, (part, cout), (part, cout)]
    return pl.pallas_call(
        functools.partial(edge_kernel, count * rows * width, stage),
        in_specs=[resident()] * 7,
        out_specs=[resident()] * 4,
        out_shape=[jax.ShapeDtypeStruct(shape, F32) for shape in shapes],
        scratch_shapes=[pltpu.VMEM((2 * part, cout), F32)],
        compiler_params=pltpu.CompilerParams(vmem_limit_bytes=12 * MIB),
        cost_estimate=pl.CostEstimate(
            flops=2 * 2 * count * width * 3 * top.shape[3] * cout,
            bytes_accessed=4 * top.size + 24 * count * width * cout,
            transcendentals=0,
        ),
        name="forward_edges",
    )(top, bot, pre, upstream, kernel, acc, sums)


def moments(first, count, pre, low, high, upstream, images, top, bot, sums, *sofar):
    width, cin = images.shape[2:]
    cout = upstream.shape[3]
    rows = images.shape[1]
    operands = (pre, low, high, upstream, images, top, bot, sums, *sofar)
    return pl.pallas_call(
        functools.partial(moment_kernel, first, count),
        in_specs=[resident()] * len(operands),
        out_specs=[resident()] * 2,
        out_shape=[
            jax.ShapeDtypeStruct((3 * cin, 6 * cout), F32),
            jax.ShapeDtypeStruct((3 * cin, width), F32),
        ],
        input_output_aliases={8: 0, 9: 1} if sofar else {},
        compiler_params=pltpu.CompilerParams(vmem_limit_bytes=28 * MIB),
        cost_estimate=pl.CostEstimate(
            flops=2 * count * rows * width * 18 * cin * cout, bytes_accessed=8 * MIB, transcendentals=0
        ),
        name="moments",
    )(*operands)


def whitened(total_pix, stage, own, other, colors, offset, sums, acc, maps):
    half = colors.shape[1]
    cout = 2 * half
    cin = acc.shape[0] // 3
    shapes = [
        ((9 * cin // 2, cout), F32),
        ((9 * cin // 2, cout), F32),
        ((2, half, half), F32),
        ((3 * cout, 2 * cout), BF16),
        ((2 * cout, 2 * cout), BF16),
        ((8, cout), F32),
    ]
    return pl.pallas_call(
        functools.partial(whitening_kernel, total_pix, stage),
        in_specs=[resident()] * 7,
        out_specs=[resident()] * len(shapes),
        out_shape=[jax.ShapeDtypeStruct(shape, dtype) for shape, dtype in shapes],
        scratch_shapes=[pltpu.VMEM((cout + 16, cout), F32)],
        compiler_params=pltpu.CompilerParams(vmem_limit_bytes=20 * MIB),
        cost_estimate=pl.CostEstimate(
            flops=2 * 9 * cin * 8 * cout * cout, bytes_accessed=8 * MIB, transcendentals=0
        ),
        name="whitening",
    )(own, other, colors, offset, sums, acc, maps)


def edge_gradients(low, high, upstream, mats, paint_rows):
    return pl.pallas_call(
        edge_gradient_kernel,
        in_specs=[resident()] * 5,
        out_specs=[resident()] * 2,
        out_shape=[jax.ShapeDtypeStruct(low.shape, BF16)] * 2,
        compiler_params=pltpu.CompilerParams(vmem_limit_bytes=16 * MIB),
        name="edge_gradients",
    )(low, high, upstream, mats, paint_rows)


def gradients(pre, low, high, upstream, mats, paint_rows):
    count, rows, width, cout = pre.shape
    return pl.pallas_call(
        gradient_kernel,
        grid=(count,),
        in_specs=[resident()] * 6,
        out_specs=resident(),
        out_shape=jax.ShapeDtypeStruct(pre.shape, BF16),
        compiler_params=pltpu.CompilerParams(vmem_limit_bytes=16 * MIB),
        cost_estimate=pl.CostEstimate(
            flops=2 * count * rows * width * 6 * cout * cout,
            bytes_accessed=8 * pre.size,
            transcendentals=0,
        ),
        name="pre_gradient",
    )(pre, low, high, upstream, mats, paint_rows)


def painted(pre, low, high, paint, paint_rows):
    count, rows, width, cout = pre.shape
    return pl.pallas_call(
        paint_kernel,
        grid=(count,),
        in_specs=[resident()] * 5,
        out_specs=image_spec(pre.shape),
        out_shape=jax.ShapeDtypeStruct(pre.shape, BF16),
        compiler_params=pltpu.CompilerParams(vmem_limit_bytes=16 * MIB),
        cost_estimate=pl.CostEstimate(
            flops=2 * count * rows * width * 4 * cout * cout,
            bytes_accessed=6 * pre.size,
            transcendentals=0,
        ),
        name="colored",
    )(pre, low, high, paint, paint_rows)


def turned_weights(kernel):
    cin, cout = kernel.shape[2:]
    return pl.pallas_call(
        turn_kernel,
        out_shape=jax.ShapeDtypeStruct((9 * cout, cin), BF16),
        compiler_params=pltpu.CompilerParams(vmem_limit_bytes=4 * MIB),
        name="turned_weights",
    )(kernel)


def image_gradient(first, count, pre_grad, top, bot, turned, out=None):
    images, rows, width, cout = pre_grad.shape
    cin = turned.shape[1]
    shape = (images, rows, width, cin)

    def place(b):
        return b + first

    operands = [pre_grad, top, bot, turned]
    in_specs = [resident()] * 4
    aliases = {}
    if out is not None:
        operands.append(out)
        in_specs.append(pl.BlockSpec(memory_space=pl.ANY))
        aliases = {4: 0}
    return pl.pallas_call(
        functools.partial(image_kernel, first),
        grid=(count,),
        in_specs=in_specs,
        out_specs=image_spec(shape, place),
        out_shape=jax.ShapeDtypeStruct(shape, BF16),
        input_output_aliases=aliases,
        compiler_params=pltpu.CompilerParams(vmem_limit_bytes=12 * MIB),
        cost_estimate=pl.CostEstimate(
            flops=2 * count * rows * width * 9 * cin * cout,
            bytes_accessed=2 * count * rows * width * (cin + cout),
            transcendentals=0,
        ),
        name="image_gradient",
    )(*operands)


def images_per_step(count):
    return 2 if count % 2 == 0 else 1


def fetched(images, kernel):
    count, rows, width, cin = images.shape
    edge = (count, 1, width, cin)
    space = pl.BlockSpec(memory_space=pltpu.HBM)
    return pl.pallas_call(
        functools.partial(fetch_kernel, images_per_step(count)),
        in_specs=[space, space],
        out_specs=[resident()] * 4,
        out_shape=[
            jax.ShapeDtypeStruct(shape, BF16) for shape in (edge, edge, kernel.shape, images.shape)
        ],
        scratch_shapes=[pltpu.SemaphoreType.DMA((4,))],
        compiler_params=pltpu.CompilerParams(vmem_limit_bytes=4 * MIB),
        name="edge_rows",
    )(in_hbm(images), in_hbm(kernel))


def small_call(kernel, name, *operands, out):
    return pl.pallas_call(
        kernel,
        in_specs=[resident()] * len(operands),
        out_specs=[resident()] * len(out),
        out_shape=out,
        compiler_params=pltpu.CompilerParams(vmem_limit_bytes=4 * MIB),
        name=name,
    )(*operands)


def fold(value, received, stage):
    half = jax.ShapeDtypeStruct((value.shape[0] // 2, value.shape[1]), value.dtype)
    return small_call(
        functools.partial(fold_kernel, stage), "fold", value, received, out=[half, half]
    )


def join(value, received, stage):
    whole = jax.ShapeDtypeStruct((value.shape[0] * 2, value.shape[1]), value.dtype)
    return small_call(
        functools.partial(join_kernel, stage), "join", value, received, out=[whole]
    )[0]


def finish(stage, value, out=None):
    part, lanes = value.shape
    operands, aliases = (value,), {}
    if out is not None:
        operands, aliases = (value, out), {1: 0}
    space = pl.BlockSpec(memory_space=pltpu.HBM)
    return pl.pallas_call(
        functools.partial(finish_kernel, stage, out is None),
        in_specs=[resident(), space][: len(operands)],
        out_specs=space,
        out_shape=jax.ShapeDtypeStruct((2 * part, lanes), F32),
        scratch_shapes=[
            pltpu.VMEM((2, part // 2, lanes), F32),
            pltpu.SemaphoreType.DMA((2,)),
        ],
        input_output_aliases=aliases,
        compiler_params=pltpu.CompilerParams(vmem_limit_bytes=4 * MIB),
        name="finish",
    )(*operands)


def halos(ahead, across):
    count, groups = lax.axis_size("rows"), lax.axis_size("dp")
    offset = 2 if groups % 4 == 0 else 1 if groups % 2 == 0 else 0
    pairs = ([], [])
    for group in range(groups):
        for place in range(count):
            for first in (0, 1):
                partner = place + 1 if place % 2 == first else place - 1
                inside = 0 <= partner < count
                other = (group, partner) if inside else (group ^ offset, place)
                pairs[first].append((group * count + place, other[0] * count + other[1]))
    return lax.ppermute(ahead, AXES, pairs[0]), lax.ppermute(across, AXES, pairs[1])


def exchange(value, devices, stage):
    pairs = [(i, i ^ (stage[1] if i & 1 else stage[0])) for i in range(devices)]
    return lax.ppermute(value, AXES, pairs)


def beside(send, devices, stage, task, operands):
    send, operands = lax.optimization_barrier((send, operands))
    received = exchange(send, devices, stage)
    result = task(*operands)
    return lax.optimization_barrier((received, result))


def body(images, kernel, colors, offset, upstream):
    count, rows, width, cin = images.shape
    cout = kernel.shape[3]
    devices = lax.axis_size("dp") * lax.axis_size("rows")
    total_pix = count * rows * width * devices
    plan = stages(devices)
    ahead, across, kernel, maps = fetched(images, kernel)
    top, bot = halos(ahead, across)
    pre, acc, sums, images, upstream = forward(maps, images, kernel, upstream)
    low, high, value, send = edges(plan[0], top, bot, pre, upstream, kernel, acc, sums)
    state = {"next": 0, "moments": (), "grad": None}

    def summed(send, stage, many):
        first = state["next"]
        many = min(many, count - first)
        if many == 0:
            return exchange(send, devices, stage)
        state["next"] = first + many
        operands = (pre, low, high, upstream, images, top, bot, sums, *state["moments"])
        received, state["moments"] = beside(
            send, devices, stage, functools.partial(moments, first, many), operands
        )
        return received

    value = value + exchange(send, devices, plan[0])
    for stage in plan[1:]:
        value = value + summed(value, stage, 2 if stage in plan[2:4] else 1)
    received = exchange(value, devices, plan[0])
    first = state["next"]
    if first < count:
        operands = (pre, low, high, upstream, images, top, bot, sums, *state["moments"])
        state["moments"] = moments(first, count - first, *operands)
    value, send, grad_colors, mats, paint, paint_rows = whitened(
        total_pix,
        plan[0],
        value,
        received,
        colors,
        offset.reshape(1, cout),
        sums,
        *state["moments"],
    )
    received, (edge_ahead, edge_across, turned) = beside(
        send,
        devices,
        plan[0],
        lambda kernel, *operands: (*edge_gradients(*operands), turned_weights(kernel)),
        (kernel, low, high, upstream, mats, paint_rows),
    )
    state["next"] = 0
    shares = [1, 1, 1, 1, 2]

    def transfer(send, stage):
        first = state["next"]
        if first >= count:
            return exchange(send, devices, stage)
        many = min(shares.pop(0), count - first) if shares else count - first
        state["next"] = first + many
        operands = (pre_grad, grad_top, grad_bot, turned)
        if state["grad"] is not None:
            operands = (*operands, state["grad"])
        received, state["grad"] = beside(
            send, devices, stage, functools.partial(image_gradient, first, many), operands
        )
        return received

    cuts = []
    for stage in plan[1:]:
        if value.shape[0] % 32 == 0 and value.shape[0] > 144:
            value, send = fold(value, received, stage)
            cuts.append(stage)
        else:
            value = send = value + received
        if stage == plan[1]:
            send, edge_ahead, edge_across = lax.optimization_barrier(
                (send, edge_ahead, edge_across)
            )
            grad_top, grad_bot = halos(edge_ahead, edge_across)
            received, pre_grad = beside(
                send, devices, stage, gradients, (pre, low, high, upstream, mats, paint_rows)
            )
        elif stage == plan[2]:
            received, colored = beside(
                send, devices, stage, painted, (pre, low, high, paint, paint_rows)
            )
        else:
            received = transfer(send, stage)
    value = (value + received).astype(BF16)
    for stage in reversed(cuts):
        value = join(value, transfer(value, stage), stage)
    received, result = beside(
        value, devices, plan[0], functools.partial(finish, plan[0]), (value,)
    )
    first = state["next"]
    if first < count:
        operands = (pre_grad, grad_top, grad_bot, turned, state["grad"])
        state["grad"] = image_gradient(first, count - first, *operands)
    grad_kernel = finish(plan[0], received, result).reshape(3, 3, cin, cout)
    return colored, state["grad"], grad_kernel, grad_colors


def solution(mesh):
    placed = (P("dp", "rows", None, None), P(), P(), P(), P("dp", "rows", None, None))
    return jax.shard_map(
        body,
        mesh=mesh,
        in_specs=placed,
        out_specs=(P("dp", "rows", None, None), P("dp", "rows", None, None), P(), P()),
        check_vma=False,
    )
```

```python
import functools
import math

import jax
import jax.numpy as jnp
from jax import lax
from jax.experimental import pallas as pl
from jax.experimental.pallas import tpu as pltpu
from jax.sharding import PartitionSpec as P

NS_ITERS = 5
EPSILON = 1e-05
F32 = jnp.float32
BF16 = jnp.bfloat16
MIB = 1024 * 1024
AXES = ("dp", "rows")


def device_index():
    return lax.axis_index("dp") * lax.axis_size("rows") + lax.axis_index("rows")


def is_even():
    return lax.axis_index("rows") % 2 == 0


def is_upper(stage):
    index = device_index()
    return index & jnp.where(index & 1 != 0, stage[1], stage[0]) != 0


def stages(devices):
    bits = [1 << i for i in range(devices.bit_length() - 1)]
    plan = [(bit, bit) for bit in bits]
    if len(bits) > 2:
        plan[1:3] = [(4, 2), (2, 4)]
    return plan


def split(value):
    high = value.astype(BF16)
    return high, (value - high.astype(F32)).astype(BF16)


def dot(left, right, dims=((1,), (0,))):
    return lax.dot_general(left, right, (dims, ((), ())), preferred_element_type=F32)


def dot3(left, right):
    lh, ll = split(left)
    rh, rl = split(right)
    return dot(
        jnp.concatenate([lh, lh, ll], axis=1), jnp.concatenate([rh, rl, rh], axis=0)
    )


def shifted(value):
    width = value.shape[1]
    col = lax.broadcasted_iota(jnp.int32, (1, *value.shape[1:]), 1)
    after = jnp.where(col == width - 1, 0.0, pltpu.roll(value, width - 1, 1))
    before = jnp.where(col == 0, 0.0, pltpu.roll(value, 1, 1))
    return after, before


def merged(prod, shape):
    cout = shape[2]
    _, left = shifted(prod[:, :cout].reshape(shape))
    right, _ = shifted(prod[:, 2 * cout :].reshape(shape))
    return prod[:, cout : 2 * cout].reshape(shape) + left + right


def paired_rows(padded, wts, cout):
    rows, width, cin = padded.shape[0] - 2, *padded.shape[1:]
    pairs = rows // 2
    parts = [
        jnp.concatenate([padded[2 * k + a : 2 * k + a + 1] for k in range(pairs)], axis=0)
        for a in range(4)
    ]
    wide = jnp.concatenate(parts, axis=2).reshape(pairs * width, 4 * cin)
    outer = dot(wide[:, : 3 * cin], wts[: 3 * cin])
    shared = dot(wide, wts[3 * cin : 7 * cin])
    inner = dot(wide[:, cin:], wts[7 * cin :])
    shape = (pairs, width, cout)

    def added_up(left, middle, right):
        _, before = shifted(left.reshape(shape))
        after, _ = shifted(right.reshape(shape))
        return middle.reshape(shape) + before + after

    first = added_up(outer[:, :cout], outer[:, cout:], shared[:, :cout])
    second = added_up(shared[:, cout:], inner[:, :cout], inner[:, cout:])
    ordered = [part[k : k + 1] for k in range(pairs) for part in (first, second)]
    return jnp.concatenate(ordered, axis=0)


def column(row):
    size = row.shape[1]
    return jnp.broadcast_to(row, (size, size)).T


def pack(full):
    half = full.shape[0] // 2
    lane = lax.broadcasted_iota(jnp.int32, (half, full.shape[1]), 1)
    return jnp.where(lane < half, full[:half], full[half:])


def unpack(packed):
    half = packed.shape[0]
    lane = lax.broadcasted_iota(jnp.int32, packed.shape, 1)
    return jnp.concatenate(
        [jnp.where(lane < half, packed, 0.0), jnp.where(lane < half, 0.0, packed)], axis=0
    )


def statistics(low, high, up):
    return dot(
        jnp.concatenate([high, up], axis=1), jnp.concatenate([low, high], axis=1), ((0,), (0,))
    )


def forward_kernel(
    many, first, img, kern, upstream, pre_out, acc, sums, maps, ups, wts, held, map_sems, up_sems
):
    step = pl.program_id(0)
    last = pl.num_programs(0) - 1
    count, rows, width, cin = img.shape
    cout = kern.shape[3]
    inner = (rows - 2) * width

    def map_copy(image):
        return pltpu.make_async_copy(img.at[image], maps.at[image], map_sems.at[image])

    def up_copy(image):
        return pltpu.make_async_copy(upstream.at[image], ups.at[image], up_sems.at[image])

    def gather(group):
        grams, totals = [], []
        for index in range(many):
            up = ups[group * many + index, 1 : rows - 1].reshape(inner, cout)
            grams.append(statistics(held[index, 0], held[index, 1], up))
            totals.append(jnp.sum(up.astype(F32), axis=0, keepdims=True))
        acc[...] += functools.reduce(jnp.add, grams)
        sums[1:2] += functools.reduce(jnp.add, totals)

    def convolve(initial):
        blank = jnp.zeros((1, width, cin), BF16)
        shift = sums[2:3]
        moved = []
        for index in range(many):
            image = step * many + index
            padded = jnp.concatenate([blank, maps[image], blank], axis=0)
            pre = paired_rows(padded, wts, cout)
            pre_out[image] = pre
            mid = pre[1 : rows - 1].reshape(inner, cout)
            if initial and index == 0:
                shift = jnp.sum(mid, axis=0, keepdims=True) / inner
                sums[2:3] = shift
            delta = mid - shift
            high, low = split(delta)
            held[index, 0] = low
            held[index, 1] = high
            moved.append(jnp.sum(delta, axis=0, keepdims=True))
        sums[0:1] += functools.reduce(jnp.add, moved)

    @pl.when(step == 0)
    def _():
        for image in range(count):
            if image >= many:
                map_copy(image).start()
            up_copy(image).start()
        blank = jnp.zeros((cin, cout), BF16)
        blocks = [(kern[a, 0], kern[a, 1]) for a in range(3)]
        blocks += [
            (kern[a, 2] if a < 3 else blank, kern[a - 1, 0] if a > 0 else blank) for a in range(4)
        ]
        blocks += [(kern[a, 1], kern[a, 2]) for a in range(3)]
        for index, (one, two) in enumerate(blocks):
            wts[index * cin : (index + 1) * cin, :cout] = one
            wts[index * cin : (index + 1) * cin, cout:] = two
        acc[...] = jnp.zeros_like(acc)
        sums[...] = jnp.zeros_like(sums)
        convolve(True)

    @pl.when(step > 0)
    def _():
        for index in range(many):
            map_copy(step * many + index).wait()
            up_copy((step - 1) * many + index).wait()
        gather(step - 1)
        convolve(False)

    @pl.when(step == last)
    def _():
        for index in range(many):
            up_copy(step * many + index).wait()
        gather(step)


def sides(ahead, across):
    place = lax.axis_index("rows")
    even = is_even()
    outermost = jnp.where(even, place == 0, place == lax.axis_size("rows") - 1)
    across = jnp.where(outermost, jnp.zeros_like(across), across)
    return jnp.where(even, across, ahead), jnp.where(even, ahead, across)


def edge_choice(first, final):
    even = is_even()
    return jnp.where(even, final, first), jnp.where(even, first, final)


def fetch_kernel(many, images, kern, ahead, across, taps, maps, sems):
    last = images.shape[1] - 1
    even = is_even()
    pairs = (
        (images.at[:, pl.ds(jnp.where(even, last, 0), 1)], ahead),
        (images.at[:, pl.ds(jnp.where(even, 0, last), 1)], across),
        (kern, taps),
        (images.at[:many], maps.at[:many]),
    )
    copies = [
        pltpu.make_async_copy(source, target, sems.at[index])
        for index, (source, target) in enumerate(pairs)
    ]
    for copy in copies:
        copy.start()
    for copy in copies:
        copy.wait()


def edge_kernel(total, stage, ahead, across, pre, ups, kern, acc, sums, low, high, keep, send, stats):
    count, _, width, cin = ahead.shape
    cout = kern.shape[3]
    last = pre.shape[1] - 1
    top, bot = sides(ahead[...], across[...])
    pixels = count * width
    shape = (count, width, cout)
    shift = sums[2:3]
    gram, moved, up_sum = acc[...], sums[0:1], sums[1:2]
    for a, source, row, out in ((0, top, 0, low), (2, bot, last, high)):
        taps = jnp.concatenate([kern[a, c] for c in range(3)], axis=1)
        value = merged(dot(source.reshape(pixels, cin), taps), shape) + pre[:, row]
        out[:, 0] = value
        delta = value.reshape(pixels, cout) - shift
        up = ups[:, row].reshape(pixels, cout)
        big, small = split(delta)
        gram = gram + statistics(small, big, up)
        moved = moved + jnp.sum(delta, axis=0, keepdims=True)
        up_sum = up_sum + jnp.sum(up.astype(F32), axis=0, keepdims=True)
    mixed = gram[:cout, :cout]
    square = gram[:cout, cout:] + mixed + mixed.T
    cross = gram[cout:, :cout] + gram[cout:, cout:]
    raw = moved + total * shift
    square = square + column(moved) * shift + column(shift) * raw
    cross = cross + column(up_sum) * shift
    half = cout // 2
    stats[0:half] = pack(square)
    stats[half : 2 * half] = pack(cross)
    stats[2 * half :] = jnp.zeros_like(stats[2 * half :])
    stats[2 * half : 2 * half + 1] = raw
    stats[2 * half + 1 : 2 * half + 2] = up_sum
    part = keep.shape[0]
    upper = is_upper(stage)
    keep[...] = jnp.where(upper, stats[part:], stats[:part])
    send[...] = jnp.where(upper, stats[:part], stats[part:])


def spread(blocks):
    zero = jnp.zeros(blocks.shape[1:], F32)
    return jnp.concatenate(
        [
            jnp.concatenate([blocks[0], zero], axis=1),
            jnp.concatenate([zero, blocks[1]], axis=1),
        ],
        axis=0,
    )


def group_sum(value, half):
    cols = jnp.sum(value, axis=0, keepdims=True)
    lane = lax.broadcasted_iota(jnp.int32, cols.shape, 1)
    low = jnp.sum(jnp.where(lane < half, cols, 0.0), axis=1, keepdims=True)
    high = jnp.sum(jnp.where(lane < half, 0.0, cols), axis=1, keepdims=True)
    return jnp.where(lane < half, low, high)


def whitening(stats, colors, offset, total_pix, half):
    cout = 2 * half
    row_i = lax.broadcasted_iota(jnp.int32, (cout, cout), 0)
    col_i = lax.broadcasted_iota(jnp.int32, (cout, cout), 1)
    eye = jnp.where(row_i == col_i, 1.0, 0.0)
    block = jnp.where((row_i < half) == (col_i < half), 1.0, 0.0)
    square = unpack(stats[0:half])
    cross = unpack(stats[half : 2 * half])
    average = stats[2 * half : 2 * half + 1] / total_pix
    up_total = stats[2 * half + 1 : 2 * half + 2]
    sigma = square / total_pix - block * (column(average) * average) + EPSILON * eye
    cross = cross - block * (column(up_total) * average)
    grad = dot3(colors.T, cross)
    direction = grad + grad.T
    traces = group_sum(sigma * eye, half)
    normed = sigma / traces
    zero = jnp.zeros_like(normed)

    def stacked(value, tangent):
        return jnp.concatenate(
            [
                jnp.concatenate([value, tangent], axis=1),
                jnp.concatenate([zero, value], axis=1),
            ],
            axis=0,
        )

    source = stacked(normed, direction)
    value = 1.5 * eye - 0.5 * normed
    tangent = -0.5 * direction
    for _ in range(NS_ITERS - 1):
        first = jnp.concatenate([value, tangent], axis=1)
        both = dot3(first, jnp.concatenate([stacked(value, tangent), source], axis=1))
        squared = both[:, : 2 * cout]
        scaled = stacked(both[:, 2 * cout : 3 * cout], both[:, 3 * cout :])
        cubed = dot3(squared, scaled)
        value = 1.5 * value - 0.5 * cubed[:, :cout]
        tangent = 1.5 * tangent - 0.5 * cubed[:, cout:]
    inverse = 1.0 / jnp.sqrt(traces)
    whitener = value * inverse
    shared = group_sum(tangent * normed, half) + 0.5 * group_sum(direction * value, half)
    symmetric = (tangent - eye * shared) * (inverse / traces)
    mixed = dot3(colors, whitener)
    color_sum = dot3(cross, whitener.T)
    up_mean = jnp.broadcast_to(up_total / total_pix, (8, cout))
    bias = -dot3(up_mean, mixed)[0:1]
    return average, mixed, symmetric / total_pix, bias, offset, color_sum


def image_moments(image, pre, low, high, ups, img, ahead, across, sums):
    rows, width, cin = img.shape[1:]
    cout = pre.shape[3]
    pixels = rows * width
    top, bot = sides(ahead[image], across[image])
    padded = jnp.concatenate([top, img[image], bot], axis=0)
    turned = padded.reshape((rows + 2) * width, cin).T
    full = jnp.concatenate([low[image], pre[image, 1 : rows - 1], high[image]], axis=0)
    columns = []
    for value in (ups[image], (full - sums[2:3]).astype(BF16)):
        after, before = shifted(value.astype(F32))
        columns += [after.astype(BF16), value, before.astype(BF16)]
    right = jnp.concatenate(columns, axis=2).reshape(pixels, 6 * cout)
    left = jnp.concatenate([turned[:, a * width : a * width + pixels] for a in range(3)], axis=0)
    tiles = [turned[:, row * width : (row + 1) * width].astype(F32) for row in range(rows + 2)]
    middle = functools.reduce(jnp.add, tiles[2:rows])
    outer = ((0, 1), (1, rows), (rows, rows + 1))
    totals = jnp.concatenate([middle + tiles[one] + tiles[two] for one, two in outer], axis=0)
    return left, right, totals


def moment_kernel(first, count, *refs):
    acc, maps = refs[-2:]
    found = [image_moments(first + index, *refs[:8]) for index in range(count)]
    product = dot(
        jnp.concatenate([left for left, _, _ in found], axis=1),
        jnp.concatenate([right for _, right, _ in found], axis=0),
    )
    totals = functools.reduce(jnp.add, [part for _, _, part in found])
    if len(refs) == 12:
        product = refs[8][...] + product
        totals = refs[9][...] + totals
    acc[...] = product
    maps[...] = totals


def whitening_kernel(
    total_pix,
    stage,
    own,
    other,
    colors,
    offset,
    sums,
    acc,
    maps,
    keep,
    send,
    grad_colors,
    mats,
    paint,
    paint_rows,
    stats,
):
    cout = 2 * colors.shape[1]
    half = cout // 2
    cin = acc.shape[0] // 3
    scaling = 1.0 / math.sqrt(total_pix)
    join_kernel(stage, own, other, stats)
    average, mixed, symmetric, bias, offs, color_sum = whitening(
        stats[...], spread(colors[...]), offset[...], total_pix, half
    )
    blank = jnp.zeros((cout, cout), BF16)
    mixed_h, mixed_l = split(mixed)
    color_h, color_l = split(mixed.T)
    sym_h, sym_l = split(symmetric)
    for target, blocks in (
        (mats, ((sym_h, sym_l), (mixed_h, mixed_l), (sym_h, blank))),
        (paint, ((color_h, color_l), (color_h, blank))),
    ):
        for index, (one, two) in enumerate(blocks):
            target[index * cout : (index + 1) * cout, :cout] = one
            target[index * cout : (index + 1) * cout, cout:] = two
    paint_rows[...] = jnp.zeros_like(paint_rows)
    paint_rows[0:1] = average
    paint_rows[1:2] = offs
    paint_rows[2:3] = bias
    scaled = color_sum * scaling
    grad_colors[0] = scaled[:half, :half]
    grad_colors[1] = pltpu.roll(scaled[half:], half, 1)[:, :half]

    moved = jnp.broadcast_to(sums[2:3] - average, (8, cout))
    constant = (bias + dot3(moved, symmetric)[0:1]) * scaling
    tall_h = jnp.concatenate([mixed_h, sym_h], axis=0)
    tall_l = jnp.concatenate([mixed_l, sym_l], axis=0)
    right = jnp.concatenate(
        [
            jnp.concatenate([tall_h, tall_l], axis=1),
            jnp.concatenate([tall_h, jnp.zeros_like(tall_l)], axis=1),
        ],
        axis=0,
    )
    lane = lax.broadcasted_iota(jnp.int32, (cin, maps.shape[1]), 1)
    seen = (lane < maps.shape[1] - 1, lane >= 0, lane > 0)
    parts = []
    for a in range(3):
        place = slice(a * cin, (a + 1) * cin)
        for c in range(3):
            pair = [acc[place, (k + c) * cout : (k + c + 1) * cout] for k in (0, 3)]
            left = jnp.concatenate(split(jnp.concatenate(pair, axis=1)), axis=1)
            result = dot(left, right)
            total = jnp.sum(jnp.where(seen[c], maps[place], 0.0), axis=1, keepdims=True)
            result = (result[:, :cout] + result[:, cout:]) * scaling + total * constant
            parts += [result[: cin // 2], result[cin // 2 :]]
    upper = is_upper(stage)
    for index in range(9):
        place = slice(index * cin // 2, (index + 1) * cin // 2)
        keep[place] = jnp.where(upper, parts[9 + index], parts[index])
        send[place] = jnp.where(upper, parts[index], parts[9 + index])


def centred_halves(image, pre, low, high, average):
    rows, width, cout = pre.shape[1:]
    full = jnp.concatenate([low[image], pre[image, 1 : rows - 1], high[image]], axis=0)
    return split(full.reshape(rows * width, cout) - average)


def edge_gradient_kernel(low, high, ups, mats, paint_rows, edge_ahead, edge_across):
    count, _, width, cout = low.shape
    last = ups.shape[1] - 1
    pre = jnp.concatenate([low[:, 0], high[:, 0]], axis=0).reshape(2 * count * width, cout)
    up = jnp.concatenate([ups[:, 0], ups[:, last]], axis=0).reshape(2 * count * width, cout)
    grad = pre_gradient(*split(pre - paint_rows[0:1]), up, mats, paint_rows)
    shaped = grad.reshape(2 * count, width, cout)
    edge_ahead[:, 0], edge_across[:, 0] = edge_choice(shaped[:count], shaped[count:])


def pre_gradient(big, small, up, mats, paint_rows):
    cout = up.shape[1]
    result = dot(jnp.concatenate([big, up, small], axis=1), mats[...])
    return (result[:, :cout] + result[:, cout:] + paint_rows[2:3]).astype(BF16)


def gradient_kernel(pre, low, high, ups, mats, paint_rows, pre_grad):
    image = pl.program_id(0)
    rows, width, cout = pre.shape[1:]
    big, small = centred_halves(image, pre, low, high, paint_rows[0:1])
    up = ups[image].reshape(rows * width, cout)
    grad = pre_gradient(big, small, up, mats, paint_rows)
    pre_grad[image] = grad.reshape(rows, width, cout)


def paint_kernel(pre, low, high, paint, paint_rows, colored):
    rows, width, cout = pre.shape[1:]
    halves = centred_halves(pl.program_id(0), pre, low, high, paint_rows[0:1])
    result = dot(jnp.concatenate(halves, axis=1), paint[...])
    result = result[:, :cout] + result[:, cout:] + paint_rows[1:2]
    colored[0] = result.astype(BF16).reshape(rows, width, cout)


def turn_kernel(kern, out):
    cout = kern.shape[3]
    for a in range(3):
        for c in range(3):
            tap = (a * 3 + c) * cout
            out[tap : tap + cout] = kern[a, c].T


def image_kernel(first, pre_grad, ahead, across, wts, *rest):
    out = rest[-1]
    image = pl.program_id(0) + first
    top, bot = sides(ahead[image], across[image])
    rows, width, cout = pre_grad.shape[1:]
    cin = wts.shape[1]
    exact = jnp.concatenate([top, pre_grad[image], bot], axis=0).astype(F32)
    after, before = shifted(exact)
    taps = [value.astype(BF16) for value in (after, exact, before)]
    wide = jnp.concatenate(
        [taps[c][2 - a : 2 - a + rows] for a in range(3) for c in range(3)], axis=2
    )
    result = dot(wide.reshape(rows * width, 9 * cout), wts[...])
    out[0] = result.astype(BF16).reshape(rows, width, cin)


def fold_kernel(stage, value, received, keep, send):
    upper = is_upper(stage)
    part = keep.shape[0]
    low = value[:part] + received[:part]
    high = value[part:] + received[part:]
    keep[...] = jnp.where(upper, high, low)
    send[...] = jnp.where(upper, low, high)


def join_kernel(stage, value, received, out):
    upper = is_upper(stage)
    part = value.shape[0]
    out[:part] = jnp.where(upper, received[...], value[...])
    out[part:] = jnp.where(upper, value[...], received[...])


def finish_kernel(stage, own, value, *rest):
    out, held, sems = rest[-3:]
    count, size = held.shape[:2]
    upper = is_upper(stage) if own else jnp.logical_not(is_upper(stage))
    start = jnp.where(upper, count * size, 0)
    copies = []
    for index in range(count):
        held[index] = value[index * size : (index + 1) * size].astype(F32)
        place = pl.ds(pl.multiple_of(start + index * size, size), size)
        copies.append(pltpu.make_async_copy(held.at[index], out.at[place], sems.at[index]))
        copies[-1].start()
    for copy in copies:
        copy.wait()


def image_spec(shape, place=lambda b: b):
    return pl.BlockSpec((1, *shape[1:]), lambda b: (place(b),) + (0,) * (len(shape) - 1))


def whole_spec(shape):
    return pl.BlockSpec(shape, lambda b: (0,) * len(shape))


def in_hbm(value):
    return pltpu.with_memory_space_constraint(value, pltpu.HBM)


def resident():
    return pl.BlockSpec(memory_space=pltpu.VMEM)


def forward(first, images, taps, upstream):
    count, rows, width, cin = images.shape
    cout = taps.shape[3]
    many = images_per_step(count)
    shapes = [
        ((count, rows, width, cout), F32),
        ((2 * cout, 2 * cout), F32),
        ((8, cout), F32),
        (images.shape, BF16),
        (upstream.shape, BF16),
    ]
    space = pl.BlockSpec(memory_space=pltpu.HBM)
    return pl.pallas_call(
        functools.partial(forward_kernel, many),
        grid=(count // many,),
        in_specs=[resident(), space, resident(), space],
        out_specs=[resident()] * len(shapes),
        out_shape=[jax.ShapeDtypeStruct(shape, dtype) for shape, dtype in shapes],
        scratch_shapes=[
            pltpu.VMEM((10 * cin, 2 * cout), BF16),
            pltpu.VMEM((many, 2, (rows - 2) * width, cout), BF16),
            pltpu.SemaphoreType.DMA((count,)),
            pltpu.SemaphoreType.DMA((count,)),
        ],
        input_output_aliases={0: 3},
        compiler_params=pltpu.CompilerParams(vmem_limit_bytes=28 * MIB),
        cost_estimate=pl.CostEstimate(
            flops=2 * count * rows * width * 9 * cin * cout,
            bytes_accessed=2 * images.size + 2 * upstream.size + 4 * upstream.size,
            transcendentals=0,
        ),
        name="forward_inner",
    )(first, in_hbm(images), taps, in_hbm(upstream))


def edges(stage, top, bot, pre, upstream, kernel, acc, sums):
    count, rows, width, cout = pre.shape
    part = (cout + 16) // 2
    edge = (count, 1, width, cout)
    shapes = [edge, edge, (part, cout), (part, cout)]
    return pl.pallas_call(
        functools.partial(edge_kernel, count * rows * width, stage),
        in_specs=[resident()] * 7,
        out_specs=[resident()] * 4,
        out_shape=[jax.ShapeDtypeStruct(shape, F32) for shape in shapes],
        scratch_shapes=[pltpu.VMEM((2 * part, cout), F32)],
        compiler_params=pltpu.CompilerParams(vmem_limit_bytes=12 * MIB),
        cost_estimate=pl.CostEstimate(
            flops=2 * 2 * count * width * 3 * top.shape[3] * cout,
            bytes_accessed=4 * top.size + 24 * count * width * cout,
            transcendentals=0,
        ),
        name="forward_edges",
    )(top, bot, pre, upstream, kernel, acc, sums)


def moments(first, count, pre, low, high, upstream, images, top, bot, sums, *sofar):
    width, cin = images.shape[2:]
    cout = upstream.shape[3]
    rows = images.shape[1]
    operands = (pre, low, high, upstream, images, top, bot, sums, *sofar)
    return pl.pallas_call(
        functools.partial(moment_kernel, first, count),
        in_specs=[resident()] * len(operands),
        out_specs=[resident()] * 2,
        out_shape=[
            jax.ShapeDtypeStruct((3 * cin, 6 * cout), F32),
            jax.ShapeDtypeStruct((3 * cin, width), F32),
        ],
        input_output_aliases={8: 0, 9: 1} if sofar else {},
        compiler_params=pltpu.CompilerParams(vmem_limit_bytes=28 * MIB),
        cost_estimate=pl.CostEstimate(
            flops=2 * count * rows * width * 18 * cin * cout, bytes_accessed=8 * MIB, transcendentals=0
        ),
        name="moments",
    )(*operands)


def whitened(total_pix, stage, own, other, colors, offset, sums, acc, maps):
    half = colors.shape[1]
    cout = 2 * half
    cin = acc.shape[0] // 3
    shapes = [
        ((9 * cin // 2, cout), F32),
        ((9 * cin // 2, cout), F32),
        ((2, half, half), F32),
        ((3 * cout, 2 * cout), BF16),
        ((2 * cout, 2 * cout), BF16),
        ((8, cout), F32),
    ]
    return pl.pallas_call(
        functools.partial(whitening_kernel, total_pix, stage),
        in_specs=[resident()] * 7,
        out_specs=[resident()] * len(shapes),
        out_shape=[jax.ShapeDtypeStruct(shape, dtype) for shape, dtype in shapes],
        scratch_shapes=[pltpu.VMEM((cout + 16, cout), F32)],
        compiler_params=pltpu.CompilerParams(vmem_limit_bytes=20 * MIB),
        cost_estimate=pl.CostEstimate(
            flops=2 * 9 * cin * 8 * cout * cout, bytes_accessed=8 * MIB, transcendentals=0
        ),
        name="whitening",
    )(own, other, colors, offset, sums, acc, maps)


def edge_gradients(low, high, upstream, mats, paint_rows):
    return pl.pallas_call(
        edge_gradient_kernel,
        in_specs=[resident()] * 5,
        out_specs=[resident()] * 2,
        out_shape=[jax.ShapeDtypeStruct(low.shape, BF16)] * 2,
        compiler_params=pltpu.CompilerParams(vmem_limit_bytes=16 * MIB),
        name="edge_gradients",
    )(low, high, upstream, mats, paint_rows)


def gradients(pre, low, high, upstream, mats, paint_rows):
    count, rows, width, cout = pre.shape
    return pl.pallas_call(
        gradient_kernel,
        grid=(count,),
        in_specs=[resident()] * 6,
        out_specs=resident(),
        out_shape=jax.ShapeDtypeStruct(pre.shape, BF16),
        compiler_params=pltpu.CompilerParams(vmem_limit_bytes=16 * MIB),
        cost_estimate=pl.CostEstimate(
            flops=2 * count * rows * width * 6 * cout * cout,
            bytes_accessed=8 * pre.size,
            transcendentals=0,
        ),
        name="pre_gradient",
    )(pre, low, high, upstream, mats, paint_rows)


def painted(pre, low, high, paint, paint_rows):
    count, rows, width, cout = pre.shape
    return pl.pallas_call(
        paint_kernel,
        grid=(count,),
        in_specs=[resident()] * 5,
        out_specs=image_spec(pre.shape),
        out_shape=jax.ShapeDtypeStruct(pre.shape, BF16),
        compiler_params=pltpu.CompilerParams(vmem_limit_bytes=16 * MIB),
        cost_estimate=pl.CostEstimate(
            flops=2 * count * rows * width * 4 * cout * cout,
            bytes_accessed=6 * pre.size,
            transcendentals=0,
        ),
        name="colored",
    )(pre, low, high, paint, paint_rows)


def turned_weights(kernel):
    cin, cout = kernel.shape[2:]
    return pl.pallas_call(
        turn_kernel,
        out_shape=jax.ShapeDtypeStruct((9 * cout, cin), BF16),
        compiler_params=pltpu.CompilerParams(vmem_limit_bytes=4 * MIB),
        name="turned_weights",
    )(kernel)


def image_gradient(first, count, pre_grad, top, bot, turned, out=None):
    images, rows, width, cout = pre_grad.shape
    cin = turned.shape[1]
    shape = (images, rows, width, cin)

    def place(b):
        return b + first

    operands = [pre_grad, top, bot, turned]
    in_specs = [resident()] * 4
    aliases = {}
    if out is not None:
        operands.append(out)
        in_specs.append(pl.BlockSpec(memory_space=pl.ANY))
        aliases = {4: 0}
    return pl.pallas_call(
        functools.partial(image_kernel, first),
        grid=(count,),
        in_specs=in_specs,
        out_specs=image_spec(shape, place),
        out_shape=jax.ShapeDtypeStruct(shape, BF16),
        input_output_aliases=aliases,
        compiler_params=pltpu.CompilerParams(vmem_limit_bytes=12 * MIB),
        cost_estimate=pl.CostEstimate(
            flops=2 * count * rows * width * 9 * cin * cout,
            bytes_accessed=2 * count * rows * width * (cin + cout),
            transcendentals=0,
        ),
        name="image_gradient",
    )(*operands)


def images_per_step(count):
    return 2 if count % 2 == 0 else 1


def fetched(images, kernel):
    count, rows, width, cin = images.shape
    edge = (count, 1, width, cin)
    space = pl.BlockSpec(memory_space=pltpu.HBM)
    return pl.pallas_call(
        functools.partial(fetch_kernel, images_per_step(count)),
        in_specs=[space, space],
        out_specs=[resident()] * 4,
        out_shape=[
            jax.ShapeDtypeStruct(shape, BF16) for shape in (edge, edge, kernel.shape, images.shape)
        ],
        scratch_shapes=[pltpu.SemaphoreType.DMA((4,))],
        compiler_params=pltpu.CompilerParams(vmem_limit_bytes=4 * MIB),
        name="edge_rows",
    )(in_hbm(images), in_hbm(kernel))


def small_call(kernel, name, *operands, out):
    return pl.pallas_call(
        kernel,
        in_specs=[resident()] * len(operands),
        out_specs=[resident()] * len(out),
        out_shape=out,
        compiler_params=pltpu.CompilerParams(vmem_limit_bytes=4 * MIB),
        name=name,
    )(*operands)


def fold(value, received, stage):
    half = jax.ShapeDtypeStruct((value.shape[0] // 2, value.shape[1]), value.dtype)
    return small_call(
        functools.partial(fold_kernel, stage), "fold", value, received, out=[half, half]
    )


def join(value, received, stage):
    whole = jax.ShapeDtypeStruct((value.shape[0] * 2, value.shape[1]), value.dtype)
    return small_call(
        functools.partial(join_kernel, stage), "join", value, received, out=[whole]
    )[0]


def finish(stage, value, out=None):
    part, lanes = value.shape
    operands, aliases = (value,), {}
    if out is not None:
        operands, aliases = (value, out), {1: 0}
    space = pl.BlockSpec(memory_space=pltpu.HBM)
    return pl.pallas_call(
        functools.partial(finish_kernel, stage, out is None),
        in_specs=[resident(), space][: len(operands)],
        out_specs=space,
        out_shape=jax.ShapeDtypeStruct((2 * part, lanes), F32),
        scratch_shapes=[
            pltpu.VMEM((2, part // 2, lanes), F32),
            pltpu.SemaphoreType.DMA((2,)),
        ],
        input_output_aliases=aliases,
        compiler_params=pltpu.CompilerParams(vmem_limit_bytes=4 * MIB),
        name="finish",
    )(*operands)


def halos(ahead, across):
    count, groups = lax.axis_size("rows"), lax.axis_size("dp")
    offset = 2 if groups % 4 == 0 else 1 if groups % 2 == 0 else 0
    pairs = ([], [])
    for group in range(groups):
        for place in range(count):
            for first in (0, 1):
                partner = place + 1 if place % 2 == first else place - 1
                inside = 0 <= partner < count
                other = (group, partner) if inside else (group ^ offset, place)
                pairs[first].append((group * count + place, other[0] * count + other[1]))
    return lax.ppermute(ahead, AXES, pairs[0]), lax.ppermute(across, AXES, pairs[1])


def exchange(value, devices, stage):
    pairs = [(i, i ^ (stage[1] if i & 1 else stage[0])) for i in range(devices)]
    return lax.ppermute(value, AXES, pairs)


def beside(send, devices, stage, task, operands):
    send, operands = lax.optimization_barrier((send, operands))
    received = exchange(send, devices, stage)
    result = task(*operands)
    return lax.optimization_barrier((received, result))


def body(images, kernel, colors, offset, upstream):
    count, rows, width, cin = images.shape
    cout = kernel.shape[3]
    devices = lax.axis_size("dp") * lax.axis_size("rows")
    total_pix = count * rows * width * devices
    plan = stages(devices)
    ahead, across, kernel, maps = fetched(images, kernel)
    top, bot = halos(ahead, across)
    pre, acc, sums, images, upstream = forward(maps, images, kernel, upstream)
    low, high, value, send = edges(plan[0], top, bot, pre, upstream, kernel, acc, sums)
    state = {"next": 0, "moments": (), "grad": None}

    def summed(send, stage, many):
        first = state["next"]
        many = min(many, count - first)
        if many == 0:
            return exchange(send, devices, stage)
        state["next"] = first + many
        operands = (pre, low, high, upstream, images, top, bot, sums, *state["moments"])
        received, state["moments"] = beside(
            send, devices, stage, functools.partial(moments, first, many), operands
        )
        return received

    value = value + exchange(send, devices, plan[0])
    for stage in plan[1:]:
        value = value + summed(value, stage, 2 if stage in plan[2:4] else 1)
    received = exchange(value, devices, plan[0])
    first = state["next"]
    if first < count:
        operands = (pre, low, high, upstream, images, top, bot, sums, *state["moments"])
        state["moments"] = moments(first, count - first, *operands)
    value, send, grad_colors, mats, paint, paint_rows = whitened(
        total_pix,
        plan[0],
        value,
        received,
        colors,
        offset.reshape(1, cout),
        sums,
        *state["moments"],
    )
    received, (edge_ahead, edge_across, turned) = beside(
        send,
        devices,
        plan[0],
        lambda kernel, *operands: (*edge_gradients(*operands), turned_weights(kernel)),
        (kernel, low, high, upstream, mats, paint_rows),
    )
    state["next"] = 0
    shares = [1, 1, 1, 1, 2]

    def transfer(send, stage):
        first = state["next"]
        if first >= count:
            return exchange(send, devices, stage)
        many = min(shares.pop(0), count - first) if shares else count - first
        state["next"] = first + many
        operands = (pre_grad, grad_top, grad_bot, turned)
        if state["grad"] is not None:
            operands = (*operands, state["grad"])
        received, state["grad"] = beside(
            send, devices, stage, functools.partial(image_gradient, first, many), operands
        )
        return received

    cuts = []
    for stage in plan[1:]:
        if value.shape[0] % 32 == 0 and value.shape[0] > 144:
            value, send = fold(value, received, stage)
            cuts.append(stage)
        else:
            value = send = value + received
        if stage == plan[1]:
            send, edge_ahead, edge_across = lax.optimization_barrier(
                (send, edge_ahead, edge_across)
            )
            grad_top, grad_bot = halos(edge_ahead, edge_across)
            received, pre_grad = beside(
                send, devices, stage, gradients, (pre, low, high, upstream, mats, paint_rows)
            )
        elif stage == plan[2]:
            received, colored = beside(
                send, devices, stage, painted, (pre, low, high, paint, paint_rows)
            )
        else:
            received = transfer(send, stage)
    value = (value + received).astype(BF16)
    for stage in reversed(cuts):
        value = join(value, transfer(value, stage), stage)
    received, result = beside(
        value, devices, plan[0], functools.partial(finish, plan[0]), (value,)
    )
    first = state["next"]
    if first < count:
        operands = (pre_grad, grad_top, grad_bot, turned, state["grad"])
        state["grad"] = image_gradient(first, count - first, *operands)
    grad_kernel = finish(plan[0], received, result).reshape(3, 3, cin, cout)
    return colored, state["grad"], grad_kernel, grad_colors


def solution(mesh):
    placed = (P("dp", "rows", None, None), P(), P(), P(), P("dp", "rows", None, None))
    return jax.shard_map(
        body,
        mesh=mesh,
        in_specs=placed,
        out_specs=(P("dp", "rows", None, None), P("dp", "rows", None, None), P(), P()),
        check_vma=False,
    )
```
